256 devices in a mesh: row: 8 (over y, core), col: 32 (over z, x).
Axes of the slice: x: 4, y: 4, z: 8, core: 2. Of those that a mesh axis runs over, the one named last changes fastest.
Arguments:
- object_field: float32 [2, 1024, 4096], P(None, 'row', 'col'), may hold values from -3 to 3
- probe_field: float32 [2, 256, 256], replicated, may hold values from -3 to 3
- intensity: float32 [8, 32, 8, 256, 256], P('row', 'col'), may hold values from 0.05 to 1
- scan_offsets: int32 [8, 32, 8, 2], P('row', 'col'), may hold values from -128 to 0
- pattern_counts: int32 [8, 32], P('row', 'col'), may hold values from 1 to 8, as said below
Outputs:
- new_object: float32 [2, 1024, 4096], P(None, 'row', 'col')
- new_probe: float32 [2, 256, 256], replicated
The draws below stay inside these ranges and needn't reach their ends.
Inputs may be any that keep to these rules, and one draw needn't show every extreme that they name: `pattern_counts`: some region has 8 live slots in every draw.
All inputs are finite; a program needn't handle non-finite values.
Results may differ from the reference program's by a relative error of at most 0.0025.
The reference program's roundings to bfloat16 on the way count: a program that leaves them out, or rounds other values in their place, can miss the bound.
Values sent between devices are 32-bit elements; how exact they have to be, the bound alone decides.
No kernel may reach another device: no remote copies, remote signals or barrier semaphores. Data moves between devices by JAX's collectives and lax.ppermute only.
A program may use at most 64 MiB of HBM per device.

```python
import math
import jax
import jax.numpy as jnp
from jax import lax

PSIZE = 256
KMAX = 8
ITERS = 2
REGION = 128
NY = 1024
NX = 4096
N_ROW = 8
N_COL = 32


def draw_pattern_counts(key, part):
    key = jax.random.fold_in(key, 11)
    first_key, second_key = jax.random.split(key)
    values = jax.random.randint(first_key, (N_ROW * N_COL,), 1, KMAX + 1)
    place = jax.random.randint(second_key, (), 0, N_ROW * N_COL)
    values = values.at[place].set(KMAX)
    return values.reshape(N_ROW, N_COL).astype(jnp.int32)


def with_ends(result, own_key, smallest, largest):
    longest = result.shape.index(max(result.shape))
    spots = []
    for shift in (0, 1):
        where = [jax.random.randint(jax.random.fold_in(own_key, axis), (), 0, length) for axis, length in enumerate(result.shape)]
        where[longest] = (where[longest] + shift) % result.shape[longest]
        spots.append(tuple(where))
    return result.at[spots[0]].set(smallest).at[spots[1]].set(largest)


def levels(own_key, extent, cuts, low, high):
    factor_of, own = 1.0, jax.random.fold_in(own_key, 6)
    for position, parts in cuts:
        steps = jnp.exp(jax.random.uniform(jax.random.fold_in(own, position), (parts,), jnp.float32, low / len(cuts), high / len(cuts)))
        factor_of = factor_of * jnp.repeat(steps, extent[position] // parts).reshape([-1 if axis == position else 1 for axis in range(len(extent))])
    return factor_of


def normal_values(rng, shape, deviation, reach, cuts=(), kind=jnp.bfloat16):
    level = levels(rng, shape, cuts, -0.22, 0.18) if cuts else 1.0
    values = jax.random.normal(rng, shape, jnp.float32) * deviation * level
    return jnp.minimum(jnp.maximum(values, -reach), reach).astype(kind)


def setup_inputs(seed: int = 0) -> dict:
    keys = jax.random.split(jax.random.key(seed), 6)
    return {
        "object_field": normal_values(keys[0], (2, NY, NX), 0.5, 3.0, ((1, 8), (2, 32)), jnp.float32),
        "probe_field": normal_values(keys[1], (2, PSIZE, PSIZE), 0.5, 3.0, (), jnp.float32),
        "intensity": jnp.clip(jnp.exp(math.log(1.0) - 2.9957323 * jax.random.uniform(keys[2], (N_ROW, N_COL, KMAX, PSIZE, PSIZE), jnp.float32) ** levels(keys[2], (N_ROW, N_COL, KMAX, PSIZE, PSIZE), ((0, 8), (1, 32)), -0.2, 0.2)), 0.05, 1.0),
        "scan_offsets": with_ends(jax.random.randint(keys[3], (N_ROW, N_COL, KMAX, 2), 0 - REGION, 2 * REGION - PSIZE + 1), jax.random.fold_in(keys[3], 1), 0 - REGION, 2 * REGION - PSIZE).astype(jnp.int32),
        "pattern_counts": draw_pattern_counts(jax.random.fold_in(keys[5], 71), 0),
    }


def dft_tables(length):
    index = jnp.arange(length, dtype=jnp.int32)
    product = index[:, None] * index[None, :] % length
    angle = 2.0 * jnp.pi / length * product.astype(jnp.float32)
    factor = 1.0 / jnp.sqrt(jnp.float32(length))
    return ((jnp.cos(angle) * factor).astype(jnp.bfloat16), (jnp.sin(angle) * factor).astype(jnp.bfloat16))

def left_section(real_part, imag_part, cos_table, sin_table, sign_value):
    width = real_part.shape[1]
    joined = jnp.concatenate([real_part, imag_part], axis=1)
    first = jnp.dot(cos_table, joined, preferred_element_type=jnp.float32)
    second = jnp.dot(sin_table, joined, preferred_element_type=jnp.float32)
    return (first[:, :width] + sign_value * second[:, width:], first[:, width:] - sign_value * second[:, :width])

def right_section(real_part, imag_part, cos_table, sin_table, sign_value):
    height = real_part.shape[0]
    joined = jnp.concatenate([real_part, imag_part], axis=0)
    first = jnp.dot(joined, cos_table, preferred_element_type=jnp.float32)
    second = jnp.dot(joined, sin_table, preferred_element_type=jnp.float32)
    return (first[:height] + sign_value * second[height:], first[height:] - sign_value * second[:height])

def transform(real_part, imag_part, cos_table, sin_table, sign_value):
    mid_real, mid_imag = left_section(real_part.astype(jnp.bfloat16), imag_part.astype(jnp.bfloat16), cos_table, sin_table, sign_value)
    return right_section(mid_real.astype(jnp.bfloat16), mid_imag.astype(jnp.bfloat16), cos_table, sin_table, sign_value)

def pattern_terms(window, probe, pattern, weight, cos_table, sin_table):
    wave_real = probe[0] * window[0] - probe[1] * window[1]
    wave_imag = probe[0] * window[1] + probe[1] * window[0]
    far_real, far_imag = transform(wave_real, wave_imag, cos_table, sin_table, 1.0)
    misfit = (far_real * far_real + far_imag * far_imag - pattern) * weight
    back_real, back_imag = transform(misfit * far_real, misfit * far_imag, cos_table, sin_table, -1.0)
    object_term = jnp.stack([probe[0] * back_real + probe[1] * back_imag, probe[0] * back_imag - probe[1] * back_real])
    probe_term = jnp.stack([window[0] * back_real + window[1] * back_imag, window[0] * back_imag - window[1] * back_real])
    return (object_term, probe_term)

def reference(object_field, probe_field, intensity, scan_offsets, pattern_counts):
    cos_table, sin_table = dft_tables(PSIZE)
    flat_index = jnp.arange(N_ROW * N_COL * KMAX, dtype=jnp.int32)
    slot_index = flat_index % KMAX
    device = flat_index // KMAX
    dev_row = device // N_COL
    dev_col = device % N_COL
    live_counts = jnp.repeat(pattern_counts.reshape(-1), KMAX)
    weights = (slot_index < live_counts).astype(jnp.float32)
    offsets = scan_offsets.reshape(-1, 2)
    start_row = (dev_row * REGION + offsets[:, 0] + REGION).astype(jnp.int32)
    start_col = (dev_col * REGION + offsets[:, 1] + REGION).astype(jnp.int32)
    patterns = intensity.reshape(-1, PSIZE, PSIZE)
    for step in range(ITERS):
        padded = jnp.pad(object_field, ((0, 0), (REGION, REGION), (REGION, REGION)))
        probe_now = probe_field

        def visit(carry, item):
            grad_pad, grad_probe = carry
            row_start, col_start, pattern, weight = item
            anchor = jnp.zeros((), jnp.int32)
            window = lax.dynamic_slice(padded, (anchor, row_start, col_start), (2, PSIZE, PSIZE))
            object_term, probe_term = pattern_terms(window, probe_now, pattern, weight, cos_table, sin_table)
            current = lax.dynamic_slice(grad_pad, (anchor, row_start, col_start), (2, PSIZE, PSIZE))
            grad_pad = lax.dynamic_update_slice(grad_pad, current + object_term, (anchor, row_start, col_start))
            return ((grad_pad, grad_probe + probe_term), None)
        start = (jnp.zeros_like(padded), jnp.zeros_like(probe_field))
        (grad_pad, grad_probe), unused = lax.scan(visit, start, (start_row, start_col, patterns, weights))
        grad_object = grad_pad[:, REGION:-REGION, REGION:-REGION]
        peak = jnp.max(probe_now[0] * probe_now[0] + probe_now[1] * probe_now[1]) + 1e-06
        object_field = object_field - grad_object / peak
        spread = jnp.sqrt(jnp.sum(grad_probe * grad_probe) / grad_probe.size + 1e-06)
        probe_field = probe_now - 0.3 * grad_probe / spread
    return (object_field, probe_field)
```

```python
import jax
import jax.numpy as jnp
import numpy as np
from jax import lax
from jax.experimental import pallas as pl
from jax.experimental.pallas import tpu as pltpu
from jax.sharding import Mesh, PartitionSpec as P

ROW = ("y", "core")
COL = ("z", "x")
PLANE = ("y", "core", "x")
LANES = 128
F32 = jnp.float32


def dft_tables(length):
    index = jnp.arange(length, dtype=jnp.int32)
    product = index[:, None] * index[None, :] % length
    angle = 2.0 * jnp.pi / length * product.astype(F32)
    factor = 1.0 / jnp.sqrt(F32(length))
    cos_table = (jnp.cos(angle) * factor).astype(jnp.bfloat16)
    sin_table = (jnp.sin(angle) * factor).astype(jnp.bfloat16)
    forward = jnp.block([[cos_table, sin_table], [-sin_table, cos_table]])
    inverse = jnp.block([[cos_table, -sin_table], [sin_table, cos_table]])
    return forward, inverse


def dot(a, b):
    return jnp.dot(a, b, preferred_element_type=F32)


def transform(real_part, imag_part, left, right):
    size = real_part.shape[0]
    mid = dot(left, jnp.concatenate([real_part, imag_part], axis=0).astype(jnp.bfloat16))
    mid = mid.astype(jnp.bfloat16)
    out = dot(jnp.concatenate([mid[:size], mid[size:]], axis=1), right)
    return out[:, :size], out[:, size:]


def updated_probe(probe, total):
    mean = jnp.sum(total * total, keepdims=True) / total.size
    return probe - 0.3 * total / jnp.sqrt(mean + 1e-06)


def patterns_loop(count_ref, offset_ref, pattern_ref, forward_ref, inverse_ref, probe, ext, gobj, gprobe):
    size = pattern_ref.shape[1]
    region = size // 2
    tiles = size // 8
    gobj[...] = jnp.zeros_like(gobj)
    gprobe[...] = jnp.zeros_like(gprobe)

    def visit(k, carry):
        row = offset_ref[k, 0] + region
        col = offset_ref[k, 1] + region
        tile = jnp.minimum(row // 8, region // 8 - 1)
        sub = row - tile * 8
        sub_id = lax.broadcasted_iota(jnp.int32, (1, 8, LANES), 1)
        lane_id = lax.broadcasted_iota(jnp.int32, (1, 8, LANES), 2)

        def window(part):
            pieces = [
                pltpu.roll(
                    ext[part, pl.ds(tile, tiles + 1), :, v * LANES : (v + 1) * LANES],
                    lax.rem(LANES - col, LANES),
                    2,
                )
                for v in range(3)
            ]
            halves = []
            for v in range(2):
                x = jnp.where(lane_id < LANES - col, pieces[v], pieces[v + 1])
                x = pltpu.roll(x, lax.rem(8 - sub, 8), 1)
                halves.append(jnp.where(sub_id < 8 - sub, x[:tiles], x[1:]).reshape(size, LANES))
            return jnp.concatenate(halves, axis=1)

        def place(part, value):
            zero = jnp.zeros((1, 8, LANES), F32)
            rolled = []
            for v in range(2):
                x = value[:, v * LANES : (v + 1) * LANES].reshape(tiles, 8, LANES)
                x = pltpu.roll(x, lax.rem(sub, 8), 1)
                x = jnp.where(
                    sub_id < sub,
                    jnp.concatenate([zero, x], axis=0),
                    jnp.concatenate([x, zero], axis=0),
                )
                rolled.append(pltpu.roll(x, lax.rem(col, LANES), 2))
            inside = lane_id < col
            pieces = [
                jnp.where(inside, 0.0, rolled[0]),
                jnp.where(inside, rolled[0], rolled[1]),
                jnp.where(inside, rolled[1], 0.0),
            ]
            for v in range(3):
                gobj[part, pl.ds(tile, tiles + 1), :, v * LANES : (v + 1) * LANES] += pieces[v]

        def add_probe(part, value):
            for v in range(2):
                gprobe[part, v] += value[:, v * LANES : (v + 1) * LANES]

        def probe_part(part):
            return jnp.concatenate([probe[part, 0], probe[part, 1]], axis=1)

        win_real, win_imag = window(0), window(1)
        probe_real, probe_imag = probe_part(0), probe_part(1)
        far_real, far_imag = transform(
            probe_real * win_real - probe_imag * win_imag,
            probe_real * win_imag + probe_imag * win_real,
            forward_ref[...],
            inverse_ref[...],
        )
        misfit = far_real * far_real + far_imag * far_imag - pattern_ref[k]
        back_real, back_imag = transform(
            misfit * far_real, misfit * far_imag, inverse_ref[...], forward_ref[...]
        )
        add_probe(0, win_real * back_real + win_imag * back_imag)
        add_probe(1, win_real * back_imag - win_imag * back_real)
        place(0, probe_real * back_real + probe_imag * back_imag)
        place(1, probe_real * back_imag - probe_imag * back_real)
        return carry

    lax.fori_loop(0, count_ref[0], visit, 0)


def load_object(ext, strip_refs):
    rows = LANES // 8
    for i, ref in enumerate(strip_refs):
        for j in range(3):
            for part in range(2):
                ext[part, i * rows : (i + 1) * rows, :, j * LANES : (j + 1) * LANES] = ref[j, part]


def store_gradient(gobj, strip_refs):
    rows = LANES // 8
    for i, ref in enumerate(strip_refs):
        for j in range(3):
            for part in range(2):
                ref[j, part] = gobj[part, i * rows : (i + 1) * rows, :, j * LANES : (j + 1) * LANES]


def peak_of(probe):
    power = probe[0] * probe[0] + probe[1] * probe[1]
    return jnp.max(power, keepdims=True).reshape(1, 1) + 1e-06


def first_kernel(
    count_ref, offset_ref, pattern_ref, forward_ref, inverse_ref, above_ref, own_ref, below_ref, start_ref,
    up_ref, mid_ref, down_ref, gprobe_ref, peak_ref, probe_ref,
    ext, gobj,
):
    for part in range(2):
        for v in range(2):
            probe_ref[part, v] = start_ref[part, :, v * LANES : (v + 1) * LANES]
    peak_ref[...] = jnp.broadcast_to(peak_of(probe_ref[...]), peak_ref.shape)
    load_object(ext, (above_ref, own_ref, below_ref))
    patterns_loop(count_ref, offset_ref, pattern_ref, forward_ref, inverse_ref, probe_ref, ext, gobj, gprobe_ref)
    store_gradient(gobj, (up_ref, mid_ref, down_ref))


def second_kernel(
    count_ref, offset_ref, pattern_ref, forward_ref, inverse_ref, above_ref, own_ref, below_ref, start_ref, total_ref,
    up_ref, mid_ref, down_ref, gprobe_ref, peak_ref, probe_ref,
    ext, gobj,
):
    probe_ref[...] = updated_probe(start_ref[...], total_ref[...])
    peak_ref[...] = jnp.broadcast_to(peak_of(probe_ref[...]), peak_ref.shape)
    load_object(ext, (above_ref, own_ref, below_ref))
    patterns_loop(count_ref, offset_ref, pattern_ref, forward_ref, inverse_ref, probe_ref, ext, gobj, gprobe_ref)
    store_gradient(gobj, (up_ref, mid_ref, down_ref))


def gradients(kernel, count, offsets, patterns, tables, strips, *probes):
    size = patterns.shape[1]
    vmem = pl.BlockSpec(memory_space=pltpu.VMEM)
    smem = pl.BlockSpec(memory_space=pltpu.SMEM)
    strip = jax.ShapeDtypeStruct((3, 2, LANES // 8, 8, LANES), F32)
    halves = jax.ShapeDtypeStruct((2, 2, size, LANES), F32)
    return pl.pallas_call(
        kernel,
        out_shape=(strip, strip, strip, halves, jax.ShapeDtypeStruct((8, LANES), F32), halves),
        in_specs=[smem, smem] + [vmem] * (6 + len(probes)),
        out_specs=(vmem,) * 6,
        scratch_shapes=[pltpu.VMEM((2, 48, 8, 3 * LANES), F32), pltpu.VMEM((2, 48, 8, 3 * LANES), F32)],
        compiler_params=pltpu.CompilerParams(vmem_limit_bytes=40 * 1024 * 1024),
    )(count, offsets, patterns, *tables, *strips, *probes)


def small_call(kernel, out_shapes, *args):
    vmem = pl.BlockSpec(memory_space=pltpu.VMEM)
    return pl.pallas_call(
        kernel,
        out_shape=tuple(jax.ShapeDtypeStruct(shape, F32) for shape in out_shapes),
        in_specs=[vmem] * len(args),
        out_specs=(vmem,) * len(out_shapes),
        compiler_params=pltpu.CompilerParams(vmem_limit_bytes=24 * 1024 * 1024),
    )(*args)


def sum_copies_kernel(in_ref, out_ref):
    total = in_ref[0]
    for i in range(1, in_ref.shape[0]):
        total = total + in_ref[i]
    for i in range(out_ref.shape[0]):
        out_ref[i] = total


def sum_copies(value, copies):
    return small_call(sum_copies_kernel, [(copies,) + value.shape[1:]], value)[0]


def exchange(value, axes):
    return lax.all_to_all(value, axes, 0, 0, tiled=True)


def shifted(value, axes, step):
    count = lax.axis_size(axes)
    return lax.ppermute(value, axes, [(i, i + step) for i in range(count) if 0 <= i + step < count])


def final_probe_kernel(probe_ref, total_ref, out_ref):
    new = updated_probe(probe_ref[...], total_ref[...])
    for part in range(2):
        for v in range(2):
            out_ref[part, :, v * LANES : (v + 1) * LANES] = new[part, v]


def total_over_devices(gprobe):
    shape = gprobe.shape
    plane = lax.axis_size(PLANE)
    chunks = gprobe.reshape(plane, -1, LANES)
    shares = sum_copies(exchange(chunks, PLANE), lax.axis_size("z"))
    shares = sum_copies(exchange(shares, "z"), plane)
    return exchange(shares, PLANE).reshape(shape)


def body(object_field, probe_field, intensity, scan_offsets, pattern_counts):
    size = probe_field.shape[1]
    slots = intensity.shape[2]
    patterns = intensity.reshape(slots, size, size)
    offsets = scan_offsets.reshape(slots, 2)
    count = pattern_counts.reshape(1)
    tables = dft_tables(size)
    col = lax.axis_index(COL)
    cols = lax.axis_size(COL)

    block = (2, LANES // 8, 8, LANES)
    own = object_field.reshape(block)
    strip = jnp.stack([shifted(own, COL, 1), own, shifted(own, COL, -1)])
    strips = (shifted(strip, ROW, 1), strip, shifted(strip, ROW, -1))
    up, mid, down, gprobe, peak, probe = gradients(
        first_kernel, count, offsets, patterns, tables, strips, probe_field
    )
    total = total_over_devices(gprobe)
    mid = mid + shifted(up, ROW, -1) + shifted(down, ROW, 1)
    left, right = shifted(mid[1:], COL, 1), shifted(mid[:2], COL, -1)
    far_left, far_right = shifted(mid[2], COL, 2), shifted(mid[0], COL, -2)
    peak = peak[0, 0]
    grads = jnp.stack(
        [
            jnp.where(col > 0, left[0] + far_left + mid[0], 0.0),
            mid[1] + left[1] + right[0],
            jnp.where(col < cols - 1, right[1] + far_right + mid[2], 0.0),
        ]
    )
    strip = strip - grads / peak
    strips = (shifted(strip, ROW, 1), strip, shifted(strip, ROW, -1))
    up, mid, down, gprobe, peak, probe = gradients(
        second_kernel, count, offsets, patterns, tables, strips, probe, total
    )
    total = total_over_devices(gprobe)
    mid = mid + shifted(up, ROW, -1) + shifted(down, ROW, 1)
    grad = mid[1] + shifted(mid[2], COL, 1) + shifted(mid[0], COL, -1)
    new_object = strip[1] - grad / peak[0, 0]
    new_probe = small_call(final_probe_kernel, [probe_field.shape], probe, total)[0]
    return (new_object.reshape(object_field.shape), new_probe)


def solution(mesh):
    split = Mesh(mesh.devices.reshape(4, 2, 8, 4), ("y", "core", "z", "x"))
    in_specs = (
        P(None, ROW, COL),
        P(),
        P(ROW, COL, None, None, None),
        P(ROW, COL, None, None),
        P(ROW, COL),
    )
    out_specs = (P(None, ROW, COL), P())
    return jax.shard_map(body, mesh=split, in_specs=in_specs, out_specs=out_specs, check_vma=False)
```

```python
import functools

import jax
import jax.numpy as jnp
import numpy as np
from jax import lax
from jax.experimental import pallas as pl
from jax.experimental.pallas import tpu as pltpu
from jax.sharding import Mesh, PartitionSpec as P

ROW = ("y", "core")
COL = ("z", "x")
PLANE = ("y", "core", "x")
LANES = 128
TILES = 16
GROUP = 4
F32 = jnp.float32
VMEM_BYTES = 56 * 1024 * 1024


def dft_tables(length):
    index = np.arange(length, dtype=np.int64)
    angle = 2.0 * np.pi / length * (index[:, None] * index[None, :] % length)
    factor = 1.0 / np.sqrt(length)
    cos_table = (np.cos(angle) * factor).astype(np.float32)
    sin_table = (np.sin(angle) * factor).astype(np.float32)
    forward = np.block([[cos_table, sin_table], [-sin_table, cos_table]])
    inverse = np.block([[cos_table, -sin_table], [sin_table, cos_table]])
    return jnp.asarray(forward, jnp.bfloat16), jnp.asarray(inverse, jnp.bfloat16)


def place_of(axes):
    index = lax.axis_index(axes)
    odd = lax.rem(index, 2)
    at_end = (index == 0) | (index == lax.axis_size(axes) - 1)
    return index, (2 - 2 * odd, 1, 2 * odd), at_end


def paired(value, axes, side):
    count = lax.axis_size(axes)
    pairs = [(i, (i + (1 if (i + side // 2) % 2 == 0 else -1)) % count) for i in range(count)]
    return lax.ppermute(value, axes, pairs)


def paired_far(value, axes, phase):
    count = lax.axis_size(axes)
    pairs = [(i, (i + (2 if (i // 2 + phase) % 2 == 0 else -2)) % count) for i in range(count)]
    return lax.ppermute(value, axes, pairs)


def dot(a, b):
    return jnp.dot(a, b, preferred_element_type=F32)


def transform(reals, imags, left, right):
    size = reals[0].shape[0]
    columns = [jnp.concatenate(pair, axis=0).astype(jnp.bfloat16) for pair in zip(reals, imags)]
    mid = dot(left, jnp.concatenate(columns, axis=1)).astype(jnp.bfloat16)
    rows = [
        jnp.concatenate([mid[:size, i * size : (i + 1) * size], mid[size:, i * size : (i + 1) * size]], axis=1)
        for i in range(len(reals))
    ]
    out = dot(jnp.concatenate(rows, axis=0), right)
    return (
        [out[i * size : (i + 1) * size, :size] for i in range(len(reals))],
        [out[i * size : (i + 1) * size, size:] for i in range(len(reals))],
    )


def updated_probe(probe, total):
    mean = jnp.sum(total * total, keepdims=True) / total.size
    return probe - 0.3 * total / jnp.sqrt(mean + 1e-06)


def pattern_group(group, count, offset_ref, pattern, left, right, probe, ext, gobj, gprobe):
    size = pattern.shape[1]
    region = size // 2
    tiles = size // 8
    slots = [group * GROUP + i for i in range(GROUP)]
    sub_id = lax.broadcasted_iota(jnp.int32, (1, 8, LANES), 1)
    lane_id = lax.broadcasted_iota(jnp.int32, (1, 8, LANES), 2)

    def corner(slot):
        row = offset_ref[0, slot] + region
        col = offset_ref[1, slot] + region
        tile = jnp.minimum(row // 8, region // 8 - 1)
        return tile, row - tile * 8, col

    def window(part, at):
        tile, sub, col = at
        pieces = [
            pltpu.roll(ext[v, part, pl.ds(tile, tiles + 1)], lax.rem(LANES - col, LANES), 2) for v in range(3)
        ]
        halves = []
        for v in range(2):
            x = jnp.where(lane_id < LANES - col, pieces[v], pieces[v + 1])
            x = pltpu.roll(x, lax.rem(8 - sub, 8), 1)
            halves.append(jnp.where(sub_id < 8 - sub, x[:tiles], x[1:]).reshape(size, LANES))
        return jnp.concatenate(halves, axis=1)

    def add_object(part, value, at):
        tile, sub, col = at
        zero = jnp.zeros((1, 8, LANES), F32)
        rolled = []
        for v in range(2):
            x = value[:, v * LANES : (v + 1) * LANES].reshape(tiles, 8, LANES)
            x = pltpu.roll(x, lax.rem(sub, 8), 1)
            x = jnp.where(
                sub_id < sub, jnp.concatenate([zero, x], axis=0), jnp.concatenate([x, zero], axis=0)
            )
            rolled.append(pltpu.roll(x, lax.rem(col, LANES), 2))
        inside = lane_id < col
        gobj[0, part, pl.ds(tile, tiles + 1)] += jnp.where(inside, 0.0, rolled[0])
        gobj[1, part, pl.ds(tile, tiles + 1)] += jnp.where(inside, rolled[0], rolled[1])
        gobj[2, part, pl.ds(tile, tiles + 1)] += jnp.where(inside, rolled[1], 0.0)

    def add_probe(part, value):
        for v in range(2):
            gprobe[part, v] += value[:, v * LANES : (v + 1) * LANES]

    at = [corner(slot) for slot in slots]
    win_real = [window(0, a) for a in at]
    win_imag = [window(1, a) for a in at]
    probe_real = jnp.concatenate([probe[0, 0], probe[0, 1]], axis=1)
    probe_imag = jnp.concatenate([probe[1, 0], probe[1, 1]], axis=1)
    far_real, far_imag = transform(
        [probe_real * a - probe_imag * b for a, b in zip(win_real, win_imag)],
        [probe_real * b + probe_imag * a for a, b in zip(win_real, win_imag)],
        left[...],
        right[...],
    )
    misfit = [
        jnp.where(slot < count, a * a + b * b - pattern[slot], 0.0) for a, b, slot in zip(far_real, far_imag, slots)
    ]
    back_real, back_imag = transform(
        [m * a for m, a in zip(misfit, far_real)],
        [m * b for m, b in zip(misfit, far_imag)],
        right[...],
        left[...],
    )
    both = list(zip(win_real, win_imag, back_real, back_imag))
    add_probe(0, sum(a * c + b * d for a, b, c, d in both))
    add_probe(1, sum(a * d - b * c for a, b, c, d in both))
    for i in range(GROUP):
        add_object(0, probe_real * back_real[i] + probe_imag * back_imag[i], at[i])
        add_object(1, probe_real * back_imag[i] - probe_imag * back_real[i], at[i])


def gradient_kernel(
    first,
    count_ref, offset_ref, pattern_ref, left_ref, right_ref, own_ref, side0_ref, side2_ref, start_ref, total_ref,
    out0_ref, own_out_ref, out2_ref, gprobe_ref, probe_ref, peak_ref,
    pattern, left, right, probe, total, ext, gobj, gprobe,
    strip_sems, probe_sems, table_sems, pattern_sems, out_sems,
):
    row, row_places, row_end = place_of(ROW)
    col, col_places, col_end = place_of(COL)
    groups = pattern.shape[0] // GROUP
    count = count_ref[0]

    if first:
        probe_copies = [
            pltpu.make_async_copy(start_ref.at[:, :, pl.ds(v * LANES, LANES)], probe.at[:, v], probe_sems.at[v])
            for v in range(2)
        ]
    else:
        probe_copies = [
            pltpu.make_async_copy(total_ref, total, probe_sems.at[0]),
            pltpu.make_async_copy(start_ref, probe, probe_sems.at[1]),
        ]
    strip_copies = [
        pltpu.make_async_copy(
            ref.at[j],
            ext.at[col_places[j], :, pl.ds(row_places[i] * TILES, TILES)],
            strip_sems.at[i * 3 + j],
        )
        for i, ref in ((1, own_ref), (0, side0_ref), (2, side2_ref))
        for j in range(3)
    ]
    table_copies = [
        pltpu.make_async_copy(left_ref, left, table_sems.at[0]),
        pltpu.make_async_copy(right_ref, right, table_sems.at[1]),
    ]
    pattern_copies = [
        pltpu.make_async_copy(
            pattern_ref.at[pl.ds(g * GROUP, GROUP)], pattern.at[pl.ds(g * GROUP, GROUP)], pattern_sems.at[g]
        )
        for g in range(groups)
    ]
    for copy in probe_copies + strip_copies + table_copies + pattern_copies:
        copy.start()
    gobj[...] = jnp.zeros_like(gobj)
    gprobe[...] = jnp.zeros_like(gprobe)
    for copy in probe_copies:
        copy.wait()
    if not first:
        probe[...] = updated_probe(probe[...], total[...])
    power = probe[0] * probe[0] + probe[1] * probe[1]
    peak_ref[...] = jnp.broadcast_to(jnp.max(power, keepdims=True).reshape(1, 1) + 1e-06, peak_ref.shape)
    for copy in strip_copies:
        copy.wait()

    @pl.when(col_end)
    def _():
        ext[col_places[2]] = jnp.zeros(ext.shape[1:], F32)

    @pl.when(row_end)
    def _():
        ext[:, :, pl.ds(row_places[2] * TILES, TILES)] = jnp.zeros(ext.shape[:2] + (TILES, 8, LANES), F32)

    for copy in table_copies + pattern_copies:
        copy.wait()

    def visit(group, carry):
        pattern_group(group, count, offset_ref, pattern, left, right, probe, ext, gobj, gprobe)
        return carry

    lax.fori_loop(0, (count + GROUP - 1) // GROUP, visit, 0)

    out_copies = [
        pltpu.make_async_copy(gprobe, gprobe_ref, out_sems.at[9]),
        pltpu.make_async_copy(probe, probe_ref, out_sems.at[10]),
    ] + [
        pltpu.make_async_copy(
            gobj.at[col_places[j], :, pl.ds(row_places[i] * TILES, TILES)], ref.at[j], out_sems.at[i * 3 + j]
        )
        for i, ref in ((0, out0_ref), (2, out2_ref), (1, own_out_ref))
        for j in range(3)
    ]
    for copy in out_copies:
        copy.start()
    for copy in out_copies:
        copy.wait()


def gradients(first, count, offsets, patterns, tables, strips, probe, total):
    slots, size = patterns.shape[:2]
    vmem = pl.BlockSpec(memory_space=pltpu.VMEM)
    smem = pl.BlockSpec(memory_space=pltpu.SMEM)
    anywhere = pl.BlockSpec(memory_space=pl.ANY)
    hbm = pl.BlockSpec(memory_space=pltpu.HBM)
    strip = jax.ShapeDtypeStruct((3, 2, TILES, 8, LANES), F32)
    halves = jax.ShapeDtypeStruct((2, 2, size, LANES), F32)
    ext = pltpu.VMEM((3, 2, 3 * TILES, 8, LANES), F32)
    return pl.pallas_call(
        functools.partial(gradient_kernel, first),
        out_shape=(strip, strip, strip, halves, halves, jax.ShapeDtypeStruct((8, LANES), F32)),
        in_specs=[smem, smem] + [anywhere] * 8,
        out_specs=(hbm,) * 5 + (vmem,),
        scratch_shapes=[
            pltpu.VMEM(patterns.shape, F32),
            pltpu.VMEM(tables[0].shape, jnp.bfloat16),
            pltpu.VMEM(tables[1].shape, jnp.bfloat16),
            pltpu.VMEM(halves.shape, F32),
            pltpu.VMEM(halves.shape, F32),
            ext,
            ext,
            pltpu.VMEM(halves.shape, F32),
            pltpu.SemaphoreType.DMA((9,)),
            pltpu.SemaphoreType.DMA((2,)),
            pltpu.SemaphoreType.DMA((2,)),
            pltpu.SemaphoreType.DMA((slots // GROUP,)),
            pltpu.SemaphoreType.DMA((11,)),
        ],
        compiler_params=pltpu.CompilerParams(vmem_limit_bytes=VMEM_BYTES),
    )(count, offsets, patterns, *tables, *strips, probe, total)


def small_call(kernel, out_shapes, *args):
    vmem = pl.BlockSpec(memory_space=pltpu.VMEM)
    return pl.pallas_call(
        kernel,
        out_shape=tuple(jax.ShapeDtypeStruct(shape, F32) for shape in out_shapes),
        in_specs=[vmem] * len(args),
        out_specs=(vmem,) * len(out_shapes),
        compiler_params=pltpu.CompilerParams(vmem_limit_bytes=VMEM_BYTES),
    )(*args)


def sum_copies_kernel(in_ref, out_ref):
    total = in_ref[0]
    for i in range(1, in_ref.shape[0]):
        total = total + in_ref[i]
    for i in range(out_ref.shape[0]):
        out_ref[i] = total


def sum_copies(value, copies):
    return small_call(sum_copies_kernel, [(copies,) + value.shape[1:]], value)[0]


def exchange(value, axes):
    return lax.all_to_all(value, axes, 0, 0, tiled=True)


def total_over_devices(gprobe):
    shape = gprobe.shape
    plane = lax.axis_size(PLANE)
    chunks = gprobe.reshape(plane, -1, LANES)
    shares = sum_copies(exchange(chunks, PLANE), lax.axis_size("z"))
    shares = sum_copies(exchange(shares, "z"), plane)
    return exchange(shares, PLANE).reshape(shape)


def row_sum(own_ref, side0_ref, side2_ref, j):
    at_end = place_of(ROW)[2]
    return own_ref[j] + side0_ref[j] + jnp.where(at_end, 0.0, side2_ref[j])


def far_choice():
    index, places, at_end = place_of(COL)
    return lax.rem(index, 2) == lax.rem(index // 2, 2)


def rows_kernel(own_ref, side0_ref, side2_ref, sum_ref, near0_ref, near2_ref, far0_ref, far2_ref):
    side0, own, side2 = (row_sum(own_ref, side0_ref, side2_ref, j) for j in range(3))
    sum_ref[0], sum_ref[1], sum_ref[2] = side0, own, side2
    near0_ref[0], near0_ref[1] = own, side0
    near2_ref[0], near2_ref[1] = own, side2
    first = far_choice()
    far0_ref[...] = jnp.where(first, side0, side2)
    far2_ref[...] = jnp.where(first, side2, side0)


def update_kernel(strip_ref, sum_ref, near0_ref, near2_ref, far0_ref, far2_ref, peak_ref, out_ref):
    index, places, at_end = place_of(COL)
    inner = (index >= 2, index <= lax.axis_size(COL) - 3)
    odd = lax.rem(index, 2) == 1
    first = far_choice()
    far0 = jnp.where(first, far0_ref[...], far2_ref[...])
    far2 = jnp.where(first, far2_ref[...], far0_ref[...])
    reach0 = jnp.where(odd, inner[0].astype(jnp.int32), inner[1].astype(jnp.int32)) == 1
    reach2 = jnp.where(odd, inner[1].astype(jnp.int32), inner[0].astype(jnp.int32)) == 1
    peak = peak_ref[...]
    grad0 = sum_ref[0] + near0_ref[0] + jnp.where(reach0, far0, 0.0)
    grad = sum_ref[1] + near0_ref[1] + jnp.where(at_end, 0.0, near2_ref[1])
    grad2 = sum_ref[2] + near2_ref[0] + jnp.where(reach2, far2, 0.0)
    out_ref[0] = strip_ref[0] - grad0 / peak
    out_ref[1] = strip_ref[1] - grad / peak
    out_ref[2] = strip_ref[2] - grad2 / peak


def last_rows_kernel(own_ref, side0_ref, side2_ref, sum0_ref, sum1_ref, sum2_ref):
    for j, ref in enumerate((sum0_ref, sum1_ref, sum2_ref)):
        ref[...] = row_sum(own_ref, side0_ref, side2_ref, j)


def last_object_kernel(strip_ref, sum_ref, near0_ref, near2_ref, peak_ref, out_ref):
    at_end = place_of(COL)[2]
    grad = sum_ref[...] + near0_ref[...] + jnp.where(at_end, 0.0, near2_ref[...])
    out_ref[...] = strip_ref[1] - grad / peak_ref[...]


def last_probe_kernel(probe_ref, total_ref, out_ref):
    new = updated_probe(probe_ref[...], total_ref[...])
    for part in range(2):
        for v in range(2):
            out_ref[part, :, v * LANES : (v + 1) * LANES] = new[part, v]


def body(object_field, probe_field, intensity, scan_offsets, pattern_counts):
    size = probe_field.shape[1]
    slots = intensity.shape[2]
    patterns = intensity.reshape(slots, size, size)
    offsets = scan_offsets.reshape(slots, 2).T
    count = pattern_counts.reshape(1)
    tables = dft_tables(size)
    block = (2, TILES, 8, LANES)
    strip_shape = (3,) + block

    own = object_field.reshape(block)
    strip = jnp.stack([paired(own, COL, 0), own, paired(own, COL, 2)])
    strips = (strip, paired(strip, ROW, 0), paired(strip, ROW, 2))
    out0, mid, out2, gprobe, probe, peak = gradients(
        True, count, offsets, patterns, tables, strips, probe_field, probe_field
    )
    total = total_over_devices(gprobe)
    sums, near0, near2, far0, far2 = small_call(
        rows_kernel,
        [strip_shape, (2,) + block, (2,) + block, block, block],
        mid, paired(out0, ROW, 0), paired(out2, ROW, 2),
    )
    (strip,) = small_call(
        update_kernel,
        [strip_shape],
        strip, sums, paired(near0, COL, 0), paired(near2, COL, 2), paired_far(far0, COL, 0), paired_far(far2, COL, 1), peak,
    )
    strips = (strip, paired(strip, ROW, 0), paired(strip, ROW, 2))
    out0, mid, out2, gprobe, probe, peak = gradients(
        False, count, offsets, patterns, tables, strips, probe, total
    )
    total = total_over_devices(gprobe)
    sum0, sum1, sum2 = small_call(
        last_rows_kernel, [block] * 3, mid, paired(out0, ROW, 0), paired(out2, ROW, 2)
    )
    (new_object,) = small_call(
        last_object_kernel, [block], strip, sum1, paired(sum0, COL, 0), paired(sum2, COL, 2), peak
    )
    (new_probe,) = small_call(last_probe_kernel, [probe_field.shape], probe, total)
    return (new_object.reshape(object_field.shape), new_probe)


def solution(mesh):
    split = Mesh(mesh.devices.reshape(4, 2, 8, 4), ("y", "core", "z", "x"))
    in_specs = (
        P(None, ROW, COL),
        P(),
        P(ROW, COL, None, None, None),
        P(ROW, COL, None, None),
        P(ROW, COL),
    )
    out_specs = (P(None, ROW, COL), P())
    return jax.shard_map(body, mesh=split, in_specs=in_specs, out_specs=out_specs, check_vma=False)
```

```python
import functools

import jax
import jax.numpy as jnp
import numpy as np
from jax import lax
from jax.experimental import pallas as pl
from jax.experimental.pallas import tpu as pltpu
from jax.sharding import Mesh, PartitionSpec as P

ROW = ("y", "core")
COL = ("z", "x")
PLANE = ("y", "x")
LANES = 128
TILES = 16
GROUP = 4
F32 = jnp.float32
VMEM_BYTES = 50 * 1024 * 1024


def dft_tables(length):
    index = np.arange(length, dtype=np.int64)
    angle = 2.0 * np.pi / length * (index[:, None] * index[None, :] % length)
    factor = 1.0 / np.sqrt(length)
    cos_table = (np.cos(angle) * factor).astype(np.float32)
    sin_table = (np.sin(angle) * factor).astype(np.float32)
    forward = np.block([[cos_table, sin_table], [-sin_table, cos_table]])
    inverse = np.block([[cos_table, -sin_table], [sin_table, cos_table]])
    return jnp.asarray(forward, jnp.bfloat16), jnp.asarray(inverse, jnp.bfloat16)


def place_of(axes):
    index = lax.axis_index(axes)
    odd = lax.rem(index, 2)
    at_end = (index == 0) | (index == lax.axis_size(axes) - 1)
    return index, (2 - 2 * odd, 1, 2 * odd), at_end


def paired(value, axes, side):
    count = lax.axis_size(axes)
    pairs = [(i, (i + (1 if (i + side // 2) % 2 == 0 else -1)) % count) for i in range(count)]
    return lax.ppermute(value, axes, pairs)


def paired_far(value, axes, phase):
    count = lax.axis_size(axes)
    pairs = [(i, (i + (2 if (i // 2 + phase) % 2 == 0 else -2)) % count) for i in range(count)]
    return lax.ppermute(value, axes, pairs)


def dot(a, b):
    return jnp.dot(a, b, preferred_element_type=F32)


def transform(reals, imags, left, right):
    size = reals[0].shape[0]
    columns = [jnp.concatenate(pair, axis=0).astype(jnp.bfloat16) for pair in zip(reals, imags)]
    mid = dot(left, jnp.concatenate(columns, axis=1)).astype(jnp.bfloat16)
    rows = [
        jnp.concatenate([mid[:size, i * size : (i + 1) * size], mid[size:, i * size : (i + 1) * size]], axis=1)
        for i in range(len(reals))
    ]
    out = dot(jnp.concatenate(rows, axis=0), right)
    return (
        [out[i * size : (i + 1) * size, :size] for i in range(len(reals))],
        [out[i * size : (i + 1) * size, size:] for i in range(len(reals))],
    )


def updated_probe(probe, total):
    mean = jnp.sum(total * total, keepdims=True) / total.size
    return probe - 0.3 * total / jnp.sqrt(mean + 1e-06)


def pattern_group(group, count, slots_ref, pattern, pattern_copy, left, right, probe, ext, gobj, keep, send):
    size = pattern.shape[1]
    region = size // 2
    tiles = size // 8
    slots = [group * GROUP + i for i in range(GROUP)]
    sub_id = lax.broadcasted_iota(jnp.int32, (1, 8, LANES), 1)
    lane_id = lax.broadcasted_iota(jnp.int32, (1, 8, LANES), 2)

    def corner(slot):
        row = slots_ref[0, slot] + region
        col = slots_ref[1, slot] + region
        tile = jnp.minimum(row // 8, region // 8 - 1)
        return tile, row - tile * 8, col

    def window(part, at):
        tile, sub, col = at
        pieces = [
            pltpu.roll(ext[v, part, pl.ds(tile, tiles + 1)], lax.rem(LANES - col, LANES), 2) for v in range(3)
        ]
        halves = []
        for v in range(2):
            x = jnp.where(lane_id < LANES - col, pieces[v], pieces[v + 1])
            x = pltpu.roll(x, lax.rem(8 - sub, 8), 1)
            halves.append(jnp.where(sub_id < 8 - sub, x[:tiles], x[1:]).reshape(size, LANES))
        return jnp.concatenate(halves, axis=1)

    def add_object(part, value, at):
        tile, sub, col = at
        zero = jnp.zeros((1, 8, LANES), F32)
        rolled = []
        for v in range(2):
            x = value[:, v * LANES : (v + 1) * LANES].reshape(tiles, 8, LANES)
            x = pltpu.roll(x, lax.rem(sub, 8), 1)
            x = jnp.where(
                sub_id < sub, jnp.concatenate([zero, x], axis=0), jnp.concatenate([x, zero], axis=0)
            )
            rolled.append(pltpu.roll(x, lax.rem(col, LANES), 2))
        inside = lane_id < col
        gobj[0, part, pl.ds(tile, tiles + 1)] += jnp.where(inside, 0.0, rolled[0])
        gobj[1, part, pl.ds(tile, tiles + 1)] += jnp.where(inside, rolled[0], rolled[1])
        gobj[2, part, pl.ds(tile, tiles + 1)] += jnp.where(inside, rolled[1], 0.0)

    def add_probe(real, imag):
        first = lax.axis_index("core") == 0
        for v in range(2):
            lanes = slice(v * LANES, (v + 1) * LANES)
            keep[v] += jnp.where(first, real[:, lanes], imag[:, lanes])
            send[v] += jnp.where(first, imag[:, lanes], real[:, lanes])

    at = [corner(slot) for slot in slots]
    win_real = [window(0, a) for a in at]
    win_imag = [window(1, a) for a in at]
    probe_real = jnp.concatenate([probe[0, 0], probe[0, 1]], axis=1)
    probe_imag = jnp.concatenate([probe[1, 0], probe[1, 1]], axis=1)
    far_real, far_imag = transform(
        [probe_real * a - probe_imag * b for a, b in zip(win_real, win_imag)],
        [probe_real * b + probe_imag * a for a, b in zip(win_real, win_imag)],
        left[...],
        right[...],
    )
    pattern_copy(group).wait()
    misfit = [
        jnp.where(slot < count, a * a + b * b - pattern[slot], 0.0) for a, b, slot in zip(far_real, far_imag, slots)
    ]
    back_real, back_imag = transform(
        [m * a for m, a in zip(misfit, far_real)],
        [m * b for m, b in zip(misfit, far_imag)],
        right[...],
        left[...],
    )
    both = list(zip(win_real, win_imag, back_real, back_imag))
    add_probe(sum(a * c + b * d for a, b, c, d in both), sum(a * d - b * c for a, b, c, d in both))
    for i in range(GROUP):
        add_object(0, probe_real * back_real[i] + probe_imag * back_imag[i], at[i])
        add_object(1, probe_real * back_imag[i] - probe_imag * back_real[i], at[i])


def gradient_kernel(
    first,
    slots_ref, pattern_ref, left_ref, right_ref, own_ref, side0_ref, side2_ref, start_ref, mine_ref, other_ref,
    out0_ref, own_out_ref, out2_ref, probe_ref, rows_ref, keep, send, peak_ref,
    pattern, left, right, probe, total, ext, gobj,
    strip_sems, probe_sems, table_sems, pattern_sems, rows_sems, out_sems,
):
    row, row_places, row_end = place_of(ROW)
    col, col_places, col_end = place_of(COL)
    core = lax.axis_index("core")
    count = slots_ref[2, 0]
    groups = pattern.shape[0] // GROUP

    def block(ref, row_order, col_order):
        return ref.at[col_places[col_order], :, pl.ds(row_places[row_order] * TILES, TILES)]

    def pattern_copy(group):
        slots = pl.ds(group * GROUP, GROUP)
        return pltpu.make_async_copy(pattern_ref.at[slots], pattern.at[slots], pattern_sems.at[group])

    if first:
        probe_copies = [
            pltpu.make_async_copy(start_ref.at[:, :, pl.ds(v * LANES, LANES)], probe.at[:, v], probe_sems.at[v])
            for v in range(2)
        ]
    else:
        probe_copies = [
            pltpu.make_async_copy(mine_ref, total.at[core], probe_sems.at[0]),
            pltpu.make_async_copy(other_ref, total.at[1 - core], probe_sems.at[1]),
            pltpu.make_async_copy(start_ref, probe, probe_sems.at[2]),
        ]
    strip_copies = [
        pltpu.make_async_copy(
            ref.at[j], block(ext, i, j) if first else block(ext, j, i), strip_sems.at[i * 3 + j]
        )
        for i, ref in ((1, own_ref), (0, side0_ref), (2, side2_ref))
        for j in range(3)
    ]
    table_copies = [
        pltpu.make_async_copy(left_ref, left, table_sems.at[0]),
        pltpu.make_async_copy(right_ref, right, table_sems.at[1]),
    ]
    for copy in probe_copies + strip_copies + table_copies:
        copy.start()
    for group in range(groups):
        pattern_copy(group).start()
    gobj[...] = jnp.zeros_like(gobj)
    keep[...] = jnp.zeros_like(keep)
    send[...] = jnp.zeros_like(send)
    for copy in probe_copies:
        copy.wait()
    if not first:
        probe[...] = updated_probe(probe[...], total[...])
    power = probe[0] * probe[0] + probe[1] * probe[1]
    peak_ref[...] = jnp.broadcast_to(jnp.max(power, keepdims=True).reshape(1, 1) + 1e-06, peak_ref.shape)
    for copy in strip_copies:
        copy.wait()

    @pl.when(col_end)
    def _():
        ext[col_places[2]] = jnp.zeros(ext.shape[1:], F32)

    @pl.when(row_end)
    def _():
        ext[:, :, pl.ds(row_places[2] * TILES, TILES)] = jnp.zeros(ext.shape[:2] + (TILES, 8, LANES), F32)

    side_copies = [pltpu.make_async_copy(probe, probe_ref, rows_sems.at[3])] + [
        pltpu.make_async_copy(block(ext, i, 1), rows_ref.at[i], rows_sems.at[i]) for i in range(3)
    ]
    for copy in side_copies:
        copy.start()
    for copy in table_copies:
        copy.wait()

    def visit(group, carry):
        pattern_group(
            group, count, slots_ref, pattern, pattern_copy, left, right, probe, ext, gobj, keep, send
        )
        return carry

    live_groups = (count + GROUP - 1) // GROUP
    lax.fori_loop(0, live_groups, visit, 0)

    out_copies = [
        pltpu.make_async_copy(block(gobj, j, i) if first else block(gobj, i, j), ref.at[j], out_sems.at[i * 3 + j])
        for i, ref in ((0, out0_ref), (2, out2_ref), (1, own_out_ref))
        for j in range(3)
    ]
    for copy in out_copies:
        copy.start()
    for group in range(1, groups):

        @pl.when(group >= live_groups)
        def _():
            pattern_copy(group).wait()

    for copy in side_copies + out_copies:
        copy.wait()


def gradients(first, live_slots, patterns, tables, strips, *probes):
    slots, size = patterns.shape[:2]
    vmem = pl.BlockSpec(memory_space=pltpu.VMEM)
    smem = pl.BlockSpec(memory_space=pltpu.SMEM)
    hbm = pl.BlockSpec(memory_space=pltpu.HBM)
    anywhere = pl.BlockSpec(memory_space=pl.ANY)
    strip = jax.ShapeDtypeStruct((3, 2, TILES, 8, LANES), F32)
    half = jax.ShapeDtypeStruct((2, size, LANES), F32)
    both = jax.ShapeDtypeStruct((2, 2, size, LANES), F32)
    ext = pltpu.VMEM((3, 2, 3 * TILES, 8, LANES), F32)
    return pl.pallas_call(
        functools.partial(gradient_kernel, first),
        out_shape=(strip, strip, strip, both, strip, half, half, jax.ShapeDtypeStruct((8, LANES), F32)),
        in_specs=[smem, hbm, hbm, hbm] + [anywhere] * 3 + [hbm] + [anywhere] * 2,
        out_specs=(hbm,) * 5 + (vmem,) * 3,
        scratch_shapes=[
            pltpu.VMEM(patterns.shape, F32),
            pltpu.VMEM(tables[0].shape, jnp.bfloat16),
            pltpu.VMEM(tables[1].shape, jnp.bfloat16),
            pltpu.VMEM(both.shape, F32),
            pltpu.VMEM(both.shape, F32),
            ext,
            ext,
            pltpu.SemaphoreType.DMA((9,)),
            pltpu.SemaphoreType.DMA((3,)),
            pltpu.SemaphoreType.DMA((2,)),
            pltpu.SemaphoreType.DMA((slots // GROUP,)),
            pltpu.SemaphoreType.DMA((4,)),
            pltpu.SemaphoreType.DMA((9,)),
        ],
        compiler_params=pltpu.CompilerParams(vmem_limit_bytes=VMEM_BYTES),
    )(live_slots, patterns, *tables, *strips, *probes)


def exchange(value, axes):
    return lax.all_to_all(value, axes, 0, 0, tiled=True)


def core_swap(value):
    return lax.ppermute(value, "core", [(0, 1), (1, 0)])


def sum_steps(keep, send):
    plane = lax.axis_size(PLANE)
    depth = lax.axis_size("z")

    def over_plane():
        half = keep + core_swap(send)
        return exchange(half.reshape(plane, -1, LANES), PLANE).sum(0)

    def over_depth(share):
        return exchange(jnp.broadcast_to(share, (depth,) + share.shape), "z").sum(0)

    def gathered(share):
        mine = exchange(jnp.broadcast_to(share, (plane,) + share.shape), PLANE).reshape(keep.shape)
        return mine, core_swap(mine)

    return over_plane, over_depth, gathered


def side_sum(own, side0, side2, at_end):
    return own + side0 + jnp.where(at_end, 0.0, side2)


def row_reach():
    index = lax.axis_index(ROW)
    odd = lax.rem(index, 2) == 1
    first = lax.rem(index, 2) == lax.rem(index // 2, 2)
    lower, upper = index >= 2, index <= lax.axis_size(ROW) - 3
    return first, jnp.where(odd, lower, upper), jnp.where(odd, upper, lower)


def row_transfers(sums):
    first = row_reach()[0]
    return (
        paired(sums[:2], ROW, 0),
        paired(sums[1:], ROW, 2),
        paired_far(jnp.where(first, sums[0], sums[2]), ROW, 0),
        paired_far(jnp.where(first, sums[2], sums[0]), ROW, 1),
    )


def updated_strip(strip, sums, arrived, peak, at_end):
    near0, near2, far_a, far_b = arrived
    first, reach0, reach2 = row_reach()
    far0, far2 = jnp.where(first, far_a, far_b), jnp.where(first, far_b, far_a)
    grad = jnp.stack(
        [
            sums[0] + near0[1] + jnp.where(reach0, far0, 0.0),
            side_sum(sums[1], near0[0], near2[1], at_end),
            sums[2] + near2[0] + jnp.where(reach2, far2, 0.0),
        ]
    )
    return strip - grad / peak


def last_probe_kernel(probe_ref, mine_ref, other_ref, out_ref):
    first = lax.axis_index("core") == 0
    mine, other = mine_ref[...], other_ref[...]
    total = jnp.stack([jnp.where(first, mine, other), jnp.where(first, other, mine)])
    new = updated_probe(probe_ref[...], total)
    for part in range(2):
        for v in range(2):
            out_ref[part, :, v * LANES : (v + 1) * LANES] = new[part, v]


def last_probe(probe, mine, other):
    vmem = pl.BlockSpec(memory_space=pltpu.VMEM)
    size = probe.shape[2]
    return pl.pallas_call(
        last_probe_kernel,
        out_shape=jax.ShapeDtypeStruct((2, size, 2 * LANES), F32),
        in_specs=[vmem] * 3,
        out_specs=vmem,
        compiler_params=pltpu.CompilerParams(vmem_limit_bytes=8 * 1024 * 1024),
    )(probe, mine, other)


def body(object_field, probe_field, intensity, scan_offsets, pattern_counts):
    size = probe_field.shape[1]
    slots = intensity.shape[2]
    patterns = intensity.reshape(slots, size, size)
    live_slots = jnp.concatenate(
        [scan_offsets.reshape(slots, 2).T, jnp.broadcast_to(pattern_counts, (1, slots))], axis=0
    )
    tables = dft_tables(size)
    row_end, col_end = place_of(ROW)[2], place_of(COL)[2]

    own = object_field.reshape(2, TILES, 8, LANES)
    strip = jnp.stack([paired(own, COL, 0), own, paired(own, COL, 2)])
    strips = (strip, paired(strip, ROW, 0), paired(strip, ROW, 2))
    out0, mid, out2, probe, strip, keep, send, peak = gradients(
        True, live_slots, patterns, tables, strips, probe_field, probe_field, probe_field
    )
    over_plane, over_depth, gathered = sum_steps(keep, send)
    sums = side_sum(mid, paired(out0, COL, 0), paired(out2, COL, 2), col_end)
    share, sums = lax.optimization_barrier((over_plane(), sums))
    strip = updated_strip(strip, sums, row_transfers(sums), peak, row_end)
    share, strip = lax.optimization_barrier((over_depth(share), strip))
    strips = (strip, paired(strip, COL, 0), paired(strip, COL, 2))
    totals = gathered(share)

    out0, mid, out2, probe, strip, keep, send, peak = gradients(
        False, live_slots, patterns, tables, strips, probe, *totals
    )
    over_plane, over_depth, gathered = sum_steps(keep, send)
    sums = side_sum(mid, paired(out0, ROW, 0), paired(out2, ROW, 2), row_end)
    share, sums = lax.optimization_barrier((over_plane(), sums))
    grad = side_sum(sums[1], paired(sums[0], COL, 0), paired(sums[2], COL, 2), col_end)
    new_object = (strip[1] - grad / peak).reshape(object_field.shape)
    share, new_object = lax.optimization_barrier((over_depth(share), new_object))
    return (new_object, last_probe(probe, *gathered(share)))


def solution(mesh):
    split = Mesh(mesh.devices.reshape(4, 2, 8, 4), ("y", "core", "z", "x"))
    in_specs = (
        P(None, ROW, COL),
        P(),
        P(ROW, COL, None, None, None),
        P(ROW, COL, None, None),
        P(ROW, COL),
    )
    out_specs = (P(None, ROW, COL), P())
    return jax.shard_map(body, mesh=split, in_specs=in_specs, out_specs=out_specs, check_vma=False)
```

```python
import functools

import jax
import jax.numpy as jnp
import numpy as np
from jax import lax
from jax.experimental import pallas as pl
from jax.experimental.pallas import tpu as pltpu
from jax.sharding import Mesh, PartitionSpec as P

ROW = ("y", "core")
COL = ("z", "x")
PLANE = ("y", "x")
LANES = 128
TILES = 16
GROUP = 4
F32 = jnp.float32
VMEM_BYTES = 101 * 512 * 1024


def dft_tables(length):
    index = np.arange(length, dtype=np.int64)
    angle = 2.0 * np.pi / length * (index[:, None] * index[None, :] % length)
    factor = 1.0 / np.sqrt(length)
    cos_table = (np.cos(angle) * factor).astype(np.float32)
    sin_table = (np.sin(angle) * factor).astype(np.float32)
    forward = np.block([[cos_table, sin_table], [-sin_table, cos_table]])
    inverse = np.block([[cos_table, -sin_table], [sin_table, cos_table]])
    return jnp.asarray(forward, jnp.bfloat16), jnp.asarray(inverse, jnp.bfloat16)


def place_of(axes):
    index = lax.axis_index(axes)
    odd = lax.rem(index, 2)
    at_end = (index == 0) | (index == lax.axis_size(axes) - 1)
    return index, (2 - 2 * odd, 1, 2 * odd), at_end


def paired(value, axes, side):
    count = lax.axis_size(axes)
    pairs = [(i, (i + (1 if (i + side // 2) % 2 == 0 else -1)) % count) for i in range(count)]
    return lax.ppermute(value, axes, pairs)


def paired_far(value, axes, phase):
    count = lax.axis_size(axes)
    pairs = [(i, (i + (2 if (i // 2 + phase) % 2 == 0 else -2)) % count) for i in range(count)]
    return lax.ppermute(value, axes, pairs)


def dot(a, b):
    return jnp.dot(a, b, preferred_element_type=F32)


def transform_pair(reals, imags, left, right):
    size = reals[0].shape[0]
    columns = [jnp.concatenate(pair, axis=0).astype(jnp.bfloat16) for pair in zip(reals, imags)]
    mid = dot(left, jnp.concatenate(columns, axis=1)).astype(jnp.bfloat16)
    rows = [
        jnp.concatenate([mid[:size, i * size : (i + 1) * size], mid[size:, i * size : (i + 1) * size]], axis=1)
        for i in range(len(reals))
    ]
    out = dot(jnp.concatenate(rows, axis=0), right)
    return [(out[i * size : (i + 1) * size, :size], out[i * size : (i + 1) * size, size:]) for i in range(len(reals))]


def transform(reals, imags, left, right):
    out = []
    for i in range(0, len(reals), 2):
        out += transform_pair(reals[i : i + 2], imags[i : i + 2], left, right)
    return [pair[0] for pair in out], [pair[1] for pair in out]


def updated_probe(probe, total):
    mean = jnp.sum(total * total, keepdims=True) / total.size
    return probe - 0.3 * total / jnp.sqrt(mean + 1e-06)


def pattern_group(group, count, slots_ref, pattern, pattern_copy, left, right, probe, ext, gobj, keep, send):
    size = pattern.shape[1]
    region = size // 2
    tiles = size // 8
    slots = [group * GROUP + i for i in range(GROUP)]
    sub_id = lax.broadcasted_iota(jnp.int32, (1, 8, LANES), 1)
    lane_id = lax.broadcasted_iota(jnp.int32, (1, 8, LANES), 2)

    def corner(slot):
        row = slots_ref[0, slot] + region
        col = slots_ref[1, slot] + region
        tile = jnp.minimum(row // 8, region // 8 - 1)
        return tile, row - tile * 8, col

    def window(part, at):
        tile, sub, col = at
        pieces = [ext[v, part, pl.ds(tile, tiles + 1)] for v in range(3)]
        halves = []
        for v in range(2):
            x = pltpu.roll(jnp.where(lane_id >= col, pieces[v], pieces[v + 1]), lax.rem(LANES - col, LANES), 2)
            x = pltpu.roll(jnp.where(sub_id >= sub, x[:tiles], x[1:]), lax.rem(8 - sub, 8), 1)
            halves.append(x.reshape(size, LANES))
        return jnp.concatenate(halves, axis=1)

    def add_object(part, value, at):
        tile, sub, col = at
        zero = jnp.zeros((1, 8, LANES), F32)
        rolled = []
        for v in range(2):
            x = value[:, v * LANES : (v + 1) * LANES].reshape(tiles, 8, LANES)
            x = pltpu.roll(x, lax.rem(sub, 8), 1)
            x = jnp.where(
                sub_id < sub, jnp.concatenate([zero, x], axis=0), jnp.concatenate([x, zero], axis=0)
            )
            rolled.append(pltpu.roll(x, lax.rem(col, LANES), 2))
        inside = lane_id < col
        gobj[0, part, pl.ds(tile, tiles + 1)] += jnp.where(inside, 0.0, rolled[0])
        gobj[1, part, pl.ds(tile, tiles + 1)] += jnp.where(inside, rolled[0], rolled[1])
        gobj[2, part, pl.ds(tile, tiles + 1)] += jnp.where(inside, rolled[1], 0.0)

    def add_probe(real, imag):
        first = lax.axis_index("core") == 0
        for v in range(2):
            lanes = slice(v * LANES, (v + 1) * LANES)
            keep[v] += jnp.where(first, real[:, lanes], imag[:, lanes])
            send[v] += jnp.where(first, imag[:, lanes], real[:, lanes])

    at = [corner(slot) for slot in slots]
    win_real = [window(0, a) for a in at]
    win_imag = [window(1, a) for a in at]
    probe_real = jnp.concatenate([probe[0, 0], probe[0, 1]], axis=1)
    probe_imag = jnp.concatenate([probe[1, 0], probe[1, 1]], axis=1)
    far_real, far_imag = transform(
        [probe_real * a - probe_imag * b for a, b in zip(win_real, win_imag)],
        [probe_real * b + probe_imag * a for a, b in zip(win_real, win_imag)],
        left[...],
        right[...],
    )
    pattern_copy(group).wait()
    misfit = [
        jnp.where(slot < count, a * a + b * b - pattern[slot], 0.0) for a, b, slot in zip(far_real, far_imag, slots)
    ]
    back_real, back_imag = transform(
        [m * a for m, a in zip(misfit, far_real)],
        [m * b for m, b in zip(misfit, far_imag)],
        right[...],
        left[...],
    )
    both = list(zip(win_real, win_imag, back_real, back_imag))
    add_probe(sum(a * c + b * d for a, b, c, d in both), sum(a * d - b * c for a, b, c, d in both))
    for i in range(GROUP):
        add_object(0, probe_real * back_real[i] + probe_imag * back_imag[i], at[i])
        add_object(1, probe_real * back_imag[i] - probe_imag * back_real[i], at[i])


def gradient_kernel(first, *refs):
    if first:
        slots_ref, pattern_ref, left_ref, right_ref, start_ref, own_ref, side0_ref, side2_ref = refs[:8]
        col0_ref, col1_ref, col2_ref, keep, send, peak_ref, rows_ref = refs[8:15]
    else:
        slots_ref, pattern_ref, left_ref, right_ref, start_ref, own_ref, side0_ref, side2_ref = refs[:8]
        mine_ref, other_ref = refs[8:10]
        col0_ref, col1_ref, col2_ref, keep, send, peak_ref, probe_ref = refs[10:17]
    pattern, left, right, probe, ext, gobj, probe_sems, table_sems, pattern_sems = refs[-9:]
    row, row_places, row_end = place_of(ROW)
    col, col_places, col_end = place_of(COL)
    count = slots_ref[2, 0]
    groups = pattern.shape[0] // GROUP

    def pattern_copy(group):
        slots = pl.ds(group * GROUP, GROUP)
        return pltpu.make_async_copy(pattern_ref.at[slots], pattern.at[slots], pattern_sems.at[group])

    probe_copies = [
        pltpu.make_async_copy(start_ref.at[:, :, pl.ds(v * LANES, LANES)], probe.at[:, v], probe_sems.at[v])
        for v in range(2)
    ]
    table_copies = [
        pltpu.make_async_copy(left_ref, left, table_sems.at[0]),
        pltpu.make_async_copy(right_ref, right, table_sems.at[1]),
    ]
    for copy in probe_copies + table_copies:
        copy.start()
    for group in range(groups):
        pattern_copy(group).start()

    strips = ((1, own_ref, False), (0, side0_ref, False), (2, side2_ref, row_end if first else col_end))
    for i, ref, outside in strips:
        if first:
            for j in range(3):
                bad = outside | col_end if j == 2 else outside
                value = ref[j] if bad is False else jnp.where(bad, 0.0, ref[j])
                ext[col_places[j], :, pl.ds(row_places[i] * TILES, TILES)] = value
        else:
            ext[col_places[i]] = ref[...] if outside is False else jnp.where(outside, 0.0, ref[...])
    if first:
        rows_ref[...] = ext[1]
    gobj[...] = jnp.zeros_like(gobj)
    keep[...] = jnp.zeros_like(keep)
    send[...] = jnp.zeros_like(send)
    for copy in probe_copies:
        copy.wait()
    if not first:
        real = lax.axis_index("core") == 0
        mine, other = mine_ref[...], other_ref[...]
        total = jnp.stack([jnp.where(real, mine, other), jnp.where(real, other, mine)])
        probe[...] = updated_probe(probe[...], total)
        probe_ref[...] = probe[...]
    power = probe[0] * probe[0] + probe[1] * probe[1]
    peak_ref[...] = jnp.broadcast_to(jnp.max(power, keepdims=True).reshape(1, 1) + 1e-06, peak_ref.shape)
    for copy in table_copies:
        copy.wait()

    def visit(group, carry):
        pattern_group(
            group, count, slots_ref, pattern, pattern_copy, left, right, probe, ext, gobj, keep, send
        )
        return carry

    live_groups = (count + GROUP - 1) // GROUP
    lax.fori_loop(0, live_groups, visit, 0)
    for j, ref in enumerate((col0_ref, col1_ref, col2_ref)):
        ref[...] = gobj[col_places[j]]
    for group in range(1, groups):

        @pl.when(group >= live_groups)
        def _():
            pattern_copy(group).wait()


def gradients(first, live_slots, patterns, tables, probe, *vmem_args):
    slots, size = patterns.shape[:2]
    vmem = pl.BlockSpec(memory_space=pltpu.VMEM)
    smem = pl.BlockSpec(memory_space=pltpu.SMEM)
    hbm = pl.BlockSpec(memory_space=pltpu.HBM)
    strip = jax.ShapeDtypeStruct((2, 3 * TILES, 8, LANES), F32)
    half = jax.ShapeDtypeStruct((2, size, LANES), F32)
    both = jax.ShapeDtypeStruct((2, 2, size, LANES), F32)
    ext = pltpu.VMEM((3, 2, 3 * TILES, 8, LANES), F32)
    return pl.pallas_call(
        functools.partial(gradient_kernel, first),
        out_shape=(strip,) * 3 + (half, half, jax.ShapeDtypeStruct((8, LANES), F32), strip if first else both),
        in_specs=[smem] + [hbm] * 4 + [vmem] * len(vmem_args),
        out_specs=(vmem,) * 7,
        scratch_shapes=[
            pltpu.VMEM(patterns.shape, F32),
            pltpu.VMEM(tables[0].shape, jnp.bfloat16),
            pltpu.VMEM(tables[1].shape, jnp.bfloat16),
            pltpu.VMEM(both.shape, F32),
            ext,
            ext,
            pltpu.SemaphoreType.DMA((2,)),
            pltpu.SemaphoreType.DMA((2,)),
            pltpu.SemaphoreType.DMA((slots // GROUP,)),
        ],
        compiler_params=pltpu.CompilerParams(vmem_limit_bytes=VMEM_BYTES),
    )(live_slots, patterns, *tables, probe, *vmem_args)


def exchange(value, axes):
    return lax.all_to_all(value, axes, 0, 0, tiled=True)


def core_swap(value):
    return lax.ppermute(value, "core", [(0, 1), (1, 0)])


def sum_steps(keep, send):
    plane = lax.axis_size(PLANE)
    depth = lax.axis_size("z")

    def over_plane():
        half = keep + core_swap(send)
        return exchange(half.reshape(plane, -1, LANES), PLANE).sum(0)

    def over_depth(share):
        return exchange(jnp.broadcast_to(share, (depth,) + share.shape), "z").sum(0)

    def gathered(share):
        mine = exchange(jnp.broadcast_to(share, (plane,) + share.shape), PLANE).reshape(keep.shape)
        return mine, core_swap(mine)

    return over_plane, over_depth, gathered


def side_sum(own, side0, side2, at_end):
    return own + side0 + jnp.where(at_end, 0.0, side2)


def updated_strip(strip, sums, peak):
    index, places, at_end = place_of(ROW)
    last = lax.axis_size(ROW) - 1
    odd = lax.rem(index, 2) == 1
    down_first = lax.rem(index // 2, 2) == 0
    upper, lower = sums[:, : 2 * TILES], sums[:, TILES:]
    near0 = paired(jnp.where(odd, upper, lower), ROW, 0)
    near2 = paired(jnp.where(odd, lower, upper), ROW, 2)
    above, below = sums[:, :TILES], sums[:, 2 * TILES :]
    far_a = paired_far(jnp.where(down_first, below, above), ROW, 0)
    far_b = paired_far(jnp.where(down_first, above, below), ROW, 1)
    near2 = jnp.where(at_end, 0.0, near2)
    far_b = jnp.where((index < 2) | (index > last - 2), 0.0, far_b)
    from_upper, from_lower = jnp.where(odd, near0, near2), jnp.where(odd, near2, near0)
    grad_above = above + from_upper[:, :TILES] + jnp.where(down_first, far_b, far_a)
    grad = sums[:, TILES : 2 * TILES] + from_upper[:, TILES:] + from_lower[:, :TILES]
    grad_below = below + from_lower[:, TILES:] + jnp.where(down_first, far_a, far_b)
    return jnp.concatenate(
        [
            jnp.where(index == 0, 0.0, strip[:, :TILES] - grad_above / peak),
            strip[:, TILES : 2 * TILES] - grad / peak,
            jnp.where(index == last, 0.0, strip[:, 2 * TILES :] - grad_below / peak),
        ],
        axis=1,
    )


def last_probe_kernel(probe_ref, mine_ref, other_ref, out_ref):
    first = lax.axis_index("core") == 0
    mine, other = mine_ref[...], other_ref[...]
    total = jnp.stack([jnp.where(first, mine, other), jnp.where(first, other, mine)])
    new = updated_probe(probe_ref[...], total)
    for part in range(2):
        for v in range(2):
            out_ref[part, :, v * LANES : (v + 1) * LANES] = new[part, v]


def last_probe(probe, mine, other):
    vmem = pl.BlockSpec(memory_space=pltpu.VMEM)
    size = probe.shape[2]
    return pl.pallas_call(
        last_probe_kernel,
        out_shape=jax.ShapeDtypeStruct((2, size, 2 * LANES), F32),
        in_specs=[vmem] * 3,
        out_specs=vmem,
        compiler_params=pltpu.CompilerParams(vmem_limit_bytes=8 * 1024 * 1024),
    )(probe, mine, other)


def body(object_field, probe_field, intensity, scan_offsets, pattern_counts):
    size = probe_field.shape[1]
    slots = intensity.shape[2]
    patterns = intensity.reshape(slots, size, size)
    live_slots = jnp.concatenate(
        [scan_offsets.reshape(slots, 2).T, jnp.broadcast_to(pattern_counts, (1, slots))], axis=0
    )
    tables = dft_tables(size)
    row_end, col_end = place_of(ROW)[2], place_of(COL)[2]

    own = object_field.reshape(2, TILES, 8, LANES)
    strip = jnp.stack([paired(own, COL, 0), own, paired(own, COL, 2)])
    strips = (strip, paired(strip, ROW, 0), paired(strip, ROW, 2))
    col0, col1, col2, keep, send, peak, strip = gradients(True, live_slots, patterns, tables, probe_field, *strips)
    over_plane, over_depth, gathered = sum_steps(keep, send)
    sums = side_sum(col1, paired(col0, COL, 0), paired(col2, COL, 2), col_end)
    share, sums = lax.optimization_barrier((over_plane(), sums))
    strip = updated_strip(strip, sums, peak)
    share, strip = lax.optimization_barrier((over_depth(share), strip))
    strips = (strip, paired(strip, COL, 0), paired(strip, COL, 2))
    totals = gathered(share)

    col0, col1, col2, keep, send, peak, probe = gradients(
        False, live_slots, patterns, tables, probe_field, *strips, *totals
    )
    over_plane, over_depth, gathered = sum_steps(keep, send)
    sums = side_sum(col1, paired(col0, COL, 0), paired(col2, COL, 2), col_end)
    share, sums = lax.optimization_barrier((over_plane(), sums))
    odd = lax.rem(lax.axis_index(ROW), 2) == 1
    above, grad, below = (sums[:, i * TILES : (i + 1) * TILES] for i in range(3))
    arrived = (paired(jnp.where(odd, above, below), ROW, 0), paired(jnp.where(odd, below, above), ROW, 2))
    grad = side_sum(grad, *arrived, row_end)
    new_object = (strip[:, TILES : 2 * TILES] - grad / peak).reshape(object_field.shape)
    share, new_object = lax.optimization_barrier((over_depth(share), new_object))
    return (new_object, last_probe(probe, *gathered(share)))


def solution(mesh):
    split = Mesh(mesh.devices.reshape(4, 2, 8, 4), ("y", "core", "z", "x"))
    in_specs = (
        P(None, ROW, COL),
        P(),
        P(ROW, COL, None, None, None),
        P(ROW, COL, None, None),
        P(ROW, COL),
    )
    out_specs = (P(None, ROW, COL), P())
    return jax.shard_map(body, mesh=split, in_specs=in_specs, out_specs=out_specs, check_vma=False)
```

```python
import functools

import jax
import jax.numpy as jnp
import numpy as np
from jax import lax
from jax.experimental import pallas as pl
from jax.experimental.pallas import tpu as pltpu
from jax.sharding import Mesh, PartitionSpec as P

ROW = ("y", "core")
COL = ("z", "x")
CHIPS = ("y", "z", "x")
LANES = 128
TILES = 16
GROUP = 4
F32 = jnp.float32
VMEM_BYTES = 101 * 512 * 1024


def dft_tables(length):
    index = np.arange(length, dtype=np.int64)
    angle = 2.0 * np.pi / length * (index[:, None] * index[None, :] % length)
    factor = 1.0 / np.sqrt(length)
    cos_table = (np.cos(angle) * factor).astype(np.float32)
    sin_table = (np.sin(angle) * factor).astype(np.float32)
    forward = np.block([[cos_table, sin_table], [-sin_table, cos_table]])
    inverse = np.block([[cos_table, -sin_table], [sin_table, cos_table]])
    return jnp.asarray(forward, jnp.bfloat16), jnp.asarray(inverse, jnp.bfloat16)


def place_of(axes):
    index = lax.axis_index(axes)
    odd = lax.rem(index, 2)
    at_end = (index == 0) | (index == lax.axis_size(axes) - 1)
    return index, (2 - 2 * odd, 1, 2 * odd), at_end


def paired(value, axes, side):
    count = lax.axis_size(axes)
    pairs = [(i, (i + (1 if (i + side // 2) % 2 == 0 else -1)) % count) for i in range(count)]
    return lax.ppermute(value, axes, pairs)


def paired_far(value, axes, phase):
    count = lax.axis_size(axes)
    pairs = [(i, (i + (2 if (i // 2 + phase) % 2 == 0 else -2)) % count) for i in range(count)]
    return lax.ppermute(value, axes, pairs)


def dot(a, b):
    return jnp.dot(a, b, preferred_element_type=F32)


def transform_pair(reals, imags, left, right):
    size = reals[0].shape[0]
    columns = [jnp.concatenate(pair, axis=0).astype(jnp.bfloat16) for pair in zip(reals, imags)]
    mid = dot(left, jnp.concatenate(columns, axis=1)).astype(jnp.bfloat16)
    rows = [
        jnp.concatenate([mid[:size, i * size : (i + 1) * size], mid[size:, i * size : (i + 1) * size]], axis=1)
        for i in range(len(reals))
    ]
    out = dot(jnp.concatenate(rows, axis=0), right)
    return [(out[i * size : (i + 1) * size, :size], out[i * size : (i + 1) * size, size:]) for i in range(len(reals))]


def transform(reals, imags, left, right):
    out = []
    for i in range(0, len(reals), 2):
        out += transform_pair(reals[i : i + 2], imags[i : i + 2], left, right)
    return [pair[0] for pair in out], [pair[1] for pair in out]


def updated_probe(probe, total):
    mean = jnp.sum(total * total, keepdims=True) / total.size
    return probe - 0.3 * total / jnp.sqrt(mean + 1e-06)


def pattern_group(group, count, slots_ref, pattern, pattern_copy, left, right, probe, ext, gobj, keep, send):
    size = pattern.shape[1]
    region = size // 2
    tiles = size // 8
    slots = [group * GROUP + i for i in range(GROUP)]
    sub_id = lax.broadcasted_iota(jnp.int32, (1, 8, LANES), 1)
    lane_id = lax.broadcasted_iota(jnp.int32, (1, 8, LANES), 2)

    def corner(slot):
        row = slots_ref[0, slot] + region
        col = slots_ref[1, slot] + region
        tile = jnp.minimum(row // 8, region // 8 - 1)
        return tile, row - tile * 8, col

    def window(part, at):
        tile, sub, col = at
        pieces = [ext[v, part, pl.ds(tile, tiles + 1)] for v in range(3)]
        halves = []
        for v in range(2):
            x = pltpu.roll(jnp.where(lane_id >= col, pieces[v], pieces[v + 1]), lax.rem(LANES - col, LANES), 2)
            x = pltpu.roll(jnp.where(sub_id >= sub, x[:tiles], x[1:]), lax.rem(8 - sub, 8), 1)
            halves.append(x.reshape(size, LANES))
        return jnp.concatenate(halves, axis=1)

    def add_object(part, value, at):
        tile, sub, col = at
        zero = jnp.zeros((1, 8, LANES), F32)
        rolled = []
        for v in range(2):
            x = value[:, v * LANES : (v + 1) * LANES].reshape(tiles, 8, LANES)
            x = pltpu.roll(x, lax.rem(sub, 8), 1)
            x = jnp.where(
                sub_id < sub, jnp.concatenate([zero, x], axis=0), jnp.concatenate([x, zero], axis=0)
            )
            rolled.append(pltpu.roll(x, lax.rem(col, LANES), 2))
        inside = lane_id < col
        gobj[0, part, pl.ds(tile, tiles + 1)] += jnp.where(inside, 0.0, rolled[0])
        gobj[1, part, pl.ds(tile, tiles + 1)] += jnp.where(inside, rolled[0], rolled[1])
        gobj[2, part, pl.ds(tile, tiles + 1)] += jnp.where(inside, rolled[1], 0.0)

    def add_probe(real, imag):
        first = lax.axis_index("core") == 0
        for v in range(2):
            lanes = slice(v * LANES, (v + 1) * LANES)
            keep[v] += jnp.where(first, real[:, lanes], imag[:, lanes])
            send[v] += jnp.where(first, imag[:, lanes], real[:, lanes])

    at = [corner(slot) for slot in slots]
    win_real = [window(0, a) for a in at]
    win_imag = [window(1, a) for a in at]
    probe_real = jnp.concatenate([probe[0, 0], probe[0, 1]], axis=1)
    probe_imag = jnp.concatenate([probe[1, 0], probe[1, 1]], axis=1)
    far_real, far_imag = transform(
        [probe_real * a - probe_imag * b for a, b in zip(win_real, win_imag)],
        [probe_real * b + probe_imag * a for a, b in zip(win_real, win_imag)],
        left[...],
        right[...],
    )
    pattern_copy(group).wait()
    misfit = [
        jnp.where(slot < count, a * a + b * b - pattern[slot], 0.0) for a, b, slot in zip(far_real, far_imag, slots)
    ]
    back_real, back_imag = transform(
        [m * a for m, a in zip(misfit, far_real)],
        [m * b for m, b in zip(misfit, far_imag)],
        right[...],
        left[...],
    )
    both = list(zip(win_real, win_imag, back_real, back_imag))
    add_probe(sum(a * c + b * d for a, b, c, d in both), sum(a * d - b * c for a, b, c, d in both))
    for i in range(GROUP):
        add_object(0, probe_real * back_real[i] + probe_imag * back_imag[i], at[i])
        add_object(1, probe_real * back_imag[i] - probe_imag * back_real[i], at[i])


def gradient_kernel(first, *refs):
    if first:
        slots_ref, pattern_ref, left_ref, right_ref, start_ref, own_ref, side0_ref, side2_ref = refs[:8]
        col0_ref, col1_ref, col2_ref, keep, send, peak_ref, rows_ref = refs[8:15]
    else:
        slots_ref, pattern_ref, left_ref, right_ref, start_ref, own_ref, side0_ref, side2_ref = refs[:8]
        mine_ref, other_ref = refs[8:10]
        col0_ref, col1_ref, col2_ref, keep, send, peak_ref, probe_ref = refs[10:17]
    pattern, left, right, probe, ext, gobj, probe_sems, table_sems, pattern_sems = refs[-9:]
    row, row_places, row_end = place_of(ROW)
    col, col_places, col_end = place_of(COL)
    count = slots_ref[2, 0]
    groups = pattern.shape[0] // GROUP

    def pattern_copy(group):
        slots = pl.ds(group * GROUP, GROUP)
        return pltpu.make_async_copy(pattern_ref.at[slots], pattern.at[slots], pattern_sems.at[group])

    probe_copies = [
        pltpu.make_async_copy(start_ref.at[:, :, pl.ds(v * LANES, LANES)], probe.at[:, v], probe_sems.at[v])
        for v in range(2)
    ]
    table_copies = [
        pltpu.make_async_copy(left_ref, left, table_sems.at[0]),
        pltpu.make_async_copy(right_ref, right, table_sems.at[1]),
    ]
    for copy in probe_copies + table_copies:
        copy.start()
    for group in range(groups):
        pattern_copy(group).start()

    strips = ((1, own_ref, False), (0, side0_ref, False), (2, side2_ref, row_end if first else col_end))
    for i, ref, outside in strips:
        if first:
            for j in range(3):
                bad = outside | col_end if j == 2 else outside
                value = ref[j] if bad is False else jnp.where(bad, 0.0, ref[j])
                ext[col_places[j], :, pl.ds(row_places[i] * TILES, TILES)] = value
        else:
            ext[col_places[i]] = ref[...] if outside is False else jnp.where(outside, 0.0, ref[...])
    if first:
        rows_ref[...] = ext[1]
    gobj[...] = jnp.zeros_like(gobj)
    keep[...] = jnp.zeros_like(keep)
    send[...] = jnp.zeros_like(send)
    for copy in probe_copies:
        copy.wait()
    if not first:
        real = lax.axis_index("core") == 0
        mine, other = mine_ref[...], other_ref[...]
        total = jnp.stack([jnp.where(real, mine, other), jnp.where(real, other, mine)])
        probe[...] = updated_probe(probe[...], total)
        probe_ref[...] = probe[...]
    power = probe[0] * probe[0] + probe[1] * probe[1]
    peak_ref[...] = jnp.broadcast_to(jnp.max(power, keepdims=True).reshape(1, 1) + 1e-06, peak_ref.shape)
    for copy in table_copies:
        copy.wait()

    def visit(group, carry):
        pattern_group(
            group, count, slots_ref, pattern, pattern_copy, left, right, probe, ext, gobj, keep, send
        )
        return carry

    live_groups = (count + GROUP - 1) // GROUP
    lax.fori_loop(0, live_groups, visit, 0)
    for j, ref in enumerate((col0_ref, col1_ref, col2_ref)):
        ref[...] = gobj[col_places[j]]
    for group in range(1, groups):

        @pl.when(group >= live_groups)
        def _():
            pattern_copy(group).wait()


def gradients(first, live_slots, patterns, tables, probe, *vmem_args):
    slots, size = patterns.shape[:2]
    vmem = pl.BlockSpec(memory_space=pltpu.VMEM)
    smem = pl.BlockSpec(memory_space=pltpu.SMEM)
    hbm = pl.BlockSpec(memory_space=pltpu.HBM)
    strip = jax.ShapeDtypeStruct((2, 3 * TILES, 8, LANES), F32)
    half = jax.ShapeDtypeStruct((2, size, LANES), F32)
    both = jax.ShapeDtypeStruct((2, 2, size, LANES), F32)
    ext = pltpu.VMEM((3, 2, 3 * TILES, 8, LANES), F32)
    return pl.pallas_call(
        functools.partial(gradient_kernel, first),
        out_shape=(strip,) * 3 + (half, half, jax.ShapeDtypeStruct((8, LANES), F32), strip if first else both),
        in_specs=[smem] + [hbm] * 4 + [vmem] * len(vmem_args),
        out_specs=(vmem,) * 7,
        scratch_shapes=[
            pltpu.VMEM(patterns.shape, F32),
            pltpu.VMEM(tables[0].shape, jnp.bfloat16),
            pltpu.VMEM(tables[1].shape, jnp.bfloat16),
            pltpu.VMEM(both.shape, F32),
            ext,
            ext,
            pltpu.SemaphoreType.DMA((2,)),
            pltpu.SemaphoreType.DMA((2,)),
            pltpu.SemaphoreType.DMA((slots // GROUP,)),
        ],
        compiler_params=pltpu.CompilerParams(vmem_limit_bytes=VMEM_BYTES),
    )(live_slots, patterns, *tables, probe, *vmem_args)


def exchange(value, axes):
    return lax.all_to_all(value, axes, 0, 0, tiled=True)


def core_swap(value):
    return lax.ppermute(value, "core", [(0, 1), (1, 0)])


def shares(keep, send):
    half = keep + core_swap(send)
    return exchange(half.reshape(lax.axis_size(CHIPS), -1, LANES), CHIPS).sum(0)


def gathered(share, shape):
    chips = lax.axis_size(CHIPS)
    mine = exchange(jnp.broadcast_to(share, (chips,) + share.shape), CHIPS).reshape(shape)
    return mine, core_swap(mine)


def side_sum(own, side0, side2, at_end):
    return own + side0 + jnp.where(at_end, 0.0, side2)


def row_payloads(sums):
    index = lax.axis_index(ROW)
    odd = lax.rem(index, 2) == 1
    down_first = lax.rem(index // 2, 2) == 0
    upper, lower = sums[:, : 2 * TILES], sums[:, TILES:]
    above, below = sums[:, :TILES], sums[:, 2 * TILES :]
    return (
        jnp.where(odd, upper, lower),
        jnp.where(odd, lower, upper),
        jnp.where(down_first, below, above),
        jnp.where(down_first, above, below),
    )


def updated_strip(strip, sums, payloads, peak):
    index, places, at_end = place_of(ROW)
    last = lax.axis_size(ROW) - 1
    odd = lax.rem(index, 2) == 1
    down_first = lax.rem(index // 2, 2) == 0
    near0 = paired(payloads[0], ROW, 0)
    near2 = jnp.where(at_end, 0.0, paired(payloads[1], ROW, 2))
    far_a = paired_far(payloads[2], ROW, 0)
    far_b = jnp.where((index < 2) | (index > last - 2), 0.0, paired_far(payloads[3], ROW, 1))
    from_upper, from_lower = jnp.where(odd, near0, near2), jnp.where(odd, near2, near0)
    grad_above = sums[:, :TILES] + from_upper[:, :TILES] + jnp.where(down_first, far_b, far_a)
    grad = sums[:, TILES : 2 * TILES] + from_upper[:, TILES:] + from_lower[:, :TILES]
    grad_below = sums[:, 2 * TILES :] + from_lower[:, TILES:] + jnp.where(down_first, far_a, far_b)
    return jnp.concatenate(
        [
            jnp.where(index == 0, 0.0, strip[:, :TILES] - grad_above / peak),
            strip[:, TILES : 2 * TILES] - grad / peak,
            jnp.where(index == last, 0.0, strip[:, 2 * TILES :] - grad_below / peak),
        ],
        axis=1,
    )


def after(value, *others):
    return lax.optimization_barrier((value, others))[0]


def last_probe_kernel(probe_ref, mine_ref, other_ref, out_ref):
    first = lax.axis_index("core") == 0
    mine, other = mine_ref[...], other_ref[...]
    total = jnp.stack([jnp.where(first, mine, other), jnp.where(first, other, mine)])
    new = updated_probe(probe_ref[...], total)
    for part in range(2):
        for v in range(2):
            out_ref[part, :, v * LANES : (v + 1) * LANES] = new[part, v]


def last_probe(probe, mine, other):
    vmem = pl.BlockSpec(memory_space=pltpu.VMEM)
    size = probe.shape[2]
    return pl.pallas_call(
        last_probe_kernel,
        out_shape=jax.ShapeDtypeStruct((2, size, 2 * LANES), F32),
        in_specs=[vmem] * 3,
        out_specs=vmem,
        compiler_params=pltpu.CompilerParams(vmem_limit_bytes=8 * 1024 * 1024),
    )(probe, mine, other)


def body(object_field, probe_field, intensity, scan_offsets, pattern_counts):
    size = probe_field.shape[1]
    slots = intensity.shape[2]
    patterns = intensity.reshape(slots, size, size)
    live_slots = jnp.concatenate(
        [scan_offsets.reshape(slots, 2).T, jnp.broadcast_to(pattern_counts, (1, slots))], axis=0
    )
    tables = dft_tables(size)
    row_end, col_end = place_of(ROW)[2], place_of(COL)[2]

    own = object_field.reshape(2, TILES, 8, LANES)
    strip = jnp.stack([paired(own, COL, 0), own, paired(own, COL, 2)])
    strips = (strip, paired(strip, ROW, 0), paired(strip, ROW, 2))
    col0, col1, col2, keep, send, peak, strip = gradients(True, live_slots, patterns, tables, probe_field, *strips)
    sums = side_sum(col1, paired(col0, COL, 0), paired(col2, COL, 2), col_end)
    payloads = row_payloads(sums)
    totals = gathered(after(shares(keep, send), *payloads), keep.shape)
    strip = updated_strip(strip, sums, payloads, peak)
    strips = (strip, paired(strip, COL, 0), paired(strip, COL, 2))

    col0, col1, col2, keep, send, peak, probe = gradients(
        False, live_slots, patterns, tables, probe_field, *strips, *totals
    )
    sums = side_sum(col1, paired(col0, COL, 0), paired(col2, COL, 2), col_end)
    odd = lax.rem(lax.axis_index(ROW), 2) == 1
    above, grad, below = (sums[:, i * TILES : (i + 1) * TILES] for i in range(3))
    payloads = (jnp.where(odd, above, below), jnp.where(odd, below, above))
    totals = gathered(after(shares(keep, send), *payloads), keep.shape)
    grad = side_sum(grad, paired(payloads[0], ROW, 0), paired(payloads[1], ROW, 2), row_end)
    new_object = (strip[:, TILES : 2 * TILES] - grad / peak).reshape(object_field.shape)
    return (new_object, last_probe(probe, *totals))


def solution(mesh):
    split = Mesh(mesh.devices.reshape(4, 2, 8, 4), ("y", "core", "z", "x"))
    in_specs = (
        P(None, ROW, COL),
        P(),
        P(ROW, COL, None, None, None),
        P(ROW, COL, None, None),
        P(ROW, COL),
    )
    out_specs = (P(None, ROW, COL), P())
    return jax.shard_map(body, mesh=split, in_specs=in_specs, out_specs=out_specs, check_vma=False)
```

```python
import functools

import jax
import jax.numpy as jnp
import numpy as np
from jax import lax
from jax.experimental import pallas as pl
from jax.experimental.pallas import tpu as pltpu
from jax.sharding import Mesh, PartitionSpec as P

ROW = ("y", "core")
COL = ("z", "x")
PLANE = ("y", "x")
LANES = 128
TILES = 16
GROUP = 4
F32 = jnp.float32
VMEM_BYTES = 102 * 512 * 1024


def dft_tables(length):
    index = np.arange(length, dtype=np.int64)
    angle = 2.0 * np.pi / length * (index[:, None] * index[None, :] % length)
    factor = 1.0 / np.sqrt(length)
    cos_table = (np.cos(angle) * factor).astype(np.float32)
    sin_table = (np.sin(angle) * factor).astype(np.float32)
    forward = np.block([[cos_table, sin_table], [-sin_table, cos_table]])
    inverse = np.block([[cos_table, -sin_table], [sin_table, cos_table]])
    return jnp.asarray(forward, jnp.bfloat16), jnp.asarray(inverse, jnp.bfloat16)


def place_of(axes):
    index = lax.axis_index(axes)
    odd = lax.rem(index, 2)
    at_end = (index == 0) | (index == lax.axis_size(axes) - 1)
    return index, (2 - 2 * odd, 1, 2 * odd), at_end


def paired(value, axes, side):
    count = lax.axis_size(axes)
    pairs = [(i, (i + (1 if (i + side // 2) % 2 == 0 else -1)) % count) for i in range(count)]
    return lax.ppermute(value, axes, pairs)


def paired_far(value, axes, phase):
    count = lax.axis_size(axes)
    pairs = [(i, (i + (2 if (i // 2 + phase) % 2 == 0 else -2)) % count) for i in range(count)]
    return lax.ppermute(value, axes, pairs)


def dot(a, b):
    return jnp.dot(a, b, preferred_element_type=F32)


def transform_pair(reals, imags, left, right):
    size = reals[0].shape[0]
    columns = [jnp.concatenate(pair, axis=0).astype(jnp.bfloat16) for pair in zip(reals, imags)]
    mid = dot(left, jnp.concatenate(columns, axis=1)).astype(jnp.bfloat16)
    rows = [
        jnp.concatenate([mid[:size, i * size : (i + 1) * size], mid[size:, i * size : (i + 1) * size]], axis=1)
        for i in range(len(reals))
    ]
    out = dot(jnp.concatenate(rows, axis=0), right)
    return [(out[i * size : (i + 1) * size, :size], out[i * size : (i + 1) * size, size:]) for i in range(len(reals))]


def transform(reals, imags, left, right):
    out = []
    for i in range(0, len(reals), 2):
        out += transform_pair(reals[i : i + 2], imags[i : i + 2], left, right)
    return [pair[0] for pair in out], [pair[1] for pair in out]


def updated_probe(probe, total):
    mean = jnp.sum(total * total, keepdims=True) / total.size
    return probe - 0.3 * total / jnp.sqrt(mean + 1e-06)


def pattern_group(group, count, slots_ref, pattern, pattern_copy, left, right, probe, ext, gobj, keep, send):
    size = pattern.shape[1]
    region = size // 2
    tiles = size // 8
    slots = [group * GROUP + i for i in range(GROUP)]
    sub_id = lax.broadcasted_iota(jnp.int32, (1, 8, LANES), 1)
    lane_id = lax.broadcasted_iota(jnp.int32, (1, 8, LANES), 2)

    def corner(slot):
        row = slots_ref[0, slot] + region
        col = slots_ref[1, slot] + region
        tile = jnp.minimum(row // 8, region // 8 - 1)
        return tile, row - tile * 8, col

    def window(part, at):
        tile, sub, col = at
        pieces = [ext[v, part, pl.ds(tile, tiles + 1)] for v in range(3)]
        halves = []
        for v in range(2):
            x = pltpu.roll(jnp.where(lane_id >= col, pieces[v], pieces[v + 1]), lax.rem(LANES - col, LANES), 2)
            x = pltpu.roll(jnp.where(sub_id >= sub, x[:tiles], x[1:]), lax.rem(8 - sub, 8), 1)
            halves.append(x.reshape(size, LANES))
        return jnp.concatenate(halves, axis=1)

    def add_object(part, value, at):
        tile, sub, col = at
        zero = jnp.zeros((1, 8, LANES), F32)
        rolled = []
        for v in range(2):
            x = value[:, v * LANES : (v + 1) * LANES].reshape(tiles, 8, LANES)
            x = pltpu.roll(x, lax.rem(sub, 8), 1)
            x = jnp.where(
                sub_id < sub, jnp.concatenate([zero, x], axis=0), jnp.concatenate([x, zero], axis=0)
            )
            rolled.append(pltpu.roll(x, lax.rem(col, LANES), 2))
        inside = lane_id < col
        gobj[0, part, pl.ds(tile, tiles + 1)] += jnp.where(inside, 0.0, rolled[0])
        gobj[1, part, pl.ds(tile, tiles + 1)] += jnp.where(inside, rolled[0], rolled[1])
        gobj[2, part, pl.ds(tile, tiles + 1)] += jnp.where(inside, rolled[1], 0.0)

    def add_probe(real, imag):
        first = lax.axis_index("core") == 0
        for v in range(2):
            lanes = slice(v * LANES, (v + 1) * LANES)
            keep[v] += jnp.where(first, real[:, lanes], imag[:, lanes])
            send[v] += jnp.where(first, imag[:, lanes], real[:, lanes])

    at = [corner(slot) for slot in slots]
    win_real = [window(0, a) for a in at]
    win_imag = [window(1, a) for a in at]
    probe_real = jnp.concatenate([probe[0, 0], probe[0, 1]], axis=1)
    probe_imag = jnp.concatenate([probe[1, 0], probe[1, 1]], axis=1)
    far_real, far_imag = transform(
        [probe_real * a - probe_imag * b for a, b in zip(win_real, win_imag)],
        [probe_real * b + probe_imag * a for a, b in zip(win_real, win_imag)],
        left[...],
        right[...],
    )
    pattern_copy(group).wait()
    misfit = [
        jnp.where(slot < count, a * a + b * b - pattern[slot], 0.0) for a, b, slot in zip(far_real, far_imag, slots)
    ]
    back_real, back_imag = transform(
        [m * a for m, a in zip(misfit, far_real)],
        [m * b for m, b in zip(misfit, far_imag)],
        right[...],
        left[...],
    )
    both = list(zip(win_real, win_imag, back_real, back_imag))
    add_probe(sum(a * c + b * d for a, b, c, d in both), sum(a * d - b * c for a, b, c, d in both))
    for i in range(GROUP):
        add_object(0, probe_real * back_real[i] + probe_imag * back_imag[i], at[i])
        add_object(1, probe_real * back_imag[i] - probe_imag * back_real[i], at[i])


def gradient_kernel(first, *refs):
    slots_ref, pattern_ref, left_ref, right_ref, start_ref, own_ref, side0_ref, side2_ref = refs[:8]
    if first:
        row0_ref, row1_ref, row2_ref, keep, send, peak_ref = refs[8:14]
    else:
        mine_ref, other_ref = refs[8:10]
        row0_ref, row1_ref, row2_ref, keep, send, peak_ref, probe_ref = refs[10:17]
    pattern, left, right, probe, ext, gobj, probe_sems, table_sems, pattern_sems = refs[-9:]
    row, row_places, row_end = place_of(ROW)
    count = slots_ref[2, 0]
    groups = pattern.shape[0] // GROUP

    def pattern_copy(group):
        slots = pl.ds(group * GROUP, GROUP)
        return pltpu.make_async_copy(pattern_ref.at[slots], pattern.at[slots], pattern_sems.at[group])

    probe_copies = [
        pltpu.make_async_copy(start_ref.at[:, :, pl.ds(v * LANES, LANES)], probe.at[:, v], probe_sems.at[v])
        for v in range(2)
    ]
    table_copies = [
        pltpu.make_async_copy(left_ref, left, table_sems.at[0]),
        pltpu.make_async_copy(right_ref, right, table_sems.at[1]),
    ]
    for copy in probe_copies + table_copies:
        copy.start()
    for group in range(groups):
        pattern_copy(group).start()

    for i, ref in ((1, own_ref), (0, side0_ref), (2, side2_ref)):
        value = jnp.where(row_end, 0.0, ref[...]) if i == 2 else ref[...]
        ext[:, :, pl.ds(row_places[i] * TILES, TILES)] = value
    gobj[...] = jnp.zeros_like(gobj)
    keep[...] = jnp.zeros_like(keep)
    send[...] = jnp.zeros_like(send)
    for copy in probe_copies:
        copy.wait()
    if not first:
        real = lax.axis_index("core") == 0
        mine, other = mine_ref[...], other_ref[...]
        total = jnp.stack([jnp.where(real, mine, other), jnp.where(real, other, mine)])
        probe[...] = updated_probe(probe[...], total)
        probe_ref[...] = probe[...]
    power = probe[0] * probe[0] + probe[1] * probe[1]
    peak_ref[...] = jnp.broadcast_to(jnp.max(power, keepdims=True).reshape(1, 1) + 1e-06, peak_ref.shape)
    for copy in table_copies:
        copy.wait()

    def visit(group, carry):
        pattern_group(
            group, count, slots_ref, pattern, pattern_copy, left, right, probe, ext, gobj, keep, send
        )
        return carry

    live_groups = (count + GROUP - 1) // GROUP
    lax.fori_loop(0, live_groups, visit, 0)
    for i, ref in enumerate((row0_ref, row1_ref, row2_ref)):
        ref[...] = gobj[:, :, pl.ds(row_places[i] * TILES, TILES)]
    for group in range(1, groups):

        @pl.when(group >= live_groups)
        def _():
            pattern_copy(group).wait()


def gradients(first, live_slots, patterns, tables, probe, *vmem_args):
    slots, size = patterns.shape[:2]
    vmem = pl.BlockSpec(memory_space=pltpu.VMEM)
    smem = pl.BlockSpec(memory_space=pltpu.SMEM)
    hbm = pl.BlockSpec(memory_space=pltpu.HBM)
    strip = jax.ShapeDtypeStruct((3, 2, TILES, 8, LANES), F32)
    half = jax.ShapeDtypeStruct((2, size, LANES), F32)
    both = jax.ShapeDtypeStruct((2, 2, size, LANES), F32)
    ext = pltpu.VMEM((3, 2, 3 * TILES, 8, LANES), F32)
    return pl.pallas_call(
        functools.partial(gradient_kernel, first),
        out_shape=(strip,) * 3 + (half, half, jax.ShapeDtypeStruct((8, LANES), F32)) + (() if first else (both,)),
        in_specs=[smem] + [hbm] * 4 + [vmem] * len(vmem_args),
        out_specs=(vmem,) * (6 if first else 7),
        scratch_shapes=[
            pltpu.VMEM(patterns.shape, F32),
            pltpu.VMEM(tables[0].shape, jnp.bfloat16),
            pltpu.VMEM(tables[1].shape, jnp.bfloat16),
            pltpu.VMEM(both.shape, F32),
            ext,
            ext,
            pltpu.SemaphoreType.DMA((2,)),
            pltpu.SemaphoreType.DMA((2,)),
            pltpu.SemaphoreType.DMA((slots // GROUP,)),
        ],
        compiler_params=pltpu.CompilerParams(vmem_limit_bytes=VMEM_BYTES),
    )(live_slots, patterns, *tables, probe, *vmem_args)


def exchange(value, axes):
    return lax.all_to_all(value, axes, 0, 0, tiled=True)


def core_swap(value):
    return lax.ppermute(value, "core", [(0, 1), (1, 0)])


def plane_shares(keep, send):
    half = keep + core_swap(send)
    return exchange(half.reshape(lax.axis_size(PLANE), -1, LANES), PLANE).sum(0)


def depth_sum(share):
    return exchange(jnp.broadcast_to(share, (lax.axis_size("z"),) + share.shape), "z").sum(0)


def gathered(share, shape):
    plane = lax.axis_size(PLANE)
    return exchange(jnp.broadcast_to(share, (plane,) + share.shape), PLANE).reshape(shape)


def side_sum(own, side0, side2, at_end):
    return own + side0 + jnp.where(at_end, 0.0, side2)


def column_payloads(sums):
    index = lax.axis_index(COL)
    odd = lax.rem(index, 2) == 1
    right_first = lax.rem(index // 2, 2) == 0
    return (
        jnp.where(odd, sums[:2], sums[1:]),
        jnp.where(odd, sums[1:], sums[:2]),
        jnp.where(right_first, sums[2], sums[0]),
        jnp.where(right_first, sums[0], sums[2]),
    )


def column_transfers(payloads):
    near0, near2, far_a, far_b = payloads
    return paired(near0, COL, 0), paired(near2, COL, 2), paired_far(far_a, COL, 0), paired_far(far_b, COL, 1)


def updated_strip(strip, sums, arrived, peak):
    index, places, at_end = place_of(COL)
    last = lax.axis_size(COL) - 1
    odd = lax.rem(index, 2) == 1
    right_first = lax.rem(index // 2, 2) == 0
    near0, near2, far_a, far_b = arrived
    near2 = jnp.where(at_end, 0.0, near2)
    far_b = jnp.where((index < 2) | (index > last - 2), 0.0, far_b)
    from_left, from_right = jnp.where(odd, near0, near2), jnp.where(odd, near2, near0)
    grad_left = sums[0] + from_left[0] + jnp.where(right_first, far_b, far_a)
    grad = sums[1] + from_left[1] + from_right[0]
    grad_right = sums[2] + from_right[1] + jnp.where(right_first, far_a, far_b)
    return jnp.stack(
        [
            jnp.where(index == 0, 0.0, strip[0] - grad_left / peak),
            strip[1] - grad / peak,
            jnp.where(index == last, 0.0, strip[2] - grad_right / peak),
        ]
    )


def after(value, *others):
    return lax.optimization_barrier((value, others))[0]


def last_probe_kernel(probe_ref, mine_ref, other_ref, out_ref):
    first = lax.axis_index("core") == 0
    mine, other = mine_ref[...], other_ref[...]
    total = jnp.stack([jnp.where(first, mine, other), jnp.where(first, other, mine)])
    new = updated_probe(probe_ref[...], total)
    for part in range(2):
        for v in range(2):
            out_ref[part, :, v * LANES : (v + 1) * LANES] = new[part, v]


def last_probe(probe, mine, other):
    vmem = pl.BlockSpec(memory_space=pltpu.VMEM)
    size = probe.shape[2]
    return pl.pallas_call(
        last_probe_kernel,
        out_shape=jax.ShapeDtypeStruct((2, size, 2 * LANES), F32),
        in_specs=[vmem] * 3,
        out_specs=vmem,
        compiler_params=pltpu.CompilerParams(vmem_limit_bytes=8 * 1024 * 1024),
    )(probe, mine, other)


def body(object_field, probe_field, intensity, scan_offsets, pattern_counts):
    size = probe_field.shape[1]
    slots = intensity.shape[2]
    patterns = intensity.reshape(slots, size, size)
    live_slots = jnp.concatenate(
        [scan_offsets.reshape(slots, 2).T, jnp.broadcast_to(pattern_counts, (1, slots))], axis=0
    )
    tables = dft_tables(size)
    row_end, col_end = place_of(ROW)[2], place_of(COL)[2]
    odd = lax.rem(lax.axis_index(COL), 2) == 1

    own = object_field.reshape(2, TILES, 8, LANES)
    side0, side2 = paired(own, COL, 0), jnp.where(col_end, 0.0, paired(own, COL, 2))
    strip = jnp.stack([jnp.where(odd, side0, side2), own, jnp.where(odd, side2, side0)])
    strips = (strip, paired(strip, ROW, 0), paired(strip, ROW, 2))
    row0, row1, row2, keep, send, peak = gradients(True, live_slots, patterns, tables, probe_field, *strips)
    arrived = (paired(row0, ROW, 0), paired(row2, ROW, 2))
    share, arrived = lax.optimization_barrier((plane_shares(keep, send), arrived))
    sums = side_sum(row1, *arrived, row_end)
    payloads = column_payloads(sums)
    arrived = column_transfers(payloads)
    share, arrived = lax.optimization_barrier((depth_sum(after(share, *payloads)), arrived))
    strip = updated_strip(strip, sums, arrived, peak)
    sides = (paired(strip, ROW, 0), paired(strip, ROW, 2))
    mine, sides = lax.optimization_barrier((gathered(after(share, strip), keep.shape), sides))
    totals = (mine, core_swap(mine))

    strips = (strip,) + sides
    row0, row1, row2, keep, send, peak, probe = gradients(
        False, live_slots, patterns, tables, probe_field, *strips, *totals
    )
    sums = side_sum(row1, paired(row0, ROW, 0), paired(row2, ROW, 2), row_end)
    payloads = (jnp.where(odd, sums[0], sums[2]), jnp.where(odd, sums[2], sums[0]))
    share = after(plane_shares(keep, send), *payloads)
    grad = side_sum(sums[1], paired(payloads[0], COL, 0), paired(payloads[1], COL, 2), col_end)
    new_object = (strip[1] - grad / peak).reshape(object_field.shape)
    mine = gathered(after(depth_sum(share), new_object), keep.shape)
    return (new_object, last_probe(probe, mine, core_swap(mine)))


def solution(mesh):
    split = Mesh(mesh.devices.reshape(4, 2, 8, 4), ("y", "core", "z", "x"))
    in_specs = (
        P(None, ROW, COL),
        P(),
        P(ROW, COL, None, None, None),
        P(ROW, COL, None, None),
        P(ROW, COL),
    )
    out_specs = (P(None, ROW, COL), P())
    return jax.shard_map(body, mesh=split, in_specs=in_specs, out_specs=out_specs, check_vma=False)
```

```python
import functools

import jax
import jax.numpy as jnp
import numpy as np
from jax import lax
from jax.experimental import pallas as pl
from jax.experimental.pallas import tpu as pltpu
from jax.sharding import Mesh, PartitionSpec as P

ROW = ("y", "core")
COL = ("z", "x")
PLANE = ("y", "x")
LANES = 128
TILES = 16
GROUP = 4
F32 = jnp.float32
VMEM_BYTES = 102 * 512 * 1024


def dft_tables(length):
    index = np.arange(length, dtype=np.int64)
    angle = 2.0 * np.pi / length * (index[:, None] * index[None, :] % length)
    factor = 1.0 / np.sqrt(length)
    cos_table = (np.cos(angle) * factor).astype(np.float32)
    sin_table = (np.sin(angle) * factor).astype(np.float32)
    forward = np.block([[cos_table, sin_table], [-sin_table, cos_table]])
    inverse = np.block([[cos_table, -sin_table], [sin_table, cos_table]])
    return jnp.asarray(forward, jnp.bfloat16), jnp.asarray(inverse, jnp.bfloat16)


def place_of(axes):
    index = lax.axis_index(axes)
    odd = lax.rem(index, 2)
    at_end = (index == 0) | (index == lax.axis_size(axes) - 1)
    return index, (2 - 2 * odd, 1, 2 * odd), at_end


def paired(value, axes, side):
    count = lax.axis_size(axes)
    pairs = [(i, (i + (1 if (i + side // 2) % 2 == 0 else -1)) % count) for i in range(count)]
    return lax.ppermute(value, axes, pairs)


def paired_far(value, axes, phase):
    count = lax.axis_size(axes)
    pairs = [(i, (i + (2 if (i // 2 + phase) % 2 == 0 else -2)) % count) for i in range(count)]
    return lax.ppermute(value, axes, pairs)


def dot(a, b):
    return jnp.dot(a, b, preferred_element_type=F32)


def updated_probe(probe, total):
    mean = jnp.sum(total * total, keepdims=True) / total.size
    return probe - 0.3 * total / jnp.sqrt(mean + 1e-06)


def pattern_group(group, count, slots_ref, pattern, pattern_copy, left, right, probe, ext, gobj, keep, send):
    size = pattern.shape[1]
    region = size // 2
    tiles = size // 8
    slots = [group * GROUP + i for i in range(GROUP)]
    sub_id = lax.broadcasted_iota(jnp.int32, (1, 8, LANES), 1)
    lane_id = lax.broadcasted_iota(jnp.int32, (1, 8, LANES), 2)

    def corner(slot):
        row = slots_ref[0, slot] + region
        col = slots_ref[1, slot] + region
        tile = jnp.minimum(row // 8, region // 8 - 1)
        return tile, row - tile * 8, col

    def window(part, at):
        tile, sub, col = at
        pieces = [ext[v, part, pl.ds(tile, tiles + 1)] for v in range(3)]
        halves = []
        for v in range(2):
            x = pltpu.roll(jnp.where(lane_id >= col, pieces[v], pieces[v + 1]), lax.rem(LANES - col, LANES), 2)
            x = pltpu.roll(jnp.where(sub_id >= sub, x[:tiles], x[1:]), lax.rem(8 - sub, 8), 1)
            halves.append(x.reshape(size, LANES))
        return jnp.concatenate(halves, axis=1)

    def add_object(part, value, at):
        tile, sub, col = at
        zero = jnp.zeros((1, 8, LANES), F32)
        rolled = []
        for v in range(2):
            x = value[:, v * LANES : (v + 1) * LANES].reshape(tiles, 8, LANES)
            x = pltpu.roll(x, lax.rem(sub, 8), 1)
            x = jnp.where(
                sub_id < sub, jnp.concatenate([zero, x], axis=0), jnp.concatenate([x, zero], axis=0)
            )
            rolled.append(pltpu.roll(x, lax.rem(col, LANES), 2))
        inside = lane_id < col
        gobj[0, part, pl.ds(tile, tiles + 1)] += jnp.where(inside, 0.0, rolled[0])
        gobj[1, part, pl.ds(tile, tiles + 1)] += jnp.where(inside, rolled[0], rolled[1])
        gobj[2, part, pl.ds(tile, tiles + 1)] += jnp.where(inside, rolled[1], 0.0)

    def add_probe(real, imag):
        first = lax.axis_index("core") == 0
        for v in range(2):
            lanes = slice(v * LANES, (v + 1) * LANES)
            keep[v] += jnp.where(first, real[:, lanes], imag[:, lanes])
            send[v] += jnp.where(first, imag[:, lanes], real[:, lanes])

    probe_real = jnp.concatenate([probe[0, 0], probe[0, 1]], axis=1)
    probe_imag = jnp.concatenate([probe[1, 0], probe[1, 1]], axis=1)
    lanes2 = range(2)

    def windows(pair):
        at = [corner(slot) for slot in pair]
        return at, [window(0, a) for a in at], [window(1, a) for a in at]

    def exits(state):
        at, reals, imags = state
        return [
            jnp.concatenate([probe_real * a - probe_imag * b, probe_real * b + probe_imag * a], axis=0).astype(jnp.bfloat16)
            for a, b in zip(reals, imags)
        ]

    def left_side(columns, table):
        mid = dot(table[...], jnp.concatenate(columns, axis=1)).astype(jnp.bfloat16)
        return jnp.concatenate(
            [
                jnp.concatenate([mid[:size, i * size : (i + 1) * size], mid[size:, i * size : (i + 1) * size]], axis=1)
                for i in lanes2
            ],
            axis=0,
        )

    def right_side(rows, table):
        out = dot(rows, table[...])
        return [(out[i * size : (i + 1) * size, :size], out[i * size : (i + 1) * size, size:]) for i in lanes2]

    def misfits(far, pair):
        out = []
        for (a, b), slot in zip(far, pair):
            m = jnp.where(slot < count, a * a + b * b - pattern[slot], 0.0)
            out.append(jnp.concatenate([m * a, m * b], axis=0).astype(jnp.bfloat16))
        return out

    def add(state, back):
        both = list(zip(state[1], state[2], back))
        add_probe(sum(a * c + b * d for a, b, (c, d) in both), sum(a * d - b * c for a, b, (c, d) in both))
        for a, (c, d) in zip(state[0], back):
            add_object(0, probe_real * c + probe_imag * d, a)
            add_object(1, probe_real * d - probe_imag * c, a)

    pairs = slots[:2], slots[2:]
    state_a = windows(pairs[0])
    mid_a = left_side(exits(state_a), left)
    state_b = windows(pairs[1])
    exit_b = exits(state_b)
    far_a = right_side(mid_a, right)
    mid_b = left_side(exit_b, left)
    pattern_copy(group).wait()
    misfit_a = misfits(far_a, pairs[0])
    far_b = right_side(mid_b, right)
    mid_a = left_side(misfit_a, right)
    misfit_b = misfits(far_b, pairs[1])
    back_a = right_side(mid_a, left)
    mid_b = left_side(misfit_b, right)
    add(state_a, back_a)
    back_b = right_side(mid_b, left)
    add(state_b, back_b)


def gradient_kernel(first, *refs):
    slots_ref, pattern_ref, left_ref, right_ref, start_ref, own_ref, side0_ref, side2_ref = refs[:8]
    if first:
        row0_ref, row1_ref, row2_ref, keep, send, peak_ref = refs[8:14]
    else:
        mine_ref, other_ref = refs[8:10]
        row0_ref, row1_ref, row2_ref, keep, send, peak_ref, probe_ref = refs[10:17]
    pattern, left, right, probe, ext, gobj, probe_sems, table_sems, pattern_sems = refs[-9:]
    row, row_places, row_end = place_of(ROW)
    count = slots_ref[2, 0]
    groups = pattern.shape[0] // GROUP

    def pattern_copy(group):
        slots = pl.ds(group * GROUP, GROUP)
        return pltpu.make_async_copy(pattern_ref.at[slots], pattern.at[slots], pattern_sems.at[group])

    probe_copies = [
        pltpu.make_async_copy(start_ref.at[:, :, pl.ds(v * LANES, LANES)], probe.at[:, v], probe_sems.at[v])
        for v in range(2)
    ]
    table_copies = [
        pltpu.make_async_copy(left_ref, left, table_sems.at[0]),
        pltpu.make_async_copy(right_ref, right, table_sems.at[1]),
    ]
    for copy in probe_copies + table_copies:
        copy.start()

    for i, ref in ((1, own_ref), (0, side0_ref), (2, side2_ref)):
        value = jnp.where(row_end, 0.0, ref[...]) if i == 2 else ref[...]
        ext[:, :, pl.ds(row_places[i] * TILES, TILES)] = value
    gobj[...] = jnp.zeros_like(gobj)
    keep[...] = jnp.zeros_like(keep)
    send[...] = jnp.zeros_like(send)
    for copy in probe_copies:
        copy.wait()
    if not first:
        real = lax.axis_index("core") == 0
        mine, other = mine_ref[...], other_ref[...]
        total = jnp.stack([jnp.where(real, mine, other), jnp.where(real, other, mine)])
        probe[...] = updated_probe(probe[...], total)
        probe_ref[...] = probe[...]
    power = probe[0] * probe[0] + probe[1] * probe[1]
    peak_ref[...] = jnp.broadcast_to(jnp.max(power, keepdims=True).reshape(1, 1) + 1e-06, peak_ref.shape)
    for copy in table_copies:
        copy.wait()
    for group in range(groups):
        pattern_copy(group).start()

    def visit(group, carry):
        pattern_group(
            group, count, slots_ref, pattern, pattern_copy, left, right, probe, ext, gobj, keep, send
        )
        return carry

    live_groups = (count + GROUP - 1) // GROUP
    lax.fori_loop(0, live_groups, visit, 0)
    for i, ref in enumerate((row0_ref, row1_ref, row2_ref)):
        ref[...] = gobj[:, :, pl.ds(row_places[i] * TILES, TILES)]
    for group in range(1, groups):

        @pl.when(group >= live_groups)
        def _():
            pattern_copy(group).wait()


def gradients(first, live_slots, patterns, tables, probe, *vmem_args):
    slots, size = patterns.shape[:2]
    vmem = pl.BlockSpec(memory_space=pltpu.VMEM)
    smem = pl.BlockSpec(memory_space=pltpu.SMEM)
    hbm = pl.BlockSpec(memory_space=pltpu.HBM)
    strip = jax.ShapeDtypeStruct((3, 2, TILES, 8, LANES), F32)
    half = jax.ShapeDtypeStruct((2, size, LANES), F32)
    both = jax.ShapeDtypeStruct((2, 2, size, LANES), F32)
    ext = pltpu.VMEM((3, 2, 3 * TILES, 8, LANES), F32)
    return pl.pallas_call(
        functools.partial(gradient_kernel, first),
        out_shape=(strip,) * 3 + (half, half, jax.ShapeDtypeStruct((8, LANES), F32)) + (() if first else (both,)),
        in_specs=[smem] + [hbm] * 4 + [vmem] * len(vmem_args),
        out_specs=(vmem,) * (6 if first else 7),
        scratch_shapes=[
            pltpu.VMEM(patterns.shape, F32),
            pltpu.VMEM(tables[0].shape, jnp.bfloat16),
            pltpu.VMEM(tables[1].shape, jnp.bfloat16),
            pltpu.VMEM(both.shape, F32),
            ext,
            ext,
            pltpu.SemaphoreType.DMA((2,)),
            pltpu.SemaphoreType.DMA((2,)),
            pltpu.SemaphoreType.DMA((slots // GROUP,)),
        ],
        compiler_params=pltpu.CompilerParams(vmem_limit_bytes=VMEM_BYTES),
    )(live_slots, patterns, *tables, probe, *vmem_args)


def exchange(value, axes):
    return lax.all_to_all(value, axes, 0, 0, tiled=True)


def core_swap(value):
    return lax.ppermute(value, "core", [(0, 1), (1, 0)])


def plane_shares(keep, send):
    half = keep + core_swap(send)
    return exchange(half.reshape(lax.axis_size(PLANE), -1, LANES), PLANE)


def depth_shares(shares):
    share = shares.sum(0)
    return exchange(jnp.broadcast_to(share, (lax.axis_size("z"),) + share.shape), "z")


def gathered(shares, shape):
    plane = lax.axis_size(PLANE)
    share = shares.sum(0)
    return exchange(jnp.broadcast_to(share, (plane,) + share.shape), PLANE).reshape(shape)


def side_sum(own, side0, side2, at_end):
    return own + side0 + jnp.where(at_end, 0.0, side2)


def column_payloads(sums):
    index = lax.axis_index(COL)
    odd = lax.rem(index, 2) == 1
    right_first = lax.rem(index // 2, 2) == 0
    return (
        jnp.where(odd, sums[:2], sums[1:]),
        jnp.where(odd, sums[1:], sums[:2]),
        jnp.where(right_first, sums[2], sums[0]),
        jnp.where(right_first, sums[0], sums[2]),
    )


def column_transfers(payloads):
    near0, near2, far_a, far_b = payloads
    return paired(near0, COL, 0), paired(near2, COL, 2), paired_far(far_a, COL, 0), paired_far(far_b, COL, 1)


def updated_strip(strip, sums, arrived, peak):
    index, places, at_end = place_of(COL)
    last = lax.axis_size(COL) - 1
    odd = lax.rem(index, 2) == 1
    right_first = lax.rem(index // 2, 2) == 0
    near0, near2, far_a, far_b = arrived
    near2 = jnp.where(at_end, 0.0, near2)
    far_b = jnp.where((index < 2) | (index > last - 2), 0.0, far_b)
    from_left, from_right = jnp.where(odd, near0, near2), jnp.where(odd, near2, near0)
    grad_left = sums[0] + from_left[0] + jnp.where(right_first, far_b, far_a)
    grad = sums[1] + from_left[1] + from_right[0]
    grad_right = sums[2] + from_right[1] + jnp.where(right_first, far_a, far_b)
    return jnp.stack(
        [
            jnp.where(index == 0, 0.0, strip[0] - grad_left / peak),
            strip[1] - grad / peak,
            jnp.where(index == last, 0.0, strip[2] - grad_right / peak),
        ]
    )


def after(value, *others):
    return lax.optimization_barrier((value, others))[0]


def last_probe_kernel(probe_ref, mine_ref, other_ref, out_ref):
    first = lax.axis_index("core") == 0
    mine, other = mine_ref[...], other_ref[...]
    total = jnp.stack([jnp.where(first, mine, other), jnp.where(first, other, mine)])
    new = updated_probe(probe_ref[...], total)
    for part in range(2):
        for v in range(2):
            out_ref[part, :, v * LANES : (v + 1) * LANES] = new[part, v]


def last_probe(probe, mine, other):
    vmem = pl.BlockSpec(memory_space=pltpu.VMEM)
    size = probe.shape[2]
    return pl.pallas_call(
        last_probe_kernel,
        out_shape=jax.ShapeDtypeStruct((2, size, 2 * LANES), F32),
        in_specs=[vmem] * 3,
        out_specs=vmem,
        compiler_params=pltpu.CompilerParams(vmem_limit_bytes=8 * 1024 * 1024),
    )(probe, mine, other)


def body(object_field, probe_field, intensity, scan_offsets, pattern_counts):
    size = probe_field.shape[1]
    slots = intensity.shape[2]
    patterns = intensity.reshape(slots, size, size)
    live_slots = jnp.concatenate(
        [scan_offsets.reshape(slots, 2).T, jnp.broadcast_to(pattern_counts, (1, slots))], axis=0
    )
    tables = dft_tables(size)
    row_end, col_end = place_of(ROW)[2], place_of(COL)[2]
    odd = lax.rem(lax.axis_index(COL), 2) == 1

    own = object_field.reshape(2, TILES, 8, LANES)
    side0, side2 = paired(own, COL, 0), jnp.where(col_end, 0.0, paired(own, COL, 2))
    strip = jnp.stack([jnp.where(odd, side0, side2), own, jnp.where(odd, side2, side0)])
    strips = (strip, paired(strip, ROW, 0), paired(strip, ROW, 2))
    row0, row1, row2, keep, send, peak = gradients(True, live_slots, patterns, tables, probe_field, *strips)
    arrived = (paired(row0, ROW, 0), paired(row2, ROW, 2))
    shares, arrived = lax.optimization_barrier((plane_shares(keep, send), arrived))
    sums = side_sum(row1, *arrived, row_end)
    payloads = column_payloads(sums)
    arrived = column_transfers(payloads)
    shares, arrived = lax.optimization_barrier((depth_shares(after(shares, *payloads)), arrived))
    strip = updated_strip(strip, sums, arrived, peak)
    sides = (paired(strip, ROW, 0), paired(strip, ROW, 2))
    mine, sides = lax.optimization_barrier((gathered(after(shares, strip), keep.shape), sides))
    totals = (mine, core_swap(mine))

    strips = (strip,) + sides
    row0, row1, row2, keep, send, peak, probe = gradients(
        False, live_slots, patterns, tables, probe_field, *strips, *totals
    )
    sums = side_sum(row1, paired(row0, ROW, 0), paired(row2, ROW, 2), row_end)
    payloads = (jnp.where(odd, sums[0], sums[2]), jnp.where(odd, sums[2], sums[0]))
    shares = after(plane_shares(keep, send), *payloads)
    grad = side_sum(sums[1], paired(payloads[0], COL, 0), paired(payloads[1], COL, 2), col_end)
    new_object = (strip[1] - grad / peak).reshape(object_field.shape)
    mine = gathered(after(depth_shares(shares), new_object), keep.shape)
    return (new_object, last_probe(probe, mine, core_swap(mine)))


def solution(mesh):
    split = Mesh(mesh.devices.reshape(4, 2, 8, 4), ("y", "core", "z", "x"))
    in_specs = (
        P(None, ROW, COL),
        P(),
        P(ROW, COL, None, None, None),
        P(ROW, COL, None, None),
        P(ROW, COL),
    )
    out_specs = (P(None, ROW, COL), P())
    return jax.shard_map(body, mesh=split, in_specs=in_specs, out_specs=out_specs, check_vma=False)
```

```python
import functools

import jax
import jax.numpy as jnp
import numpy as np
from jax import lax
from jax.experimental import pallas as pl
from jax.experimental.pallas import tpu as pltpu
from jax.sharding import Mesh, PartitionSpec as P

ROW = ("y", "core")
COL = ("z", "x")
PLANE = ("y", "x")
LANES = 128
TILES = 16
GROUP = 4
F32 = jnp.float32
VMEM_BYTES = 101 * 512 * 1024


def dft_tables(length):
    index = np.arange(length, dtype=np.int64)
    angle = 2.0 * np.pi / length * (index[:, None] * index[None, :] % length)
    factor = 1.0 / np.sqrt(length)
    cos_table = (np.cos(angle) * factor).astype(np.float32)
    sin_table = (np.sin(angle) * factor).astype(np.float32)
    forward = np.block([[cos_table, sin_table], [-sin_table, cos_table]])
    inverse = np.block([[cos_table, -sin_table], [sin_table, cos_table]])
    return jnp.asarray(forward, jnp.bfloat16), jnp.asarray(inverse, jnp.bfloat16)


def place_of(axes):
    index = lax.axis_index(axes)
    odd = lax.rem(index, 2)
    at_end = (index == 0) | (index == lax.axis_size(axes) - 1)
    return index, (2 - 2 * odd, 1, 2 * odd), at_end


def paired(value, axes, side):
    count = lax.axis_size(axes)
    pairs = [(i, (i + (1 if (i + side // 2) % 2 == 0 else -1)) % count) for i in range(count)]
    return lax.ppermute(value, axes, pairs)


def paired_far(value, axes, phase):
    count = lax.axis_size(axes)
    pairs = [(i, (i + (2 if (i // 2 + phase) % 2 == 0 else -2)) % count) for i in range(count)]
    return lax.ppermute(value, axes, pairs)


def dot(a, b):
    return jnp.dot(a, b, preferred_element_type=F32)


def updated_probe(probe, total):
    mean = jnp.sum(total * total, keepdims=True) / total.size
    return probe - 0.3 * total / jnp.sqrt(mean + 1e-06)


def pattern_group(group, count, slots_ref, pattern, pattern_copy, left, right, probe, ext, gobj, keep, send):
    size = pattern.shape[1]
    region = size // 2
    tiles = size // 8
    slots = [group * GROUP + i for i in range(GROUP)]
    sub_id = lax.broadcasted_iota(jnp.int32, (1, 8, LANES), 1)
    lane_id = lax.broadcasted_iota(jnp.int32, (1, 8, LANES), 2)

    def corner(slot):
        row = slots_ref[0, slot] + region
        col = slots_ref[1, slot] + region
        tile = jnp.minimum(row // 8, region // 8 - 1)
        return tile, row - tile * 8, col

    def window(part, at):
        tile, sub, col = at
        pieces = [ext[v, part, pl.ds(tile, tiles + 1)] for v in range(3)]
        halves = []
        for v in range(2):
            x = pltpu.roll(jnp.where(lane_id >= col, pieces[v], pieces[v + 1]), lax.rem(LANES - col, LANES), 2)
            x = pltpu.roll(jnp.where(sub_id >= sub, x[:tiles], x[1:]), lax.rem(8 - sub, 8), 1)
            halves.append(x.reshape(size, LANES))
        return jnp.concatenate(halves, axis=1)

    def add_object(part, value, at):
        tile, sub, col = at
        zero = jnp.zeros((1, 8, LANES), F32)
        rolled = []
        for v in range(2):
            x = value[:, v * LANES : (v + 1) * LANES].reshape(tiles, 8, LANES)
            x = pltpu.roll(x, lax.rem(sub, 8), 1)
            x = jnp.where(
                sub_id < sub, jnp.concatenate([zero, x], axis=0), jnp.concatenate([x, zero], axis=0)
            )
            rolled.append(pltpu.roll(x, lax.rem(col, LANES), 2))
        inside = lane_id < col
        gobj[0, part, pl.ds(tile, tiles + 1)] += jnp.where(inside, 0.0, rolled[0])
        gobj[1, part, pl.ds(tile, tiles + 1)] += jnp.where(inside, rolled[0], rolled[1])
        gobj[2, part, pl.ds(tile, tiles + 1)] += jnp.where(inside, rolled[1], 0.0)

    def add_probe(real, imag):
        first = lax.axis_index("core") == 0
        for v in range(2):
            lanes = slice(v * LANES, (v + 1) * LANES)
            keep[v] += jnp.where(first, real[:, lanes], imag[:, lanes])
            send[v] += jnp.where(first, imag[:, lanes], real[:, lanes])

    probe_real = jnp.concatenate([probe[0, 0], probe[0, 1]], axis=1)
    probe_imag = jnp.concatenate([probe[1, 0], probe[1, 1]], axis=1)
    lanes2 = range(2)

    def windows(pair):
        at = [corner(slot) for slot in pair]
        return at, [window(0, a) for a in at], [window(1, a) for a in at]

    def exits(state):
        at, reals, imags = state
        return [
            jnp.concatenate([probe_real * a - probe_imag * b, probe_real * b + probe_imag * a], axis=0).astype(jnp.bfloat16)
            for a, b in zip(reals, imags)
        ]

    def left_side(columns, table):
        mid = dot(table[...], jnp.concatenate(columns, axis=1)).astype(jnp.bfloat16)
        return jnp.concatenate(
            [
                jnp.concatenate([mid[:size, i * size : (i + 1) * size], mid[size:, i * size : (i + 1) * size]], axis=1)
                for i in lanes2
            ],
            axis=0,
        )

    def right_side(rows, table):
        out = dot(rows, table[...])
        return [(out[i * size : (i + 1) * size, :size], out[i * size : (i + 1) * size, size:]) for i in lanes2]

    def misfits(far, pair):
        out = []
        for (a, b), slot in zip(far, pair):
            m = jnp.where(slot < count, a * a + b * b - pattern[slot], 0.0)
            out.append(jnp.concatenate([m * a, m * b], axis=0).astype(jnp.bfloat16))
        return out

    def add(state, back):
        both = list(zip(state[1], state[2], back))
        add_probe(sum(a * c + b * d for a, b, (c, d) in both), sum(a * d - b * c for a, b, (c, d) in both))
        for a, (c, d) in zip(state[0], back):
            add_object(0, probe_real * c + probe_imag * d, a)
            add_object(1, probe_real * d - probe_imag * c, a)

    pairs = slots[:2], slots[2:]
    state_a = windows(pairs[0])
    mid_a = left_side(exits(state_a), left)
    state_b = windows(pairs[1])
    exit_b = exits(state_b)
    far_a = right_side(mid_a, right)
    mid_b = left_side(exit_b, left)
    pattern_copy(group).wait()
    misfit_a = misfits(far_a, pairs[0])
    far_b = right_side(mid_b, right)
    mid_a = left_side(misfit_a, right)
    misfit_b = misfits(far_b, pairs[1])
    back_a = right_side(mid_a, left)
    mid_b = left_side(misfit_b, right)
    add(state_a, back_a)
    back_b = right_side(mid_b, left)
    add(state_b, back_b)


def gradient_kernel(first, *refs):
    slots_ref, pattern_ref, left_ref, right_ref, start_ref, own_ref, side0_ref, side2_ref = refs[:8]
    if first:
        out0_ref, out1_ref, out2_ref, keep, send, peak_ref, rows_ref = refs[8:15]
    else:
        mine_ref, other_ref = refs[8:10]
        out0_ref, out1_ref, out2_ref, keep, send, peak_ref, probe_ref = refs[10:17]
    pattern, left, right, probe, ext, gobj, probe_sems, table_sems, pattern_sems = refs[-9:]
    row, row_places, row_end = place_of(ROW)
    col, col_places, col_end = place_of(COL)
    count = slots_ref[2, 0]
    groups = pattern.shape[0] // GROUP

    def pattern_copy(group):
        slots = pl.ds(group * GROUP, GROUP)
        return pltpu.make_async_copy(pattern_ref.at[slots], pattern.at[slots], pattern_sems.at[group])

    probe_copies = [
        pltpu.make_async_copy(start_ref.at[:, :, pl.ds(v * LANES, LANES)], probe.at[:, v], probe_sems.at[v])
        for v in range(2)
    ]
    table_copies = [
        pltpu.make_async_copy(left_ref, left, table_sems.at[0]),
        pltpu.make_async_copy(right_ref, right, table_sems.at[1]),
    ]
    for copy in probe_copies + table_copies:
        copy.start()

    for i, ref in ((1, own_ref), (0, side0_ref), (2, side2_ref)):
        value = jnp.where(row_end if first else col_end, 0.0, ref[...]) if i == 2 else ref[...]
        if first:
            ext[:, :, pl.ds(row_places[i] * TILES, TILES)] = value
        else:
            ext[col_places[i]] = value
    if first:
        rows_ref[...] = ext[1]
    gobj[...] = jnp.zeros_like(gobj)
    keep[...] = jnp.zeros_like(keep)
    send[...] = jnp.zeros_like(send)
    for copy in probe_copies:
        copy.wait()
    if not first:
        real = lax.axis_index("core") == 0
        mine, other = mine_ref[...], other_ref[...]
        total = jnp.stack([jnp.where(real, mine, other), jnp.where(real, other, mine)])
        probe[...] = updated_probe(probe[...], total)
        probe_ref[...] = probe[...]
    power = probe[0] * probe[0] + probe[1] * probe[1]
    peak_ref[...] = jnp.broadcast_to(jnp.max(power, keepdims=True).reshape(1, 1) + 1e-06, peak_ref.shape)
    for copy in table_copies:
        copy.wait()
    for group in range(groups):
        pattern_copy(group).start()

    def visit(group, carry):
        pattern_group(
            group, count, slots_ref, pattern, pattern_copy, left, right, probe, ext, gobj, keep, send
        )
        return carry

    live_groups = (count + GROUP - 1) // GROUP
    lax.fori_loop(0, live_groups, visit, 0)
    for i, ref in enumerate((out0_ref, out1_ref, out2_ref)):
        ref[...] = gobj[col_places[i]] if first else gobj[:, :, pl.ds(row_places[i] * TILES, TILES)]
    for group in range(1, groups):

        @pl.when(group >= live_groups)
        def _():
            pattern_copy(group).wait()


def gradients(first, live_slots, patterns, tables, probe, *vmem_args):
    slots, size = patterns.shape[:2]
    vmem = pl.BlockSpec(memory_space=pltpu.VMEM)
    smem = pl.BlockSpec(memory_space=pltpu.SMEM)
    hbm = pl.BlockSpec(memory_space=pltpu.HBM)
    row_strip = jax.ShapeDtypeStruct((3, 2, TILES, 8, LANES), F32)
    col_strip = jax.ShapeDtypeStruct((2, 3 * TILES, 8, LANES), F32)
    half = jax.ShapeDtypeStruct((2, size, LANES), F32)
    both = jax.ShapeDtypeStruct((2, 2, size, LANES), F32)
    ext = pltpu.VMEM((3, 2, 3 * TILES, 8, LANES), F32)
    return pl.pallas_call(
        functools.partial(gradient_kernel, first),
        out_shape=(
            (col_strip if first else row_strip,) * 3
            + (half, half, jax.ShapeDtypeStruct((8, LANES), F32), col_strip if first else both)
        ),
        in_specs=[smem] + [hbm] * 4 + [vmem] * len(vmem_args),
        out_specs=(vmem,) * 7,
        scratch_shapes=[
            pltpu.VMEM(patterns.shape, F32),
            pltpu.VMEM(tables[0].shape, jnp.bfloat16),
            pltpu.VMEM(tables[1].shape, jnp.bfloat16),
            pltpu.VMEM(both.shape, F32),
            ext,
            ext,
            pltpu.SemaphoreType.DMA((2,)),
            pltpu.SemaphoreType.DMA((2,)),
            pltpu.SemaphoreType.DMA((slots // GROUP,)),
        ],
        compiler_params=pltpu.CompilerParams(vmem_limit_bytes=VMEM_BYTES),
    )(live_slots, patterns, *tables, probe, *vmem_args)


def exchange(value, axes):
    return lax.all_to_all(value, axes, 0, 0, tiled=True)


def core_swap(value):
    return lax.ppermute(value, "core", [(0, 1), (1, 0)])


def plane_shares(keep, send):
    half = keep + core_swap(send)
    return exchange(half.reshape(lax.axis_size(PLANE), -1, LANES), PLANE)


def depth_shares(shares):
    share = shares.sum(0)
    return exchange(jnp.broadcast_to(share, (lax.axis_size("z"),) + share.shape), "z")


def gathered(shares, shape):
    plane = lax.axis_size(PLANE)
    share = shares.sum(0)
    return exchange(jnp.broadcast_to(share, (plane,) + share.shape), PLANE).reshape(shape)


def side_sum(own, side0, side2, at_end):
    return own + side0 + jnp.where(at_end, 0.0, side2)


def row_payloads(sums):
    index = lax.axis_index(ROW)
    odd = lax.rem(index, 2) == 1
    down_first = lax.rem(index // 2, 2) == 0
    upper, lower = sums[:, : 2 * TILES], sums[:, TILES:]
    above, below = sums[:, :TILES], sums[:, 2 * TILES :]
    return (
        jnp.where(odd, upper, lower),
        jnp.where(odd, lower, upper),
        jnp.where(down_first, below, above),
        jnp.where(down_first, above, below),
    )


def row_transfers(payloads):
    near0, near2, far_a, far_b = payloads
    return paired(near0, ROW, 0), paired(near2, ROW, 2), paired_far(far_a, ROW, 0), paired_far(far_b, ROW, 1)


def updated_strip(strip, sums, arrived, peak):
    index, places, at_end = place_of(ROW)
    last = lax.axis_size(ROW) - 1
    odd = lax.rem(index, 2) == 1
    down_first = lax.rem(index // 2, 2) == 0
    near0, near2, far_a, far_b = arrived
    near2 = jnp.where(at_end, 0.0, near2)
    far_b = jnp.where((index < 2) | (index > last - 2), 0.0, far_b)
    from_upper, from_lower = jnp.where(odd, near0, near2), jnp.where(odd, near2, near0)
    grad_above = sums[:, :TILES] + from_upper[:, :TILES] + jnp.where(down_first, far_b, far_a)
    grad = sums[:, TILES : 2 * TILES] + from_upper[:, TILES:] + from_lower[:, :TILES]
    grad_below = sums[:, 2 * TILES :] + from_lower[:, TILES:] + jnp.where(down_first, far_a, far_b)
    return jnp.concatenate(
        [
            jnp.where(index == 0, 0.0, strip[:, :TILES] - grad_above / peak),
            strip[:, TILES : 2 * TILES] - grad / peak,
            jnp.where(index == last, 0.0, strip[:, 2 * TILES :] - grad_below / peak),
        ],
        axis=1,
    )


def after(value, *others):
    return lax.optimization_barrier((value, others))[0]


def last_probe_kernel(probe_ref, mine_ref, other_ref, out_ref):
    first = lax.axis_index("core") == 0
    mine, other = mine_ref[...], other_ref[...]
    total = jnp.stack([jnp.where(first, mine, other), jnp.where(first, other, mine)])
    new = updated_probe(probe_ref[...], total)
    for part in range(2):
        for v in range(2):
            out_ref[part, :, v * LANES : (v + 1) * LANES] = new[part, v]


def last_probe(probe, mine, other):
    vmem = pl.BlockSpec(memory_space=pltpu.VMEM)
    size = probe.shape[2]
    return pl.pallas_call(
        last_probe_kernel,
        out_shape=jax.ShapeDtypeStruct((2, size, 2 * LANES), F32),
        in_specs=[vmem] * 3,
        out_specs=vmem,
        compiler_params=pltpu.CompilerParams(vmem_limit_bytes=8 * 1024 * 1024),
    )(probe, mine, other)


def body(object_field, probe_field, intensity, scan_offsets, pattern_counts):
    size = probe_field.shape[1]
    slots = intensity.shape[2]
    patterns = intensity.reshape(slots, size, size)
    live_slots = jnp.concatenate(
        [scan_offsets.reshape(slots, 2).T, jnp.broadcast_to(pattern_counts, (1, slots))], axis=0
    )
    tables = dft_tables(size)
    row_end, col_end = place_of(ROW)[2], place_of(COL)[2]
    odd = lax.rem(lax.axis_index(COL), 2) == 1

    own = object_field.reshape(2, TILES, 8, LANES)
    side0, side2 = paired(own, COL, 0), jnp.where(col_end, 0.0, paired(own, COL, 2))
    strip = jnp.stack([jnp.where(odd, side0, side2), own, jnp.where(odd, side2, side0)])
    strips = (strip, paired(strip, ROW, 0), paired(strip, ROW, 2))
    col0, col1, col2, keep, send, peak, strip = gradients(True, live_slots, patterns, tables, probe_field, *strips)
    arrived = (paired(col0, COL, 0), paired(col2, COL, 2))
    shares, arrived = lax.optimization_barrier((plane_shares(keep, send), arrived))
    sums = side_sum(col1, *arrived, col_end)
    payloads = row_payloads(sums)
    arrived = row_transfers(payloads)
    shares, arrived = lax.optimization_barrier((depth_shares(after(shares, *payloads)), arrived))
    strip = updated_strip(strip, sums, arrived, peak)
    sides = (paired(strip, COL, 0), paired(strip, COL, 2))
    mine, sides = lax.optimization_barrier((gathered(after(shares, strip), keep.shape), sides))
    totals = (mine, core_swap(mine))

    strips = (strip,) + sides
    row0, row1, row2, keep, send, peak, probe = gradients(
        False, live_slots, patterns, tables, probe_field, *strips, *totals
    )
    sums = side_sum(row1, paired(row0, ROW, 0), paired(row2, ROW, 2), row_end)
    payloads = (jnp.where(odd, sums[0], sums[2]), jnp.where(odd, sums[2], sums[0]))
    shares = after(plane_shares(keep, send), *payloads)
    grad = side_sum(sums[1], paired(payloads[0], COL, 0), paired(payloads[1], COL, 2), col_end)
    new_object = (strip[:, TILES : 2 * TILES] - grad / peak).reshape(object_field.shape)
    mine = gathered(after(depth_shares(shares), new_object), keep.shape)
    return (new_object, last_probe(probe, mine, core_swap(mine)))


def solution(mesh):
    split = Mesh(mesh.devices.reshape(4, 2, 8, 4), ("y", "core", "z", "x"))
    in_specs = (
        P(None, ROW, COL),
        P(),
        P(ROW, COL, None, None, None),
        P(ROW, COL, None, None),
        P(ROW, COL),
    )
    out_specs = (P(None, ROW, COL), P())
    return jax.shard_map(body, mesh=split, in_specs=in_specs, out_specs=out_specs, check_vma=False)
```

```python
import functools

import jax
import jax.numpy as jnp
import numpy as np
from jax import lax
from jax.experimental import pallas as pl
from jax.experimental.pallas import tpu as pltpu
from jax.sharding import Mesh, PartitionSpec as P

ROW = ("y", "core")
COL = ("z", "x")
PLANE = ("y", "x")
LANES = 128
TILES = 16
GROUP = 4
F32 = jnp.float32
VMEM_BYTES = 102 * 512 * 1024


def dft_tables(length):
    index = np.arange(length, dtype=np.int64)
    angle = 2.0 * np.pi / length * (index[:, None] * index[None, :] % length)
    factor = 1.0 / np.sqrt(length)
    cos_table = (np.cos(angle) * factor).astype(np.float32)
    sin_table = (np.sin(angle) * factor).astype(np.float32)
    forward = np.block([[cos_table, sin_table], [-sin_table, cos_table]])
    inverse = np.block([[cos_table, -sin_table], [sin_table, cos_table]])
    return jnp.asarray(forward, jnp.bfloat16), jnp.asarray(inverse, jnp.bfloat16)


def place_of(axes):
    index = lax.axis_index(axes)
    odd = lax.rem(index, 2)
    at_end = (index == 0) | (index == lax.axis_size(axes) - 1)
    return index, (2 - 2 * odd, 1, 2 * odd), at_end


def paired(value, axes, side):
    count = lax.axis_size(axes)
    pairs = [(i, (i + (1 if (i + side // 2) % 2 == 0 else -1)) % count) for i in range(count)]
    return lax.ppermute(value, axes, pairs)


def paired_far(value, axes, phase):
    count = lax.axis_size(axes)
    pairs = [(i, (i + (2 if (i // 2 + phase) % 2 == 0 else -2)) % count) for i in range(count)]
    return lax.ppermute(value, axes, pairs)


def dot(a, b):
    return jnp.dot(a, b, preferred_element_type=F32)


def updated_probe(probe, total):
    mean = jnp.sum(total * total, keepdims=True) / total.size
    return probe - total * (0.3 / jnp.sqrt(mean + 1e-06))


def pattern_group(group, count, slots_ref, pattern, pattern_copy, left, right, probe, ext, gobj, keep, send):
    size = pattern.shape[1]
    region = size // 2
    tiles = size // 8
    slots = [group * GROUP + i for i in range(GROUP)]
    sub_id = lax.broadcasted_iota(jnp.int32, (1, 8, LANES), 1)
    lane_id = lax.broadcasted_iota(jnp.int32, (1, 8, LANES), 2)

    def corner(slot):
        row = slots_ref[0, slot] + region
        col = slots_ref[1, slot] + region
        tile = jnp.minimum(row // 8, region // 8 - 1)
        return tile, row - tile * 8, col

    def window(part, at):
        tile, sub, col = at
        pieces = [ext[v, part, pl.ds(tile, tiles + 1)] for v in range(3)]
        halves = []
        for v in range(2):
            x = pltpu.roll(jnp.where(lane_id >= col, pieces[v], pieces[v + 1]), lax.rem(LANES - col, LANES), 2)
            x = pltpu.roll(jnp.where(sub_id >= sub, x[:tiles], x[1:]), lax.rem(8 - sub, 8), 1)
            halves.append(x.reshape(size, LANES))
        return jnp.concatenate(halves, axis=1)

    def add_object(part, value, at):
        tile, sub, col = at
        zero = jnp.zeros((1, 8, LANES), F32)
        rolled = []
        for v in range(2):
            x = value[:, v * LANES : (v + 1) * LANES].reshape(tiles, 8, LANES)
            x = pltpu.roll(x, lax.rem(sub, 8), 1)
            x = jnp.where(
                sub_id < sub, jnp.concatenate([zero, x], axis=0), jnp.concatenate([x, zero], axis=0)
            )
            rolled.append(pltpu.roll(x, lax.rem(col, LANES), 2))
        inside = lane_id < col
        gobj[0, part, pl.ds(tile, tiles + 1)] += jnp.where(inside, 0.0, rolled[0])
        gobj[1, part, pl.ds(tile, tiles + 1)] += jnp.where(inside, rolled[0], rolled[1])
        gobj[2, part, pl.ds(tile, tiles + 1)] += jnp.where(inside, rolled[1], 0.0)

    def add_probe(real, imag):
        first = lax.axis_index("core") == 0
        for v in range(2):
            lanes = slice(v * LANES, (v + 1) * LANES)
            keep[v] += jnp.where(first, real[:, lanes], imag[:, lanes])
            send[v] += jnp.where(first, imag[:, lanes], real[:, lanes])

    probe_real = jnp.concatenate([probe[0, 0], probe[0, 1]], axis=1)
    probe_imag = jnp.concatenate([probe[1, 0], probe[1, 1]], axis=1)
    lanes2 = range(2)

    def windows(pair):
        at = [corner(slot) for slot in pair]
        return at, [window(0, a) for a in at], [window(1, a) for a in at]

    def exits(state):
        at, reals, imags = state
        return [
            jnp.concatenate([probe_real * a - probe_imag * b, probe_real * b + probe_imag * a], axis=0).astype(jnp.bfloat16)
            for a, b in zip(reals, imags)
        ]

    def left_side(columns, table):
        mid = dot(table[...], jnp.concatenate(columns, axis=1)).astype(jnp.bfloat16)
        return jnp.concatenate(
            [
                jnp.concatenate([mid[:size, i * size : (i + 1) * size], mid[size:, i * size : (i + 1) * size]], axis=1)
                for i in lanes2
            ],
            axis=0,
        )

    def right_side(rows, table):
        out = dot(rows, table[...])
        return [(out[i * size : (i + 1) * size, :size], out[i * size : (i + 1) * size, size:]) for i in lanes2]

    def misfits(far, pair):
        out = []
        for (a, b), slot in zip(far, pair):
            m = jnp.where(slot < count, a * a + b * b - pattern[slot], 0.0)
            out.append(jnp.concatenate([m * a, m * b], axis=0).astype(jnp.bfloat16))
        return out

    def add(state, back):
        both = list(zip(state[1], state[2], back))
        add_probe(sum(a * c + b * d for a, b, (c, d) in both), sum(a * d - b * c for a, b, (c, d) in both))
        for a, (c, d) in zip(state[0], back):
            add_object(0, probe_real * c + probe_imag * d, a)
            add_object(1, probe_real * d - probe_imag * c, a)

    pairs = slots[:2], slots[2:]
    state_a = windows(pairs[0])
    mid_a = left_side(exits(state_a), left)
    state_b = windows(pairs[1])
    exit_b = exits(state_b)
    far_a = right_side(mid_a, right)
    mid_b = left_side(exit_b, left)
    pattern_copy(group).wait()
    misfit_a = misfits(far_a, pairs[0])
    far_b = right_side(mid_b, right)
    mid_a = left_side(misfit_a, right)
    misfit_b = misfits(far_b, pairs[1])
    back_a = right_side(mid_a, left)
    mid_b = left_side(misfit_b, right)
    add(state_a, back_a)
    back_b = right_side(mid_b, left)
    add(state_b, back_b)


def gradient_kernel(first, *refs):
    slots_ref, pattern_ref, left_ref, right_ref, start_ref, own_ref, side0_ref, side2_ref = refs[:8]
    if first:
        row0_ref, row1_ref, row2_ref, keep, send, peak_ref = refs[8:14]
    else:
        mine_ref, other_ref = refs[8:10]
        row0_ref, row1_ref, row2_ref, keep, send, peak_ref, probe_ref = refs[10:17]
    pattern, left, right, probe, ext, gobj, probe_sems, table_sems, pattern_sems = refs[-9:]
    row, row_places, row_end = place_of(ROW)
    count = slots_ref[2, 0]
    groups = pattern.shape[0] // GROUP

    def pattern_copy(group):
        slots = pl.ds(group * GROUP, GROUP)
        return pltpu.make_async_copy(pattern_ref.at[slots], pattern.at[slots], pattern_sems.at[group])

    probe_copies = [
        pltpu.make_async_copy(start_ref.at[:, :, pl.ds(v * LANES, LANES)], probe.at[:, v], probe_sems.at[v])
        for v in range(2)
    ]
    table_copies = [
        pltpu.make_async_copy(left_ref, left, table_sems.at[0]),
        pltpu.make_async_copy(right_ref, right, table_sems.at[1]),
    ]
    for copy in probe_copies + table_copies:
        copy.start()

    for i, ref in ((1, own_ref), (0, side0_ref), (2, side2_ref)):
        value = jnp.where(row_end, 0.0, ref[...]) if i == 2 else ref[...]
        ext[:, :, pl.ds(row_places[i] * TILES, TILES)] = value
    gobj[...] = jnp.zeros_like(gobj)
    keep[...] = jnp.zeros_like(keep)
    send[...] = jnp.zeros_like(send)
    for copy in probe_copies:
        copy.wait()
    if not first:
        real = lax.axis_index("core") == 0
        mine, other = mine_ref[...], other_ref[...]
        total = jnp.stack([jnp.where(real, mine, other), jnp.where(real, other, mine)])
        probe[...] = updated_probe(probe[...], total)
        probe_out = pltpu.make_async_copy(probe, probe_ref, probe_sems.at[2])
        probe_out.start()
    power = probe[0] * probe[0] + probe[1] * probe[1]
    peak_ref[...] = jnp.broadcast_to(jnp.max(power, keepdims=True).reshape(1, 1) + 1e-06, peak_ref.shape)
    for copy in table_copies:
        copy.wait()
    for group in range(groups):
        pattern_copy(group).start()

    def visit(group, carry):
        pattern_group(
            group, count, slots_ref, pattern, pattern_copy, left, right, probe, ext, gobj, keep, send
        )
        return carry

    live_groups = (count + GROUP - 1) // GROUP
    lax.fori_loop(0, live_groups, visit, 0)
    for i, ref in enumerate((row0_ref, row1_ref, row2_ref)):
        ref[...] = gobj[:, :, pl.ds(row_places[i] * TILES, TILES)]
    for group in range(1, groups):

        @pl.when(group >= live_groups)
        def _():
            pattern_copy(group).wait()

    if not first:
        probe_out.wait()


def gradients(first, live_slots, patterns, tables, probe, *vmem_args):
    slots, size = patterns.shape[:2]
    vmem = pl.BlockSpec(memory_space=pltpu.VMEM)
    smem = pl.BlockSpec(memory_space=pltpu.SMEM)
    hbm = pl.BlockSpec(memory_space=pltpu.HBM)
    strip = jax.ShapeDtypeStruct((3, 2, TILES, 8, LANES), F32)
    half = jax.ShapeDtypeStruct((2, size, LANES), F32)
    both = jax.ShapeDtypeStruct((2, 2, size, LANES), F32)
    ext = pltpu.VMEM((3, 2, 3 * TILES, 8, LANES), F32)
    return pl.pallas_call(
        functools.partial(gradient_kernel, first),
        out_shape=(strip,) * 3 + (half, half, jax.ShapeDtypeStruct((8, LANES), F32)) + (() if first else (both,)),
        in_specs=[smem] + [hbm] * 4 + [vmem] * len(vmem_args),
        out_specs=(vmem,) * 6 + (() if first else (hbm,)),
        scratch_shapes=[
            pltpu.VMEM(patterns.shape, F32),
            pltpu.VMEM(tables[0].shape, jnp.bfloat16),
            pltpu.VMEM(tables[1].shape, jnp.bfloat16),
            pltpu.VMEM(both.shape, F32),
            ext,
            ext,
            pltpu.SemaphoreType.DMA((3,)),
            pltpu.SemaphoreType.DMA((2,)),
            pltpu.SemaphoreType.DMA((slots // GROUP,)),
        ],
        compiler_params=pltpu.CompilerParams(vmem_limit_bytes=VMEM_BYTES),
    )(live_slots, patterns, *tables, probe, *vmem_args)


def exchange(value, axes):
    return lax.all_to_all(value, axes, 0, 0, tiled=True)


def core_swap(value):
    return lax.ppermute(value, "core", [(0, 1), (1, 0)])


def plane_shares(half):
    return exchange(half.reshape(lax.axis_size(PLANE), -1, LANES), PLANE)


def depth_shares(shares):
    share = shares.sum(0)
    return exchange(jnp.broadcast_to(share, (lax.axis_size("z"),) + share.shape), "z")


def gathered(shares, shape):
    plane = lax.axis_size(PLANE)
    share = shares.sum(0)
    return exchange(jnp.broadcast_to(share, (plane,) + share.shape), PLANE).reshape(shape)


def side_sum(own, side0, side2, at_end):
    return own + side0 + jnp.where(at_end, 0.0, side2)


def column_payloads(sums):
    index = lax.axis_index(COL)
    odd = lax.rem(index, 2) == 1
    right_first = lax.rem(index // 2, 2) == 0
    return (
        jnp.where(odd, sums[:2], sums[1:]),
        jnp.where(odd, sums[1:], sums[:2]),
        jnp.where(right_first, sums[2], sums[0]),
        jnp.where(right_first, sums[0], sums[2]),
    )


def column_transfers(payloads):
    near0, near2, far_a, far_b = payloads
    return paired(near0, COL, 0), paired(near2, COL, 2), paired_far(far_a, COL, 0), paired_far(far_b, COL, 1)


def updated_strip(strip, sums, arrived, peak):
    index, places, at_end = place_of(COL)
    last = lax.axis_size(COL) - 1
    odd = lax.rem(index, 2) == 1
    right_first = lax.rem(index // 2, 2) == 0
    near0, near2, far_a, far_b = arrived
    near2 = jnp.where(at_end, 0.0, near2)
    far_b = jnp.where((index < 2) | (index > last - 2), 0.0, far_b)
    from_left, from_right = jnp.where(odd, near0, near2), jnp.where(odd, near2, near0)
    grad_left = sums[0] + from_left[0] + jnp.where(right_first, far_b, far_a)
    grad = sums[1] + from_left[1] + from_right[0]
    grad_right = sums[2] + from_right[1] + jnp.where(right_first, far_a, far_b)
    return jnp.stack(
        [
            jnp.where(index == 0, 0.0, strip[0] - grad_left / peak),
            strip[1] - grad / peak,
            jnp.where(index == last, 0.0, strip[2] - grad_right / peak),
        ]
    )


def after(value, *others):
    return lax.optimization_barrier((value, others))[0]


def last_probe_kernel(probe_ref, mine_ref, other_ref, out_ref):
    first = lax.axis_index("core") == 0
    mine, other = mine_ref[...], other_ref[...]
    total = jnp.stack([jnp.where(first, mine, other), jnp.where(first, other, mine)])
    new = updated_probe(probe_ref[...], total)
    for part in range(2):
        for v in range(2):
            out_ref[part, :, v * LANES : (v + 1) * LANES] = new[part, v]


def last_probe(probe, mine, other):
    vmem = pl.BlockSpec(memory_space=pltpu.VMEM)
    size = probe.shape[2]
    return pl.pallas_call(
        last_probe_kernel,
        out_shape=jax.ShapeDtypeStruct((2, size, 2 * LANES), F32),
        in_specs=[vmem] * 3,
        out_specs=vmem,
        compiler_params=pltpu.CompilerParams(vmem_limit_bytes=8 * 1024 * 1024),
    )(probe, mine, other)


def body(object_field, probe_field, intensity, scan_offsets, pattern_counts):
    size = probe_field.shape[1]
    slots = intensity.shape[2]
    patterns = intensity.reshape(slots, size, size)
    live_slots = jnp.concatenate(
        [scan_offsets.reshape(slots, 2).T, jnp.broadcast_to(pattern_counts, (1, slots))], axis=0
    )
    tables = dft_tables(size)
    row_end, col_end = place_of(ROW)[2], place_of(COL)[2]
    odd = lax.rem(lax.axis_index(COL), 2) == 1

    own = object_field.reshape(2, TILES, 8, LANES)
    side0, side2 = paired(own, COL, 0), jnp.where(col_end, 0.0, paired(own, COL, 2))
    strip = jnp.stack([jnp.where(odd, side0, side2), own, jnp.where(odd, side2, side0)])
    strips = (strip, paired(strip, ROW, 0), paired(strip, ROW, 2))
    row0, row1, row2, keep, send, peak = gradients(True, live_slots, patterns, tables, probe_field, *strips)
    half = keep + core_swap(send)
    row0, row2 = after((row0, row2), half)
    sums = side_sum(row1, paired(row0, ROW, 0), paired(row2, ROW, 2), row_end)
    payloads = column_payloads(sums)
    shares = after(plane_shares(half), *payloads)
    arrived = column_transfers(payloads)
    shares, arrived = lax.optimization_barrier((depth_shares(shares), arrived))
    strip = updated_strip(strip, sums, arrived, peak)
    shares = after(shares, strip)
    sides = (paired(strip, ROW, 0), paired(strip, ROW, 2))
    mine, sides = lax.optimization_barrier((gathered(shares, keep.shape), sides))
    totals = (mine, core_swap(mine))

    strips = (strip,) + sides
    row0, row1, row2, keep, send, peak, probe = gradients(
        False, live_slots, patterns, tables, probe_field, *strips, *totals
    )
    sums = side_sum(row1, paired(row0, ROW, 0), paired(row2, ROW, 2), row_end)
    payloads = (jnp.where(odd, sums[0], sums[2]), jnp.where(odd, sums[2], sums[0]))
    shares = after(plane_shares(keep + core_swap(send)), *payloads)
    grad = side_sum(sums[1], paired(payloads[0], COL, 0), paired(payloads[1], COL, 2), col_end)
    new_object = (strip[1] - grad / peak).reshape(object_field.shape)
    mine = gathered(after(depth_shares(shares), new_object), keep.shape)
    return (new_object, last_probe(probe, mine, core_swap(mine)))


def solution(mesh):
    split = Mesh(mesh.devices.reshape(4, 2, 8, 4), ("y", "core", "z", "x"))
    in_specs = (
        P(None, ROW, COL),
        P(),
        P(ROW, COL, None, None, None),
        P(ROW, COL, None, None),
        P(ROW, COL),
    )
    out_specs = (P(None, ROW, COL), P())
    return jax.shard_map(body, mesh=split, in_specs=in_specs, out_specs=out_specs, check_vma=False)
```

```python
import functools

import jax
import jax.numpy as jnp
import numpy as np
from jax import lax
from jax.experimental import pallas as pl
from jax.experimental.pallas import tpu as pltpu
from jax.sharding import Mesh, PartitionSpec as P

ROW = ("y", "core")
COL = ("z", "x")
PLANE = ("y", "x")
LANES = 128
TILES = 16
GROUP = 4
F32 = jnp.float32
VMEM_BYTES = 102 * 512 * 1024


def dft_tables(length):
    index = np.arange(length, dtype=np.int64)
    angle = 2.0 * np.pi / length * (index[:, None] * index[None, :] % length)
    factor = 1.0 / np.sqrt(length)
    cos_table = (np.cos(angle) * factor).astype(np.float32)
    sin_table = (np.sin(angle) * factor).astype(np.float32)
    forward = np.block([[cos_table, sin_table], [-sin_table, cos_table]])
    inverse = np.block([[cos_table, -sin_table], [sin_table, cos_table]])
    return jnp.asarray(forward, jnp.bfloat16), jnp.asarray(inverse, jnp.bfloat16)


def place_of(axes):
    index = lax.axis_index(axes)
    odd = lax.rem(index, 2)
    at_end = (index == 0) | (index == lax.axis_size(axes) - 1)
    return index, (2 - 2 * odd, 1, 2 * odd), at_end


def paired(value, axes, side):
    count = lax.axis_size(axes)
    pairs = [(i, (i + (1 if (i + side // 2) % 2 == 0 else -1)) % count) for i in range(count)]
    return lax.ppermute(value, axes, pairs)


def dot(a, b):
    return jnp.dot(a, b, preferred_element_type=F32)


def updated_probe(probe, total):
    mean = jnp.sum(total * total, keepdims=True) / total.size
    return probe - total * (0.3 / jnp.sqrt(mean + 1e-06))


def pattern_group(group, count, slots_ref, pattern, pattern_copy, left, right, probe, ext, gobj, keep, send):
    size = pattern.shape[1]
    region = size // 2
    tiles = size // 8
    slots = [group * GROUP + i for i in range(GROUP)]
    sub_id = lax.broadcasted_iota(jnp.int32, (1, 8, LANES), 1)
    lane_id = lax.broadcasted_iota(jnp.int32, (1, 8, LANES), 2)

    def corner(slot):
        row = slots_ref[0, slot] + region
        col = slots_ref[1, slot] + region
        tile = jnp.minimum(row // 8, region // 8 - 1)
        return tile, row - tile * 8, col

    def window(part, at):
        tile, sub, col = at
        pieces = [ext[v, part, pl.ds(tile, tiles + 1)] for v in range(3)]
        halves = []
        for v in range(2):
            x = pltpu.roll(jnp.where(lane_id >= col, pieces[v], pieces[v + 1]), lax.rem(LANES - col, LANES), 2)
            x = pltpu.roll(jnp.where(sub_id >= sub, x[:tiles], x[1:]), lax.rem(8 - sub, 8), 1)
            halves.append(x.reshape(size, LANES))
        return jnp.concatenate(halves, axis=1)

    def add_object(part, value, at):
        tile, sub, col = at
        zero = jnp.zeros((1, 8, LANES), F32)
        rolled = []
        for v in range(2):
            x = value[:, v * LANES : (v + 1) * LANES].reshape(tiles, 8, LANES)
            x = pltpu.roll(x, lax.rem(sub, 8), 1)
            x = jnp.where(
                sub_id < sub, jnp.concatenate([zero, x], axis=0), jnp.concatenate([x, zero], axis=0)
            )
            rolled.append(pltpu.roll(x, lax.rem(col, LANES), 2))
        inside = lane_id < col
        gobj[0, part, pl.ds(tile, tiles + 1)] += jnp.where(inside, 0.0, rolled[0])
        gobj[1, part, pl.ds(tile, tiles + 1)] += jnp.where(inside, rolled[0], rolled[1])
        gobj[2, part, pl.ds(tile, tiles + 1)] += jnp.where(inside, rolled[1], 0.0)

    def add_probe(real, imag):
        first = lax.axis_index("core") == 0
        for v in range(2):
            lanes = slice(v * LANES, (v + 1) * LANES)
            keep[v] += jnp.where(first, real[:, lanes], imag[:, lanes])
            send[v] += jnp.where(first, imag[:, lanes], real[:, lanes])

    probe_real = jnp.concatenate([probe[0, 0], probe[0, 1]], axis=1)
    probe_imag = jnp.concatenate([probe[1, 0], probe[1, 1]], axis=1)
    lanes2 = range(2)

    def windows(pair):
        at = [corner(slot) for slot in pair]
        return at, [window(0, a) for a in at], [window(1, a) for a in at]

    def exits(state):
        at, reals, imags = state
        return [
            jnp.concatenate([probe_real * a - probe_imag * b, probe_real * b + probe_imag * a], axis=0).astype(jnp.bfloat16)
            for a, b in zip(reals, imags)
        ]

    def left_side(columns, table):
        mid = dot(table[...], jnp.concatenate(columns, axis=1)).astype(jnp.bfloat16)
        return jnp.concatenate(
            [
                jnp.concatenate([mid[:size, i * size : (i + 1) * size], mid[size:, i * size : (i + 1) * size]], axis=1)
                for i in lanes2
            ],
            axis=0,
        )

    def right_side(rows, table):
        out = dot(rows, table[...])
        return [(out[i * size : (i + 1) * size, :size], out[i * size : (i + 1) * size, size:]) for i in lanes2]

    def misfits(far, pair):
        out = []
        for (a, b), slot in zip(far, pair):
            m = jnp.where(slot < count, a * a + b * b - pattern[slot], 0.0)
            out.append(jnp.concatenate([m * a, m * b], axis=0).astype(jnp.bfloat16))
        return out

    def add(state, back):
        both = list(zip(state[1], state[2], back))
        add_probe(sum(a * c + b * d for a, b, (c, d) in both), sum(a * d - b * c for a, b, (c, d) in both))
        for a, (c, d) in zip(state[0], back):
            add_object(0, probe_real * c + probe_imag * d, a)
            add_object(1, probe_real * d - probe_imag * c, a)

    pairs = slots[:2], slots[2:]
    state_a = windows(pairs[0])
    mid_a = left_side(exits(state_a), left)
    state_b = windows(pairs[1])
    exit_b = exits(state_b)
    far_a = right_side(mid_a, right)
    mid_b = left_side(exit_b, left)
    pattern_copy(group).wait()
    misfit_a = misfits(far_a, pairs[0])
    far_b = right_side(mid_b, right)
    mid_a = left_side(misfit_a, right)
    misfit_b = misfits(far_b, pairs[1])
    back_a = right_side(mid_a, left)
    mid_b = left_side(misfit_b, right)
    add(state_a, back_a)
    back_b = right_side(mid_b, left)
    add(state_b, back_b)


def gradient_kernel(first, *refs):
    slots_ref, pattern_ref, left_ref, right_ref, start_ref, own_ref, side0_ref, side2_ref = refs[:8]
    if first:
        row0_ref, row1_ref, row2_ref, keep, send, peak_ref = refs[8:14]
    else:
        mine_ref, other_ref = refs[8:10]
        row0_ref, row1_ref, row2_ref, keep, send, peak_ref, probe_ref = refs[10:17]
    pattern, left, right, probe, ext, gobj, probe_sems, table_sems, pattern_sems = refs[-9:]
    row, row_places, row_end = place_of(ROW)
    count = slots_ref[2, 0]
    groups = pattern.shape[0] // GROUP

    def pattern_copy(group):
        slots = pl.ds(group * GROUP, GROUP)
        return pltpu.make_async_copy(pattern_ref.at[slots], pattern.at[slots], pattern_sems.at[group])

    probe_copies = [
        pltpu.make_async_copy(start_ref.at[:, :, pl.ds(v * LANES, LANES)], probe.at[:, v], probe_sems.at[v])
        for v in range(2)
    ]
    table_copies = [
        pltpu.make_async_copy(left_ref, left, table_sems.at[0]),
        pltpu.make_async_copy(right_ref, right, table_sems.at[1]),
    ]
    for copy in probe_copies + table_copies:
        copy.start()

    for i, ref in ((1, own_ref), (0, side0_ref), (2, side2_ref)):
        value = jnp.where(row_end, 0.0, ref[...]) if i == 2 else ref[...]
        ext[:, :, pl.ds(row_places[i] * TILES, TILES)] = value
    gobj[...] = jnp.zeros_like(gobj)
    keep[...] = jnp.zeros_like(keep)
    send[...] = jnp.zeros_like(send)
    for copy in probe_copies:
        copy.wait()
    if not first:
        real = lax.axis_index("core") == 0
        mine, other = mine_ref[...], other_ref[...]
        total = jnp.stack([jnp.where(real, mine, other), jnp.where(real, other, mine)])
        probe[...] = updated_probe(probe[...], total)
        probe_out = pltpu.make_async_copy(probe, probe_ref, probe_sems.at[2])
        probe_out.start()
    power = probe[0] * probe[0] + probe[1] * probe[1]
    peak_ref[...] = jnp.broadcast_to(jnp.max(power, keepdims=True).reshape(1, 1) + 1e-06, peak_ref.shape)
    for copy in table_copies:
        copy.wait()
    for group in range(groups):
        pattern_copy(group).start()

    def visit(group, carry):
        pattern_group(
            group, count, slots_ref, pattern, pattern_copy, left, right, probe, ext, gobj, keep, send
        )
        return carry

    live_groups = (count + GROUP - 1) // GROUP
    lax.fori_loop(0, live_groups, visit, 0)
    for i, ref in enumerate((row0_ref, row1_ref, row2_ref)):
        ref[...] = gobj[:, :, pl.ds(row_places[i] * TILES, TILES)]
    for group in range(1, groups):

        @pl.when(group >= live_groups)
        def _():
            pattern_copy(group).wait()

    if not first:
        probe_out.wait()


def gradients(first, live_slots, patterns, tables, probe, *vmem_args):
    slots, size = patterns.shape[:2]
    vmem = pl.BlockSpec(memory_space=pltpu.VMEM)
    smem = pl.BlockSpec(memory_space=pltpu.SMEM)
    hbm = pl.BlockSpec(memory_space=pltpu.HBM)
    strip = jax.ShapeDtypeStruct((3, 2, TILES, 8, LANES), F32)
    half = jax.ShapeDtypeStruct((2, size, LANES), F32)
    both = jax.ShapeDtypeStruct((2, 2, size, LANES), F32)
    ext = pltpu.VMEM((3, 2, 3 * TILES, 8, LANES), F32)
    return pl.pallas_call(
        functools.partial(gradient_kernel, first),
        out_shape=(strip,) * 3 + (half, half, jax.ShapeDtypeStruct((8, LANES), F32)) + (() if first else (both,)),
        in_specs=[smem] + [hbm] * 4 + [vmem] * len(vmem_args),
        out_specs=(vmem,) * 6 + (() if first else (hbm,)),
        scratch_shapes=[
            pltpu.VMEM(patterns.shape, F32),
            pltpu.VMEM(tables[0].shape, jnp.bfloat16),
            pltpu.VMEM(tables[1].shape, jnp.bfloat16),
            pltpu.VMEM(both.shape, F32),
            ext,
            ext,
            pltpu.SemaphoreType.DMA((3,)),
            pltpu.SemaphoreType.DMA((2,)),
            pltpu.SemaphoreType.DMA((slots // GROUP,)),
        ],
        compiler_params=pltpu.CompilerParams(vmem_limit_bytes=VMEM_BYTES),
    )(live_slots, patterns, *tables, probe, *vmem_args)


def exchange(value, axes):
    return lax.all_to_all(value, axes, 0, 0, tiled=True)


def core_swap(value):
    return lax.ppermute(value, "core", [(0, 1), (1, 0)])


def plane_shares(half):
    return exchange(half.reshape(lax.axis_size(PLANE), -1, LANES), PLANE)


def depth_shares(shares):
    share = shares.sum(0)
    return exchange(jnp.broadcast_to(share, (lax.axis_size("z"),) + share.shape), "z")


def gathered(shares, shape):
    plane = lax.axis_size(PLANE)
    share = shares.sum(0)
    return exchange(jnp.broadcast_to(share, (plane,) + share.shape), PLANE).reshape(shape)


def side_sum(own, side0, side2, at_end):
    return own + side0 + jnp.where(at_end, 0.0, side2)


def to_sides(blocks):
    odd = lax.rem(lax.axis_index(COL), 2) == 1
    return jnp.where(odd, blocks[0], blocks[2]), jnp.where(odd, blocks[2], blocks[0])


def strip_around(own):
    odd = lax.rem(lax.axis_index(COL), 2) == 1
    side0 = paired(own, COL, 0)
    side2 = jnp.where(place_of(COL)[2], 0.0, paired(own, COL, 2))
    return jnp.stack([jnp.where(odd, side0, side2), own, jnp.where(odd, side2, side0)])


def after(value, *others):
    return lax.optimization_barrier((value, others))[0]


def last_probe_kernel(probe_ref, mine_ref, other_ref, out_ref):
    first = lax.axis_index("core") == 0
    mine, other = mine_ref[...], other_ref[...]
    total = jnp.stack([jnp.where(first, mine, other), jnp.where(first, other, mine)])
    new = updated_probe(probe_ref[...], total)
    for part in range(2):
        for v in range(2):
            out_ref[part, :, v * LANES : (v + 1) * LANES] = new[part, v]


def last_probe(probe, mine, other):
    vmem = pl.BlockSpec(memory_space=pltpu.VMEM)
    size = probe.shape[2]
    return pl.pallas_call(
        last_probe_kernel,
        out_shape=jax.ShapeDtypeStruct((2, size, 2 * LANES), F32),
        in_specs=[vmem] * 3,
        out_specs=vmem,
        compiler_params=pltpu.CompilerParams(vmem_limit_bytes=8 * 1024 * 1024),
    )(probe, mine, other)


def body(object_field, probe_field, intensity, scan_offsets, pattern_counts):
    size = probe_field.shape[1]
    slots = intensity.shape[2]
    patterns = intensity.reshape(slots, size, size)
    live_slots = jnp.concatenate(
        [scan_offsets.reshape(slots, 2).T, jnp.broadcast_to(pattern_counts, (1, slots))], axis=0
    )
    tables = dft_tables(size)
    row_end, col_end = place_of(ROW)[2], place_of(COL)[2]

    own = object_field.reshape(2, TILES, 8, LANES)
    strip = strip_around(own)
    strips = (strip, paired(strip, ROW, 0), paired(strip, ROW, 2))
    row0, row1, row2, keep, send, peak = gradients(True, live_slots, patterns, tables, probe_field, *strips)
    half = keep + core_swap(send)
    row0, row2 = after((row0, row2), half)
    sums = side_sum(row1, paired(row0, ROW, 0), paired(row2, ROW, 2), row_end)
    payloads = to_sides(sums)
    shares = after(plane_shares(half), *payloads)
    grad = side_sum(sums[1], paired(payloads[0], COL, 0), paired(payloads[1], COL, 2), col_end)
    own = own - grad / peak
    shares = after(depth_shares(shares), own)
    strip = strip_around(own)
    strips = (strip, paired(strip, ROW, 0), paired(strip, ROW, 2))
    mine = gathered(shares, keep.shape)
    totals = (mine, core_swap(mine))

    row0, row1, row2, keep, send, peak, probe = gradients(
        False, live_slots, patterns, tables, probe_field, *strips, *totals
    )
    sums = side_sum(row1, paired(row0, ROW, 0), paired(row2, ROW, 2), row_end)
    payloads = to_sides(sums)
    shares = after(plane_shares(keep + core_swap(send)), *payloads)
    grad = side_sum(sums[1], paired(payloads[0], COL, 0), paired(payloads[1], COL, 2), col_end)
    new_object = (own - grad / peak).reshape(object_field.shape)
    mine = gathered(after(depth_shares(shares), new_object), keep.shape)
    return (new_object, last_probe(probe, mine, core_swap(mine)))


def solution(mesh):
    split = Mesh(mesh.devices.reshape(4, 2, 8, 4), ("y", "core", "z", "x"))
    in_specs = (
        P(None, ROW, COL),
        P(),
        P(ROW, COL, None, None, None),
        P(ROW, COL, None, None),
        P(ROW, COL),
    )
    out_specs = (P(None, ROW, COL), P())
    return jax.shard_map(body, mesh=split, in_specs=in_specs, out_specs=out_specs, check_vma=False)
```

```python
import functools

import jax
import jax.numpy as jnp
import numpy as np
from jax import lax
from jax.experimental import pallas as pl
from jax.experimental.pallas import tpu as pltpu
from jax.sharding import Mesh, PartitionSpec as P

ROW = ("y", "core")
COL = ("z", "x")
PLANE = ("y", "x")
LANES = 128
TILES = 16
GROUP = 4
F32 = jnp.float32
VMEM_BYTES = 102 * 512 * 1024


def dft_tables(length):
    index = np.arange(length, dtype=np.int64)
    angle = 2.0 * np.pi / length * (index[:, None] * index[None, :] % length)
    factor = 1.0 / np.sqrt(length)
    cos_table = (np.cos(angle) * factor).astype(np.float32)
    sin_table = (np.sin(angle) * factor).astype(np.float32)
    forward = np.block([[cos_table, sin_table], [-sin_table, cos_table]])
    inverse = np.block([[cos_table, -sin_table], [sin_table, cos_table]])
    return jnp.asarray(forward, jnp.bfloat16), jnp.asarray(inverse, jnp.bfloat16)


def place_of(axes):
    index = lax.axis_index(axes)
    odd = lax.rem(index, 2)
    at_end = (index == 0) | (index == lax.axis_size(axes) - 1)
    return index, (2 - 2 * odd, 1, 2 * odd), at_end


def paired(value, axes, side):
    count = lax.axis_size(axes)
    pairs = [(i, (i + (1 if (i + side // 2) % 2 == 0 else -1)) % count) for i in range(count)]
    return lax.ppermute(value, axes, pairs)


def dot(a, b):
    return jnp.dot(a, b, preferred_element_type=F32)


def updated_probe(probe, total):
    mean = jnp.sum(total * total, keepdims=True) / total.size
    return probe - total * (0.3 / jnp.sqrt(mean + 1e-06))


def pattern_group(group, count, slots_ref, pattern, pattern_copy, left, right, probe, ext, gobj, keep, send):
    size = pattern.shape[1]
    region = size // 2
    tiles = size // 8
    slots = [group * GROUP + i for i in range(GROUP)]
    sub_id = lax.broadcasted_iota(jnp.int32, (1, 8, LANES), 1)
    lane_id = lax.broadcasted_iota(jnp.int32, (1, 8, LANES), 2)

    def corner(slot):
        row = slots_ref[0, slot] + region
        col = slots_ref[1, slot] + region
        tile = jnp.minimum(row // 8, region // 8 - 1)
        return tile, row - tile * 8, col

    def window(part, at):
        tile, sub, col = at
        pieces = [ext[v, part, pl.ds(tile, tiles + 1)] for v in range(3)]
        halves = []
        for v in range(2):
            x = pltpu.roll(jnp.where(lane_id >= col, pieces[v], pieces[v + 1]), lax.rem(LANES - col, LANES), 2)
            x = pltpu.roll(jnp.where(sub_id >= sub, x[:tiles], x[1:]), lax.rem(8 - sub, 8), 1)
            halves.append(x.reshape(size, LANES))
        return jnp.concatenate(halves, axis=1)

    def add_object(part, value, at):
        tile, sub, col = at
        zero = jnp.zeros((1, 8, LANES), F32)
        rolled = []
        for v in range(2):
            x = value[:, v * LANES : (v + 1) * LANES].reshape(tiles, 8, LANES)
            x = pltpu.roll(x, lax.rem(sub, 8), 1)
            x = jnp.where(
                sub_id < sub, jnp.concatenate([zero, x], axis=0), jnp.concatenate([x, zero], axis=0)
            )
            rolled.append(pltpu.roll(x, lax.rem(col, LANES), 2))
        inside = lane_id < col
        gobj[0, part, pl.ds(tile, tiles + 1)] += jnp.where(inside, 0.0, rolled[0])
        gobj[1, part, pl.ds(tile, tiles + 1)] += jnp.where(inside, rolled[0], rolled[1])
        gobj[2, part, pl.ds(tile, tiles + 1)] += jnp.where(inside, rolled[1], 0.0)

    def add_probe(real, imag):
        first = lax.axis_index("core") == 0
        for v in range(2):
            lanes = slice(v * LANES, (v + 1) * LANES)
            keep[v] += jnp.where(first, real[:, lanes], imag[:, lanes])
            send[v] += jnp.where(first, imag[:, lanes], real[:, lanes])

    probe_real = jnp.concatenate([probe[0, 0], probe[0, 1]], axis=1)
    probe_imag = jnp.concatenate([probe[1, 0], probe[1, 1]], axis=1)
    lanes2 = range(2)

    def windows(pair):
        at = [corner(slot) for slot in pair]
        return at, [window(0, a) for a in at], [window(1, a) for a in at]

    def exits(state):
        at, reals, imags = state
        return [
            jnp.concatenate([probe_real * a - probe_imag * b, probe_real * b + probe_imag * a], axis=0).astype(jnp.bfloat16)
            for a, b in zip(reals, imags)
        ]

    def left_side(columns, table):
        mid = dot(table[...], jnp.concatenate(columns, axis=1)).astype(jnp.bfloat16)
        return jnp.concatenate(
            [
                jnp.concatenate([mid[:size, i * size : (i + 1) * size], mid[size:, i * size : (i + 1) * size]], axis=1)
                for i in lanes2
            ],
            axis=0,
        )

    def right_side(rows, table):
        out = dot(rows, table[...])
        return [(out[i * size : (i + 1) * size, :size], out[i * size : (i + 1) * size, size:]) for i in lanes2]

    def misfits(far, pair):
        out = []
        for (a, b), slot in zip(far, pair):
            m = jnp.where(slot < count, a * a + b * b - pattern[slot], 0.0)
            out.append(jnp.concatenate([m * a, m * b], axis=0).astype(jnp.bfloat16))
        return out

    def add(state, back):
        both = list(zip(state[1], state[2], back))
        add_probe(sum(a * c + b * d for a, b, (c, d) in both), sum(a * d - b * c for a, b, (c, d) in both))
        for a, (c, d) in zip(state[0], back):
            add_object(0, probe_real * c + probe_imag * d, a)
            add_object(1, probe_real * d - probe_imag * c, a)

    pairs = slots[:2], slots[2:]
    state_a = windows(pairs[0])
    mid_a = left_side(exits(state_a), left)
    state_b = windows(pairs[1])
    exit_b = exits(state_b)
    far_a = right_side(mid_a, right)
    mid_b = left_side(exit_b, left)
    pattern_copy(group).wait()
    misfit_a = misfits(far_a, pairs[0])
    far_b = right_side(mid_b, right)
    mid_a = left_side(misfit_a, right)
    misfit_b = misfits(far_b, pairs[1])
    back_a = right_side(mid_a, left)
    mid_b = left_side(misfit_b, right)
    add(state_a, back_a)
    back_b = right_side(mid_b, left)
    add(state_b, back_b)


def gradient_kernel(first, *refs):
    slots_ref, pattern_ref, left_ref, right_ref, start_ref, own_ref, side0_ref, side2_ref = refs[:8]
    if first:
        row0_ref, row1_ref, row2_ref, keep, send, peak_ref = refs[8:14]
    else:
        mine_ref, other_ref = refs[8:10]
        row0_ref, row1_ref, row2_ref, keep, send, peak_ref, probe_ref = refs[10:17]
    pattern, left, right, probe, ext, gobj, probe_sems, table_sems, pattern_sems = refs[-9:]
    row, row_places, row_end = place_of(ROW)
    count = slots_ref[2, 0]
    groups = pattern.shape[0] // GROUP

    def pattern_copy(group):
        slots = pl.ds(group * GROUP, GROUP)
        return pltpu.make_async_copy(pattern_ref.at[slots], pattern.at[slots], pattern_sems.at[group])

    probe_copies = [
        pltpu.make_async_copy(start_ref.at[:, :, pl.ds(v * LANES, LANES)], probe.at[:, v], probe_sems.at[v])
        for v in range(2)
    ]
    table_copies = [
        pltpu.make_async_copy(left_ref, left, table_sems.at[0]),
        pltpu.make_async_copy(right_ref, right, table_sems.at[1]),
    ]
    for copy in probe_copies + table_copies:
        copy.start()

    for i, ref in ((1, own_ref), (0, side0_ref), (2, side2_ref)):
        value = jnp.where(row_end, 0.0, ref[...]) if i == 2 else ref[...]
        ext[:, :, pl.ds(row_places[i] * TILES, TILES)] = value
    gobj[...] = jnp.zeros_like(gobj)
    keep[...] = jnp.zeros_like(keep)
    send[...] = jnp.zeros_like(send)
    for copy in probe_copies:
        copy.wait()
    if not first:
        real = lax.axis_index("core") == 0
        mine, other = mine_ref[...], other_ref[...]
        total = jnp.stack([jnp.where(real, mine, other), jnp.where(real, other, mine)])
        probe[...] = updated_probe(probe[...], total)
        probe_out = pltpu.make_async_copy(probe, probe_ref, probe_sems.at[2])
        probe_out.start()
    power = probe[0] * probe[0] + probe[1] * probe[1]
    peak_ref[...] = jnp.broadcast_to(jnp.max(power, keepdims=True).reshape(1, 1) + 1e-06, peak_ref.shape)
    for copy in table_copies:
        copy.wait()
    for group in range(groups):
        pattern_copy(group).start()

    def visit(group, carry):
        pattern_group(
            group, count, slots_ref, pattern, pattern_copy, left, right, probe, ext, gobj, keep, send
        )
        return carry

    live_groups = (count + GROUP - 1) // GROUP
    lax.fori_loop(0, live_groups, visit, 0)
    for i, ref in enumerate((row0_ref, row1_ref, row2_ref)):
        ref[...] = gobj[:, :, pl.ds(row_places[i] * TILES, TILES)]
    for group in range(1, groups):

        @pl.when(group >= live_groups)
        def _():
            pattern_copy(group).wait()

    if not first:
        probe_out.wait()


def gradients(first, live_slots, patterns, tables, probe, *vmem_args):
    slots, size = patterns.shape[:2]
    vmem = pl.BlockSpec(memory_space=pltpu.VMEM)
    smem = pl.BlockSpec(memory_space=pltpu.SMEM)
    hbm = pl.BlockSpec(memory_space=pltpu.HBM)
    strip = jax.ShapeDtypeStruct((3, 2, TILES, 8, LANES), F32)
    half = jax.ShapeDtypeStruct((2, size, LANES), F32)
    both = jax.ShapeDtypeStruct((2, 2, size, LANES), F32)
    ext = pltpu.VMEM((3, 2, 3 * TILES, 8, LANES), F32)
    return pl.pallas_call(
        functools.partial(gradient_kernel, first),
        out_shape=(strip,) * 3 + (half, half, jax.ShapeDtypeStruct((8, LANES), F32)) + (() if first else (both,)),
        in_specs=[smem] + [hbm] * 4 + [vmem] * len(vmem_args),
        out_specs=(vmem,) * 6 + (() if first else (hbm,)),
        scratch_shapes=[
            pltpu.VMEM(patterns.shape, F32),
            pltpu.VMEM(tables[0].shape, jnp.bfloat16),
            pltpu.VMEM(tables[1].shape, jnp.bfloat16),
            pltpu.VMEM(both.shape, F32),
            ext,
            ext,
            pltpu.SemaphoreType.DMA((3,)),
            pltpu.SemaphoreType.DMA((2,)),
            pltpu.SemaphoreType.DMA((slots // GROUP,)),
        ],
        compiler_params=pltpu.CompilerParams(vmem_limit_bytes=VMEM_BYTES),
    )(live_slots, patterns, *tables, probe, *vmem_args)


def exchange(value, axes):
    return lax.all_to_all(value, axes, 0, 0, tiled=True)


def core_swap(value):
    return lax.ppermute(value, "core", [(0, 1), (1, 0)])


def plane_shares(half):
    return exchange(half.reshape(lax.axis_size(PLANE), -1, LANES), PLANE)


def depth_shares(shares):
    share = shares.sum(0)
    return exchange(jnp.broadcast_to(share, (lax.axis_size("z"),) + share.shape), "z")


def gathered(shares, shape):
    plane = lax.axis_size(PLANE)
    share = shares.sum(0)
    return exchange(jnp.broadcast_to(share, (plane,) + share.shape), PLANE).reshape(shape)


def side_sum(own, side0, side2, at_end):
    return own + side0 + jnp.where(at_end, 0.0, side2)


def to_sides(blocks):
    odd = lax.rem(lax.axis_index(COL), 2) == 1
    return jnp.where(odd, blocks[0], blocks[2]), jnp.where(odd, blocks[2], blocks[0])


def strip_around(own):
    odd = lax.rem(lax.axis_index(COL), 2) == 1
    side0 = paired(own, COL, 0)
    side2 = jnp.where(place_of(COL)[2], 0.0, paired(own, COL, 2))
    return jnp.stack([jnp.where(odd, side0, side2), own, jnp.where(odd, side2, side0)])


def after(value, *others):
    return lax.optimization_barrier((value, others))[0]


def last_probe_kernel(probe_ref, mine_ref, other_ref, out_ref):
    first = lax.axis_index("core") == 0
    mine, other = mine_ref[...], other_ref[...]
    total = jnp.stack([jnp.where(first, mine, other), jnp.where(first, other, mine)])
    new = updated_probe(probe_ref[...], total)
    for part in range(2):
        for v in range(2):
            out_ref[part, :, v * LANES : (v + 1) * LANES] = new[part, v]


def last_probe(probe, mine, other):
    vmem = pl.BlockSpec(memory_space=pltpu.VMEM)
    size = probe.shape[2]
    return pl.pallas_call(
        last_probe_kernel,
        out_shape=jax.ShapeDtypeStruct((2, size, 2 * LANES), F32),
        in_specs=[vmem] * 3,
        out_specs=vmem,
        compiler_params=pltpu.CompilerParams(vmem_limit_bytes=8 * 1024 * 1024),
    )(probe, mine, other)


def body(object_field, probe_field, intensity, scan_offsets, pattern_counts):
    size = probe_field.shape[1]
    slots = intensity.shape[2]
    patterns = intensity.reshape(slots, size, size)
    live_slots = jnp.concatenate(
        [scan_offsets.reshape(slots, 2).T, jnp.broadcast_to(pattern_counts, (1, slots))], axis=0
    )
    tables = dft_tables(size)
    row_end, col_end = place_of(ROW)[2], place_of(COL)[2]

    own = object_field.reshape(2, TILES, 8, LANES)
    strip = strip_around(own)
    strips = (strip, paired(strip, ROW, 0), paired(strip, ROW, 2))
    row0, row1, row2, keep, send, peak = gradients(True, live_slots, patterns, tables, probe_field, *strips)
    half = keep + core_swap(send)
    row0, row2 = after((row0, row2), half)
    sums = side_sum(row1, paired(row0, ROW, 0), paired(row2, ROW, 2), row_end)
    payloads = to_sides(sums)
    shares = after(plane_shares(half), *payloads)
    grad = side_sum(sums[1], paired(payloads[0], COL, 0), paired(payloads[1], COL, 2), col_end)
    own = own - grad / peak
    shares = after(depth_shares(shares), own)
    strip = strip_around(own)
    strips = (strip, paired(strip, ROW, 0), paired(strip, ROW, 2))
    mine = gathered(shares, keep.shape)
    totals = (mine, core_swap(mine))

    row0, row1, row2, keep, send, peak, probe = gradients(
        False, live_slots, patterns, tables, probe_field, *strips, *totals
    )
    shares = plane_shares(keep + core_swap(send))
    shares, (row0, row2) = lax.optimization_barrier((shares, (row0, row2)))
    sums = side_sum(row1, paired(row0, ROW, 0), paired(row2, ROW, 2), row_end)
    payloads = to_sides(sums)
    shares = after(depth_shares(shares), *payloads)
    grad = side_sum(sums[1], paired(payloads[0], COL, 0), paired(payloads[1], COL, 2), col_end)
    new_object = (own - grad / peak).reshape(object_field.shape)
    mine = gathered(shares, keep.shape)
    return (new_object, last_probe(probe, mine, core_swap(mine)))


def solution(mesh):
    split = Mesh(mesh.devices.reshape(4, 2, 8, 4), ("y", "core", "z", "x"))
    in_specs = (
        P(None, ROW, COL),
        P(),
        P(ROW, COL, None, None, None),
        P(ROW, COL, None, None),
        P(ROW, COL),
    )
    out_specs = (P(None, ROW, COL), P())
    return jax.shard_map(body, mesh=split, in_specs=in_specs, out_specs=out_specs, check_vma=False)
```

```python
import functools

import jax
import jax.numpy as jnp
import numpy as np
from jax import lax
from jax.experimental import pallas as pl
from jax.experimental.pallas import tpu as pltpu
from jax.sharding import Mesh, PartitionSpec as P

ROW = ("y", "core")
COL = ("z", "x")
PLANE = ("y", "x")
LANES = 128
TILES = 16
GROUP = 4
F32 = jnp.float32
VMEM_BYTES = 102 * 512 * 1024


def dft_tables(length):
    index = np.arange(length, dtype=np.int64)
    angle = 2.0 * np.pi / length * (index[:, None] * index[None, :] % length)
    factor = 1.0 / np.sqrt(length)
    cos_table = (np.cos(angle) * factor).astype(np.float32)
    sin_table = (np.sin(angle) * factor).astype(np.float32)
    forward = np.block([[cos_table, sin_table], [-sin_table, cos_table]])
    inverse = np.block([[cos_table, -sin_table], [sin_table, cos_table]])
    return jnp.asarray(forward, jnp.bfloat16), jnp.asarray(inverse, jnp.bfloat16)


def place_of(axes):
    index = lax.axis_index(axes)
    odd = lax.rem(index, 2)
    at_end = (index == 0) | (index == lax.axis_size(axes) - 1)
    return index, (2 - 2 * odd, 1, 2 * odd), at_end


def paired(value, axes, side):
    count = lax.axis_size(axes)
    pairs = [(i, (i + (1 if (i + side // 2) % 2 == 0 else -1)) % count) for i in range(count)]
    return lax.ppermute(value, axes, pairs)


def dot(a, b):
    return jnp.dot(a, b, preferred_element_type=F32)


def updated_probe(probe, total):
    mean = jnp.sum(total * total, keepdims=True) / total.size
    return probe - total * (0.3 / jnp.sqrt(mean + 1e-06))


def pattern_group(group, count, slots_ref, pattern, pattern_copy, left, right, probe, ext, gobj, keep, send):
    size = pattern.shape[1]
    region = size // 2
    tiles = size // 8
    slots = [group * GROUP + i for i in range(GROUP)]
    sub_id = lax.broadcasted_iota(jnp.int32, (1, 8, LANES), 1)
    lane_id = lax.broadcasted_iota(jnp.int32, (1, 8, LANES), 2)

    def corner(slot):
        row = slots_ref[0, slot] + region
        col = slots_ref[1, slot] + region
        tile = jnp.minimum(row // 8, region // 8 - 1)
        return tile, row - tile * 8, col

    def window(part, at):
        tile, sub, col = at
        pieces = [ext[v, part, pl.ds(tile, tiles + 1)] for v in range(3)]
        halves = []
        for v in range(2):
            x = pltpu.roll(jnp.where(lane_id >= col, pieces[v], pieces[v + 1]), lax.rem(LANES - col, LANES), 2)
            x = pltpu.roll(jnp.where(sub_id >= sub, x[:tiles], x[1:]), lax.rem(8 - sub, 8), 1)
            halves.append(x.reshape(size, LANES))
        return jnp.concatenate(halves, axis=1)

    def add_object(part, value, at):
        tile, sub, col = at
        zero = jnp.zeros((1, 8, LANES), F32)
        rolled = []
        for v in range(2):
            x = value[:, v * LANES : (v + 1) * LANES].reshape(tiles, 8, LANES)
            x = pltpu.roll(x, lax.rem(sub, 8), 1)
            x = jnp.where(
                sub_id < sub, jnp.concatenate([zero, x], axis=0), jnp.concatenate([x, zero], axis=0)
            )
            rolled.append(pltpu.roll(x, lax.rem(col, LANES), 2))
        inside = lane_id < col
        gobj[0, part, pl.ds(tile, tiles + 1)] += jnp.where(inside, 0.0, rolled[0])
        gobj[1, part, pl.ds(tile, tiles + 1)] += jnp.where(inside, rolled[0], rolled[1])
        gobj[2, part, pl.ds(tile, tiles + 1)] += jnp.where(inside, rolled[1], 0.0)

    def add_probe(real, imag):
        first = lax.axis_index("core") == 0
        for v in range(2):
            lanes = slice(v * LANES, (v + 1) * LANES)
            keep[v] += jnp.where(first, real[:, lanes], imag[:, lanes])
            send[v] += jnp.where(first, imag[:, lanes], real[:, lanes])

    probe_real = jnp.concatenate([probe[0, 0], probe[0, 1]], axis=1)
    probe_imag = jnp.concatenate([probe[1, 0], probe[1, 1]], axis=1)
    lanes2 = range(2)

    def windows(pair):
        at = [corner(slot) for slot in pair]
        return at, [window(0, a) for a in at], [window(1, a) for a in at]

    def exits(state):
        at, reals, imags = state
        return [
            jnp.concatenate([probe_real * a - probe_imag * b, probe_real * b + probe_imag * a], axis=0).astype(jnp.bfloat16)
            for a, b in zip(reals, imags)
        ]

    def left_side(columns, table):
        mid = dot(table[...], jnp.concatenate(columns, axis=1)).astype(jnp.bfloat16)
        return jnp.concatenate(
            [
                jnp.concatenate([mid[:size, i * size : (i + 1) * size], mid[size:, i * size : (i + 1) * size]], axis=1)
                for i in lanes2
            ],
            axis=0,
        )

    def right_side(rows, table):
        out = dot(rows, table[...])
        return [(out[i * size : (i + 1) * size, :size], out[i * size : (i + 1) * size, size:]) for i in lanes2]

    def misfits(far, pair):
        out = []
        for (a, b), slot in zip(far, pair):
            m = jnp.where(slot < count, a * a + b * b - pattern[slot], 0.0)
            out.append(jnp.concatenate([m * a, m * b], axis=0).astype(jnp.bfloat16))
        return out

    def add(state, back):
        both = list(zip(state[1], state[2], back))
        add_probe(sum(a * c + b * d for a, b, (c, d) in both), sum(a * d - b * c for a, b, (c, d) in both))
        for a, (c, d) in zip(state[0], back):
            add_object(0, probe_real * c + probe_imag * d, a)
            add_object(1, probe_real * d - probe_imag * c, a)

    pairs = slots[:2], slots[2:]
    state_a = windows(pairs[0])
    mid_a = left_side(exits(state_a), left)
    state_b = windows(pairs[1])
    exit_b = exits(state_b)
    far_a = right_side(mid_a, right)
    mid_b = left_side(exit_b, left)
    pattern_copy(group).wait()
    misfit_a = misfits(far_a, pairs[0])
    far_b = right_side(mid_b, right)
    mid_a = left_side(misfit_a, right)
    misfit_b = misfits(far_b, pairs[1])
    back_a = right_side(mid_a, left)
    mid_b = left_side(misfit_b, right)
    add(state_a, back_a)
    back_b = right_side(mid_b, left)
    add(state_b, back_b)


def gradient_kernel(first, *refs):
    slots_ref, pattern_ref, left_ref, right_ref, start_ref, own_ref, side0_ref, side2_ref = refs[:8]
    if first:
        row0_ref, row1_ref, row2_ref, keep, send, peak_ref = refs[8:14]
    else:
        mine_ref, other_ref = refs[8:10]
        row0_ref, row1_ref, row2_ref, keep, send, peak_ref, probe_ref = refs[10:17]
    pattern, left, right, probe, ext, gobj, probe_sems, table_sems, pattern_sems = refs[-9:]
    row, row_places, row_end = place_of(ROW)
    count = slots_ref[2, 0]
    groups = pattern.shape[0] // GROUP

    def pattern_copy(group):
        slots = pl.ds(group * GROUP, GROUP)
        return pltpu.make_async_copy(pattern_ref.at[slots], pattern.at[slots], pattern_sems.at[group])

    probe_copies = [
        pltpu.make_async_copy(start_ref.at[:, :, pl.ds(v * LANES, LANES)], probe.at[:, v], probe_sems.at[v])
        for v in range(2)
    ]
    table_copies = [
        pltpu.make_async_copy(left_ref, left, table_sems.at[0]),
        pltpu.make_async_copy(right_ref, right, table_sems.at[1]),
    ]
    for copy in probe_copies + table_copies:
        copy.start()

    for i, ref in ((1, own_ref), (0, side0_ref), (2, side2_ref)):
        value = jnp.where(row_end, 0.0, ref[...]) if i == 2 else ref[...]
        ext[:, :, pl.ds(row_places[i] * TILES, TILES)] = value
    gobj[...] = jnp.zeros_like(gobj)
    keep[...] = jnp.zeros_like(keep)
    send[...] = jnp.zeros_like(send)
    for copy in probe_copies:
        copy.wait()
    if not first:
        real = lax.axis_index("core") == 0
        mine, other = mine_ref[...], other_ref[...]
        total = jnp.stack([jnp.where(real, mine, other), jnp.where(real, other, mine)])
        probe[...] = updated_probe(probe[...], total)
        probe_out = pltpu.make_async_copy(probe, probe_ref, probe_sems.at[2])
        probe_out.start()
    power = probe[0] * probe[0] + probe[1] * probe[1]
    peak_ref[...] = jnp.broadcast_to(jnp.max(power, keepdims=True).reshape(1, 1) + 1e-06, peak_ref.shape)
    for copy in table_copies:
        copy.wait()
    for group in range(groups):
        pattern_copy(group).start()

    def visit(group, carry):
        pattern_group(
            group, count, slots_ref, pattern, pattern_copy, left, right, probe, ext, gobj, keep, send
        )
        return carry

    live_groups = (count + GROUP - 1) // GROUP
    lax.fori_loop(0, live_groups, visit, 0)
    for i, ref in enumerate((row0_ref, row1_ref, row2_ref)):
        ref[...] = gobj[:, :, pl.ds(row_places[i] * TILES, TILES)]
    for group in range(1, groups):

        @pl.when(group >= live_groups)
        def _():
            pattern_copy(group).wait()

    if not first:
        probe_out.wait()


def gradients(first, live_slots, patterns, tables, probe, *vmem_args):
    slots, size = patterns.shape[:2]
    vmem = pl.BlockSpec(memory_space=pltpu.VMEM)
    smem = pl.BlockSpec(memory_space=pltpu.SMEM)
    hbm = pl.BlockSpec(memory_space=pltpu.HBM)
    strip = jax.ShapeDtypeStruct((3, 2, TILES, 8, LANES), F32)
    half = jax.ShapeDtypeStruct((2, size, LANES), F32)
    both = jax.ShapeDtypeStruct((2, 2, size, LANES), F32)
    ext = pltpu.VMEM((3, 2, 3 * TILES, 8, LANES), F32)
    return pl.pallas_call(
        functools.partial(gradient_kernel, first),
        out_shape=(strip,) * 3 + (half, half, jax.ShapeDtypeStruct((8, LANES), F32)) + (() if first else (both,)),
        in_specs=[smem] + [hbm] * 4 + [vmem] * len(vmem_args),
        out_specs=(vmem,) * 6 + (() if first else (hbm,)),
        scratch_shapes=[
            pltpu.VMEM(patterns.shape, F32),
            pltpu.VMEM(tables[0].shape, jnp.bfloat16),
            pltpu.VMEM(tables[1].shape, jnp.bfloat16),
            pltpu.VMEM(both.shape, F32),
            ext,
            ext,
            pltpu.SemaphoreType.DMA((3,)),
            pltpu.SemaphoreType.DMA((2,)),
            pltpu.SemaphoreType.DMA((slots // GROUP,)),
        ],
        compiler_params=pltpu.CompilerParams(vmem_limit_bytes=VMEM_BYTES),
    )(live_slots, patterns, *tables, probe, *vmem_args)


def exchange(value, axes):
    return lax.all_to_all(value, axes, 0, 0, tiled=True)


def core_swap(value):
    return lax.ppermute(value, "core", [(0, 1), (1, 0)])


def plane_shares(half):
    return exchange(half.reshape(lax.axis_size(PLANE), -1, LANES), PLANE)


def depth_shares(shares):
    share = shares.sum(0)
    return exchange(jnp.broadcast_to(share, (lax.axis_size("z"),) + share.shape), "z")


def gathered(shares, shape):
    plane = lax.axis_size(PLANE)
    share = shares.sum(0)
    return exchange(jnp.broadcast_to(share, (plane,) + share.shape), PLANE).reshape(shape)


def side_sum(own, side0, side2, at_end):
    return own + side0 + jnp.where(at_end, 0.0, side2)


def to_sides(blocks):
    odd = lax.rem(lax.axis_index(COL), 2) == 1
    return jnp.where(odd, blocks[0], blocks[2]), jnp.where(odd, blocks[2], blocks[0])


def strip_around(own):
    odd = lax.rem(lax.axis_index(COL), 2) == 1
    side0 = paired(own, COL, 0)
    side2 = jnp.where(place_of(COL)[2], 0.0, paired(own, COL, 2))
    return jnp.stack([jnp.where(odd, side0, side2), own, jnp.where(odd, side2, side0)])


def after(value, *others):
    return lax.optimization_barrier((value, others))[0]


def last_probe_kernel(probe_ref, mine_ref, other_ref, out_ref):
    first = lax.axis_index("core") == 0
    mine, other = mine_ref[...], other_ref[...]
    total = jnp.stack([jnp.where(first, mine, other), jnp.where(first, other, mine)])
    new = updated_probe(probe_ref[...], total)
    for part in range(2):
        for v in range(2):
            out_ref[part, :, v * LANES : (v + 1) * LANES] = new[part, v]


def last_probe(probe, mine, other):
    vmem = pl.BlockSpec(memory_space=pltpu.VMEM)
    size = probe.shape[2]
    return pl.pallas_call(
        last_probe_kernel,
        out_shape=jax.ShapeDtypeStruct((2, size, 2 * LANES), F32),
        in_specs=[vmem] * 3,
        out_specs=vmem,
        compiler_params=pltpu.CompilerParams(vmem_limit_bytes=8 * 1024 * 1024),
    )(probe, mine, other)


def body(object_field, probe_field, intensity, scan_offsets, pattern_counts):
    size = probe_field.shape[1]
    slots = intensity.shape[2]
    patterns = intensity.reshape(slots, size, size)
    live_slots = jnp.concatenate(
        [scan_offsets.reshape(slots, 2).T, jnp.broadcast_to(pattern_counts, (1, slots))], axis=0
    )
    tables = dft_tables(size)
    row_end, col_end = place_of(ROW)[2], place_of(COL)[2]

    own = object_field.reshape(2, TILES, 8, LANES)
    strip = strip_around(own)
    strips = (strip, paired(strip, ROW, 0), paired(strip, ROW, 2))
    row0, row1, row2, keep, send, peak = gradients(True, live_slots, patterns, tables, probe_field, *strips)
    half = keep + core_swap(send)
    row2 = after(row2, half)
    sums = side_sum(row1, paired(row0, ROW, 0), paired(row2, ROW, 2), row_end)
    payloads = to_sides(sums)
    shares = after(plane_shares(half), *payloads)
    grad = side_sum(sums[1], paired(payloads[0], COL, 0), paired(payloads[1], COL, 2), col_end)
    own = own - grad / peak
    shares = after(depth_shares(shares), own)
    strip = strip_around(own)
    strips = (strip, paired(strip, ROW, 0), paired(strip, ROW, 2))
    mine = gathered(shares, keep.shape)
    totals = (mine, core_swap(mine))

    row0, row1, row2, keep, send, peak, probe = gradients(
        False, live_slots, patterns, tables, probe_field, *strips, *totals
    )
    shares = plane_shares(keep + core_swap(send))
    shares, (row0, row2) = lax.optimization_barrier((shares, (row0, row2)))
    sums = side_sum(row1, paired(row0, ROW, 0), paired(row2, ROW, 2), row_end)
    payloads = to_sides(sums)
    shares = after(depth_shares(shares), *payloads)
    grad = side_sum(sums[1], paired(payloads[0], COL, 0), paired(payloads[1], COL, 2), col_end)
    new_object = (own - grad / peak).reshape(object_field.shape)
    mine = gathered(shares, keep.shape)
    return (new_object, last_probe(probe, mine, core_swap(mine)))


def solution(mesh):
    split = Mesh(mesh.devices.reshape(4, 2, 8, 4), ("y", "core", "z", "x"))
    in_specs = (
        P(None, ROW, COL),
        P(),
        P(ROW, COL, None, None, None),
        P(ROW, COL, None, None),
        P(ROW, COL),
    )
    out_specs = (P(None, ROW, COL), P())
    return jax.shard_map(body, mesh=split, in_specs=in_specs, out_specs=out_specs, check_vma=False)
```

```python
import functools

import jax
import jax.numpy as jnp
import numpy as np
from jax import lax
from jax.experimental import pallas as pl
from jax.experimental.pallas import tpu as pltpu
from jax.sharding import Mesh, PartitionSpec as P

ROW = ("y", "core")
COL = ("z", "x")
PLANE = ("y", "x")
LANES = 128
TILES = 16
GROUP = 4
F32 = jnp.float32
VMEM_BYTES = 102 * 512 * 1024


def dft_tables(length):
    index = np.arange(length, dtype=np.int64)
    angle = 2.0 * np.pi / length * (index[:, None] * index[None, :] % length)
    factor = 1.0 / np.sqrt(length)
    cos_table = (np.cos(angle) * factor).astype(np.float32)
    sin_table = (np.sin(angle) * factor).astype(np.float32)
    forward = np.block([[cos_table, sin_table], [-sin_table, cos_table]])
    inverse = np.block([[cos_table, -sin_table], [sin_table, cos_table]])
    return jnp.asarray(forward, jnp.bfloat16), jnp.asarray(inverse, jnp.bfloat16)


def place_of(axes):
    index = lax.axis_index(axes)
    odd = lax.rem(index, 2)
    at_end = (index == 0) | (index == lax.axis_size(axes) - 1)
    return index, (2 - 2 * odd, 1, 2 * odd), at_end


def paired(value, axes, side):
    count = lax.axis_size(axes)
    pairs = [(i, (i + (1 if (i + side // 2) % 2 == 0 else -1)) % count) for i in range(count)]
    return lax.ppermute(value, axes, pairs)


def dot(a, b):
    return jnp.dot(a, b, preferred_element_type=F32)


def updated_probe(probe, total):
    mean = jnp.sum(total * total, keepdims=True) / total.size
    return probe - total * (0.3 / jnp.sqrt(mean + 1e-06))


def pattern_group(group, count, slots_ref, pattern, pattern_copy, left, right, probe, ext, gobj, keep, send):
    size = pattern.shape[1]
    region = size // 2
    tiles = size // 8
    slots = [group * GROUP + i for i in range(GROUP)]
    sub_id = lax.broadcasted_iota(jnp.int32, (1, 8, LANES), 1)
    lane_id = lax.broadcasted_iota(jnp.int32, (1, 8, LANES), 2)

    def corner(slot):
        row = slots_ref[0, slot] + region
        col = slots_ref[1, slot] + region
        tile = jnp.minimum(row // 8, region // 8 - 1)
        return tile, row - tile * 8, col

    def window(part, at):
        tile, sub, col = at
        pieces = [ext[v, part, pl.ds(tile, tiles + 1)] for v in range(3)]
        halves = []
        for v in range(2):
            x = pltpu.roll(jnp.where(lane_id >= col, pieces[v], pieces[v + 1]), lax.rem(LANES - col, LANES), 2)
            x = pltpu.roll(jnp.where(sub_id >= sub, x[:tiles], x[1:]), lax.rem(8 - sub, 8), 1)
            halves.append(x.reshape(size, LANES))
        return jnp.concatenate(halves, axis=1)

    def add_object(part, value, at):
        tile, sub, col = at
        zero = jnp.zeros((1, 8, LANES), F32)
        rolled = []
        for v in range(2):
            x = value[:, v * LANES : (v + 1) * LANES].reshape(tiles, 8, LANES)
            x = pltpu.roll(x, lax.rem(sub, 8), 1)
            x = jnp.where(
                sub_id < sub, jnp.concatenate([zero, x], axis=0), jnp.concatenate([x, zero], axis=0)
            )
            rolled.append(pltpu.roll(x, lax.rem(col, LANES), 2))
        inside = lane_id < col
        gobj[0, part, pl.ds(tile, tiles + 1)] += jnp.where(inside, 0.0, rolled[0])
        gobj[1, part, pl.ds(tile, tiles + 1)] += jnp.where(inside, rolled[0], rolled[1])
        gobj[2, part, pl.ds(tile, tiles + 1)] += jnp.where(inside, rolled[1], 0.0)

    def add_probe(real, imag):
        first = lax.axis_index("core") == 0
        for v in range(2):
            lanes = slice(v * LANES, (v + 1) * LANES)
            keep[v] += jnp.where(first, real[:, lanes], imag[:, lanes])
            send[v] += jnp.where(first, imag[:, lanes], real[:, lanes])

    probe_real = jnp.concatenate([probe[0, 0], probe[0, 1]], axis=1)
    probe_imag = jnp.concatenate([probe[1, 0], probe[1, 1]], axis=1)
    lanes2 = range(2)

    def windows(pair):
        at = [corner(slot) for slot in pair]
        return at, [window(0, a) for a in at], [window(1, a) for a in at]

    def exits(state):
        at, reals, imags = state
        return [
            jnp.concatenate([probe_real * a - probe_imag * b, probe_real * b + probe_imag * a], axis=0).astype(jnp.bfloat16)
            for a, b in zip(reals, imags)
        ]

    def left_side(columns, table):
        mid = dot(table[...], jnp.concatenate(columns, axis=1)).astype(jnp.bfloat16)
        return jnp.concatenate(
            [
                jnp.concatenate([mid[:size, i * size : (i + 1) * size], mid[size:, i * size : (i + 1) * size]], axis=1)
                for i in lanes2
            ],
            axis=0,
        )

    def right_side(rows, table):
        out = dot(rows, table[...])
        return [(out[i * size : (i + 1) * size, :size], out[i * size : (i + 1) * size, size:]) for i in lanes2]

    def misfits(far, pair):
        out = []
        for (a, b), slot in zip(far, pair):
            m = jnp.where(slot < count, a * a + b * b - pattern[slot], 0.0)
            out.append(jnp.concatenate([m * a, m * b], axis=0).astype(jnp.bfloat16))
        return out

    def add(state, back):
        both = list(zip(state[1], state[2], back))
        add_probe(sum(a * c + b * d for a, b, (c, d) in both), sum(a * d - b * c for a, b, (c, d) in both))
        for a, (c, d) in zip(state[0], back):
            add_object(0, probe_real * c + probe_imag * d, a)
            add_object(1, probe_real * d - probe_imag * c, a)

    pairs = slots[:2], slots[2:]
    state_a = windows(pairs[0])
    mid_a = left_side(exits(state_a), left)
    state_b = windows(pairs[1])
    exit_b = exits(state_b)
    far_a = right_side(mid_a, right)
    pattern_copy(group).wait()
    mid_b = left_side(exit_b, left)
    misfit_a = misfits(far_a, pairs[0])
    mid_a = left_side(misfit_a, right)
    far_b = right_side(mid_b, right)
    misfit_b = misfits(far_b, pairs[1])
    back_a = right_side(mid_a, left)
    mid_b = left_side(misfit_b, right)
    add(state_a, back_a)
    back_b = right_side(mid_b, left)
    add(state_b, back_b)


def gradient_kernel(first, *refs):
    slots_ref, pattern_ref, left_ref, right_ref, start_ref, own_ref, side0_ref, side2_ref = refs[:8]
    if first:
        row0_ref, row1_ref, row2_ref, keep, send, peak_ref = refs[8:14]
    else:
        mine_ref, other_ref = refs[8:10]
        row0_ref, row1_ref, row2_ref, keep, send, peak_ref, probe_ref = refs[10:17]
    pattern, left, right, probe, ext, gobj, probe_sems, table_sems, pattern_sems = refs[-9:]
    row, row_places, row_end = place_of(ROW)
    count = slots_ref[2, 0]
    groups = pattern.shape[0] // GROUP

    def pattern_copy(group):
        slots = pl.ds(group * GROUP, GROUP)
        return pltpu.make_async_copy(pattern_ref.at[slots], pattern.at[slots], pattern_sems.at[group])

    probe_copies = [
        pltpu.make_async_copy(start_ref.at[:, :, pl.ds(v * LANES, LANES)], probe.at[:, v], probe_sems.at[v])
        for v in range(2)
    ]
    table_copies = [
        pltpu.make_async_copy(left_ref, left, table_sems.at[0]),
        pltpu.make_async_copy(right_ref, right, table_sems.at[1]),
    ]
    for copy in probe_copies + table_copies:
        copy.start()

    for i, ref in ((1, own_ref), (0, side0_ref), (2, side2_ref)):
        value = jnp.where(row_end, 0.0, ref[...]) if i == 2 else ref[...]
        ext[:, :, pl.ds(row_places[i] * TILES, TILES)] = value
    gobj[...] = jnp.zeros_like(gobj)
    keep[...] = jnp.zeros_like(keep)
    send[...] = jnp.zeros_like(send)
    for copy in probe_copies:
        copy.wait()
    if not first:
        real = lax.axis_index("core") == 0
        mine, other = mine_ref[...], other_ref[...]
        total = jnp.stack([jnp.where(real, mine, other), jnp.where(real, other, mine)])
        probe[...] = updated_probe(probe[...], total)
        probe_out = pltpu.make_async_copy(probe, probe_ref, probe_sems.at[2])
        probe_out.start()
    power = probe[0] * probe[0] + probe[1] * probe[1]
    peak_ref[...] = jnp.broadcast_to(jnp.max(power, keepdims=True).reshape(1, 1) + 1e-06, peak_ref.shape)
    for copy in table_copies:
        copy.wait()
    for group in range(groups):
        pattern_copy(group).start()

    def visit(group, carry):
        pattern_group(
            group, count, slots_ref, pattern, pattern_copy, left, right, probe, ext, gobj, keep, send
        )
        return carry

    live_groups = (count + GROUP - 1) // GROUP
    lax.fori_loop(0, live_groups, visit, 0)
    for i, ref in enumerate((row0_ref, row1_ref, row2_ref)):
        ref[...] = gobj[:, :, pl.ds(row_places[i] * TILES, TILES)]
    for group in range(1, groups):

        @pl.when(group >= live_groups)
        def _():
            pattern_copy(group).wait()

    if not first:
        probe_out.wait()


def gradients(first, live_slots, patterns, tables, probe, *vmem_args):
    slots, size = patterns.shape[:2]
    vmem = pl.BlockSpec(memory_space=pltpu.VMEM)
    smem = pl.BlockSpec(memory_space=pltpu.SMEM)
    hbm = pl.BlockSpec(memory_space=pltpu.HBM)
    strip = jax.ShapeDtypeStruct((3, 2, TILES, 8, LANES), F32)
    half = jax.ShapeDtypeStruct((2, size, LANES), F32)
    both = jax.ShapeDtypeStruct((2, 2, size, LANES), F32)
    ext = pltpu.VMEM((3, 2, 3 * TILES, 8, LANES), F32)
    return pl.pallas_call(
        functools.partial(gradient_kernel, first),
        out_shape=(strip,) * 3 + (half, half, jax.ShapeDtypeStruct((8, LANES), F32)) + (() if first else (both,)),
        in_specs=[smem] + [hbm] * 4 + [vmem] * len(vmem_args),
        out_specs=(vmem,) * 6 + (() if first else (hbm,)),
        scratch_shapes=[
            pltpu.VMEM(patterns.shape, F32),
            pltpu.VMEM(tables[0].shape, jnp.bfloat16),
            pltpu.VMEM(tables[1].shape, jnp.bfloat16),
            pltpu.VMEM(both.shape, F32),
            ext,
            ext,
            pltpu.SemaphoreType.DMA((3,)),
            pltpu.SemaphoreType.DMA((2,)),
            pltpu.SemaphoreType.DMA((slots // GROUP,)),
        ],
        compiler_params=pltpu.CompilerParams(vmem_limit_bytes=VMEM_BYTES),
    )(live_slots, patterns, *tables, probe, *vmem_args)


def exchange(value, axes):
    return lax.all_to_all(value, axes, 0, 0, tiled=True)


def core_swap(value):
    return lax.ppermute(value, "core", [(0, 1), (1, 0)])


def plane_shares(half):
    return exchange(half.reshape(lax.axis_size(PLANE), -1, LANES), PLANE)


def depth_shares(shares):
    share = shares.sum(0)
    return exchange(jnp.broadcast_to(share, (lax.axis_size("z"),) + share.shape), "z")


def gathered(shares, shape):
    plane = lax.axis_size(PLANE)
    share = shares.sum(0)
    return exchange(jnp.broadcast_to(share, (plane,) + share.shape), PLANE).reshape(shape)


def side_sum(own, side0, side2, at_end):
    return own + side0 + jnp.where(at_end, 0.0, side2)


def to_sides(blocks):
    odd = lax.rem(lax.axis_index(COL), 2) == 1
    return jnp.where(odd, blocks[0], blocks[2]), jnp.where(odd, blocks[2], blocks[0])


def strip_around(own):
    odd = lax.rem(lax.axis_index(COL), 2) == 1
    side0 = paired(own, COL, 0)
    side2 = jnp.where(place_of(COL)[2], 0.0, paired(own, COL, 2))
    return jnp.stack([jnp.where(odd, side0, side2), own, jnp.where(odd, side2, side0)])


def after(value, *others):
    return lax.optimization_barrier((value, others))[0]


def last_probe_kernel(probe_ref, mine_ref, other_ref, out_ref):
    first = lax.axis_index("core") == 0
    mine, other = mine_ref[...], other_ref[...]
    total = jnp.stack([jnp.where(first, mine, other), jnp.where(first, other, mine)])
    new = updated_probe(probe_ref[...], total)
    for part in range(2):
        for v in range(2):
            out_ref[part, :, v * LANES : (v + 1) * LANES] = new[part, v]


def last_probe(probe, mine, other):
    vmem = pl.BlockSpec(memory_space=pltpu.VMEM)
    size = probe.shape[2]
    return pl.pallas_call(
        last_probe_kernel,
        out_shape=jax.ShapeDtypeStruct((2, size, 2 * LANES), F32),
        in_specs=[vmem] * 3,
        out_specs=vmem,
        compiler_params=pltpu.CompilerParams(vmem_limit_bytes=8 * 1024 * 1024),
    )(probe, mine, other)


def body(object_field, probe_field, intensity, scan_offsets, pattern_counts):
    size = probe_field.shape[1]
    slots = intensity.shape[2]
    patterns = intensity.reshape(slots, size, size)
    live_slots = jnp.concatenate(
        [scan_offsets.reshape(slots, 2).T, jnp.broadcast_to(pattern_counts, (1, slots))], axis=0
    )
    tables = dft_tables(size)
    row_end, col_end = place_of(ROW)[2], place_of(COL)[2]

    own = object_field.reshape(2, TILES, 8, LANES)
    strip = strip_around(own)
    strips = (strip, paired(strip, ROW, 0), paired(strip, ROW, 2))
    row0, row1, row2, keep, send, peak = gradients(True, live_slots, patterns, tables, probe_field, *strips)
    half = keep + core_swap(send)
    row0, row2 = after((row0, row2), half)
    sums = side_sum(row1, paired(row0, ROW, 0), paired(row2, ROW, 2), row_end)
    payloads = to_sides(sums)
    shares = after(plane_shares(half), *payloads)
    grad = side_sum(sums[1], paired(payloads[0], COL, 0), paired(payloads[1], COL, 2), col_end)
    own = own - grad / peak
    shares = after(depth_shares(shares), own)
    strip = strip_around(own)
    strips = (strip, paired(strip, ROW, 0), paired(strip, ROW, 2))
    mine = gathered(shares, keep.shape)
    totals = (mine, core_swap(mine))

    row0, row1, row2, keep, send, peak, probe = gradients(
        False, live_slots, patterns, tables, probe_field, *strips, *totals
    )
    shares = plane_shares(keep + core_swap(send))
    shares, (row0, row2) = lax.optimization_barrier((shares, (row0, row2)))
    sums = side_sum(row1, paired(row0, ROW, 0), paired(row2, ROW, 2), row_end)
    payloads = to_sides(sums)
    shares = after(depth_shares(shares), *payloads)
    grad = side_sum(sums[1], paired(payloads[0], COL, 0), paired(payloads[1], COL, 2), col_end)
    new_object = (own - grad / peak).reshape(object_field.shape)
    mine = gathered(shares, keep.shape)
    return (new_object, last_probe(probe, mine, core_swap(mine)))


def solution(mesh):
    split = Mesh(mesh.devices.reshape(4, 2, 8, 4), ("y", "core", "z", "x"))
    in_specs = (
        P(None, ROW, COL),
        P(),
        P(ROW, COL, None, None, None),
        P(ROW, COL, None, None),
        P(ROW, COL),
    )
    out_specs = (P(None, ROW, COL), P())
    return jax.shard_map(body, mesh=split, in_specs=in_specs, out_specs=out_specs, check_vma=False)
```

```python
import functools

import jax
import jax.numpy as jnp
import numpy as np
from jax import lax
from jax.experimental import pallas as pl
from jax.experimental.pallas import tpu as pltpu
from jax.sharding import Mesh, PartitionSpec as P

ROW = ("y", "core")
COL = ("z", "x")
PLANE = ("y", "x")
LANES = 128
TILES = 16
GROUP = 4
F32 = jnp.float32
VMEM_BYTES = 102 * 512 * 1024


def dft_tables(length):
    index = np.arange(length, dtype=np.int64)
    angle = 2.0 * np.pi / length * (index[:, None] * index[None, :] % length)
    factor = 1.0 / np.sqrt(length)
    cos_table = (np.cos(angle) * factor).astype(np.float32)
    sin_table = (np.sin(angle) * factor).astype(np.float32)
    forward = np.block([[cos_table, sin_table], [-sin_table, cos_table]])
    inverse = np.block([[cos_table, -sin_table], [sin_table, cos_table]])
    return jnp.asarray(forward, jnp.bfloat16), jnp.asarray(inverse, jnp.bfloat16)


def place_of(axes):
    index = lax.axis_index(axes)
    odd = lax.rem(index, 2)
    at_end = (index == 0) | (index == lax.axis_size(axes) - 1)
    return index, (2 - 2 * odd, 1, 2 * odd), at_end


def paired(value, axes, side):
    count = lax.axis_size(axes)
    pairs = [(i, (i + (1 if (i + side // 2) % 2 == 0 else -1)) % count) for i in range(count)]
    return lax.ppermute(value, axes, pairs)


def dot(a, b):
    return jnp.dot(a, b, preferred_element_type=F32)


def updated_probe(probe, total):
    mean = jnp.sum(total * total, keepdims=True) / total.size
    return probe - total * (0.3 / jnp.sqrt(mean + 1e-06))


def pattern_group(group, count, slots_ref, pattern, pattern_copy, left, right, probe, ext, gobj, keep, send):
    size = pattern.shape[1]
    region = size // 2
    tiles = size // 8
    slots = [group * GROUP + i for i in range(GROUP)]
    sub_id = lax.broadcasted_iota(jnp.int32, (1, 8, LANES), 1)
    lane_id = lax.broadcasted_iota(jnp.int32, (1, 8, LANES), 2)

    def corner(slot):
        row = slots_ref[0, slot] + region
        col = slots_ref[1, slot] + region
        tile = jnp.minimum(row // 8, region // 8 - 1)
        return tile, row - tile * 8, col

    def window(part, at):
        tile, sub, col = at
        pieces = [ext[v, part, pl.ds(tile, tiles + 1)] for v in range(3)]
        halves = []
        for v in range(2):
            x = pltpu.roll(jnp.where(lane_id >= col, pieces[v], pieces[v + 1]), lax.rem(LANES - col, LANES), 2)
            x = pltpu.roll(jnp.where(sub_id >= sub, x[:tiles], x[1:]), lax.rem(8 - sub, 8), 1)
            halves.append(x.reshape(size, LANES))
        return jnp.concatenate(halves, axis=1)

    def add_object(part, value, at):
        tile, sub, col = at
        zero = jnp.zeros((1, 8, LANES), F32)
        rolled = []
        for v in range(2):
            x = value[:, v * LANES : (v + 1) * LANES].reshape(tiles, 8, LANES)
            x = pltpu.roll(x, lax.rem(sub, 8), 1)
            x = jnp.where(
                sub_id < sub, jnp.concatenate([zero, x], axis=0), jnp.concatenate([x, zero], axis=0)
            )
            rolled.append(pltpu.roll(x, lax.rem(col, LANES), 2))
        inside = lane_id < col
        gobj[0, part, pl.ds(tile, tiles + 1)] += jnp.where(inside, 0.0, rolled[0])
        gobj[1, part, pl.ds(tile, tiles + 1)] += jnp.where(inside, rolled[0], rolled[1])
        gobj[2, part, pl.ds(tile, tiles + 1)] += jnp.where(inside, rolled[1], 0.0)

    def add_probe(real, imag):
        first = lax.axis_index("core") == 0
        for v in range(2):
            lanes = slice(v * LANES, (v + 1) * LANES)
            keep[v] += jnp.where(first, real[:, lanes], imag[:, lanes])
            send[v] += jnp.where(first, imag[:, lanes], real[:, lanes])

    probe_real = jnp.concatenate([probe[0, 0], probe[0, 1]], axis=1)
    probe_imag = jnp.concatenate([probe[1, 0], probe[1, 1]], axis=1)
    lanes2 = range(2)

    def windows(pair):
        at = [corner(slot) for slot in pair]
        return at, [window(0, a) for a in at], [window(1, a) for a in at]

    def exits(state):
        at, reals, imags = state
        return [
            jnp.concatenate([probe_real * a - probe_imag * b, probe_real * b + probe_imag * a], axis=0).astype(jnp.bfloat16)
            for a, b in zip(reals, imags)
        ]

    def left_side(columns, table):
        mid = dot(table[...], jnp.concatenate(columns, axis=1)).astype(jnp.bfloat16)
        return jnp.concatenate(
            [
                jnp.concatenate([mid[:size, i * size : (i + 1) * size], mid[size:, i * size : (i + 1) * size]], axis=1)
                for i in lanes2
            ],
            axis=0,
        )

    def right_side(rows, table):
        out = dot(rows, table[...])
        return [(out[i * size : (i + 1) * size, :size], out[i * size : (i + 1) * size, size:]) for i in lanes2]

    def misfits(far, pair):
        out = []
        for (a, b), slot in zip(far, pair):
            m = jnp.where(slot < count, a * a + b * b - pattern[slot], 0.0)
            out.append(jnp.concatenate([m * a, m * b], axis=0).astype(jnp.bfloat16))
        return out

    def add(state, back):
        both = list(zip(state[1], state[2], back))
        add_probe(sum(a * c + b * d for a, b, (c, d) in both), sum(a * d - b * c for a, b, (c, d) in both))
        for a, (c, d) in zip(state[0], back):
            add_object(0, probe_real * c + probe_imag * d, a)
            add_object(1, probe_real * d - probe_imag * c, a)

    pairs = slots[:2], slots[2:]
    state_a = windows(pairs[0])
    mid_a = left_side(exits(state_a), left)
    state_b = windows(pairs[1])
    exit_b = exits(state_b)
    far_a = right_side(mid_a, right)
    mid_b = left_side(exit_b, left)
    pattern_copy(group).wait()
    misfit_a = misfits(far_a, pairs[0])
    far_b = right_side(mid_b, right)
    mid_a = left_side(misfit_a, right)
    misfit_b = misfits(far_b, pairs[1])
    back_a = right_side(mid_a, left)
    mid_b = left_side(misfit_b, right)
    add(state_a, back_a)
    back_b = right_side(mid_b, left)
    add(state_b, back_b)


def gradient_kernel(first, *refs):
    slots_ref, pattern_ref, left_ref, right_ref, start_ref, own_ref, side0_ref, side2_ref = refs[:8]
    if first:
        row0_ref, row1_ref, row2_ref, keep, send, peak_ref = refs[8:14]
    else:
        mine_ref, other_ref = refs[8:10]
        row0_ref, row1_ref, row2_ref, keep, send, peak_ref, probe_ref = refs[10:17]
    pattern, left, right, probe, ext, gobj, probe_sems, table_sems, pattern_sems = refs[-9:]
    row, row_places, row_end = place_of(ROW)
    count = slots_ref[2, 0]
    groups = pattern.shape[0] // GROUP

    def pattern_copy(group):
        slots = pl.ds(group * GROUP, GROUP)
        return pltpu.make_async_copy(pattern_ref.at[slots], pattern.at[slots], pattern_sems.at[group])

    probe_copies = [
        pltpu.make_async_copy(start_ref.at[:, :, pl.ds(v * LANES, LANES)], probe.at[:, v], probe_sems.at[v])
        for v in range(2)
    ]
    table_copies = [
        pltpu.make_async_copy(left_ref, left, table_sems.at[0]),
        pltpu.make_async_copy(right_ref, right, table_sems.at[1]),
    ]
    for copy in probe_copies + table_copies:
        copy.start()

    for i, ref in ((1, own_ref), (0, side0_ref), (2, side2_ref)):
        value = jnp.where(row_end, 0.0, ref[...]) if i == 2 else ref[...]
        ext[:, :, pl.ds(row_places[i] * TILES, TILES)] = value
    gobj[...] = jnp.zeros_like(gobj)
    keep[...] = jnp.zeros_like(keep)
    send[...] = jnp.zeros_like(send)
    for copy in probe_copies:
        copy.wait()
    if not first:
        real = lax.axis_index("core") == 0
        mine, other = mine_ref[...], other_ref[...]
        total = jnp.stack([jnp.where(real, mine, other), jnp.where(real, other, mine)])
        probe[...] = updated_probe(probe[...], total)
        probe_out = pltpu.make_async_copy(probe, probe_ref, probe_sems.at[2])
        probe_out.start()
    power = probe[0] * probe[0] + probe[1] * probe[1]
    peak_ref[...] = jnp.broadcast_to(jnp.max(power, keepdims=True).reshape(1, 1) + 1e-06, peak_ref.shape)
    for copy in table_copies:
        copy.wait()
    for group in range(groups):
        pattern_copy(group).start()

    def visit(group, carry):
        pattern_group(
            group, count, slots_ref, pattern, pattern_copy, left, right, probe, ext, gobj, keep, send
        )
        return carry

    live_groups = (count + GROUP - 1) // GROUP
    lax.fori_loop(0, live_groups, visit, 0)
    for i, ref in enumerate((row0_ref, row1_ref, row2_ref)):
        ref[...] = gobj[:, :, pl.ds(row_places[i] * TILES, TILES)]
    for group in range(1, groups):

        @pl.when(group >= live_groups)
        def _():
            pattern_copy(group).wait()

    if not first:
        probe_out.wait()


def gradients(first, live_slots, patterns, tables, probe, *vmem_args):
    slots, size = patterns.shape[:2]
    vmem = pl.BlockSpec(memory_space=pltpu.VMEM)
    smem = pl.BlockSpec(memory_space=pltpu.SMEM)
    hbm = pl.BlockSpec(memory_space=pltpu.HBM)
    strip = jax.ShapeDtypeStruct((3, 2, TILES, 8, LANES), F32)
    half = jax.ShapeDtypeStruct((2, size, LANES), F32)
    both = jax.ShapeDtypeStruct((2, 2, size, LANES), F32)
    ext = pltpu.VMEM((3, 2, 3 * TILES, 8, LANES), F32)
    return pl.pallas_call(
        functools.partial(gradient_kernel, first),
        out_shape=(strip,) * 3 + (half, half, jax.ShapeDtypeStruct((8, LANES), F32)) + (() if first else (both,)),
        in_specs=[smem] + [hbm] * 4 + [vmem] * len(vmem_args),
        out_specs=(vmem,) * 6 + (() if first else (hbm,)),
        scratch_shapes=[
            pltpu.VMEM(patterns.shape, F32),
            pltpu.VMEM(tables[0].shape, jnp.bfloat16),
            pltpu.VMEM(tables[1].shape, jnp.bfloat16),
            pltpu.VMEM(both.shape, F32),
            ext,
            ext,
            pltpu.SemaphoreType.DMA((3,)),
            pltpu.SemaphoreType.DMA((2,)),
            pltpu.SemaphoreType.DMA((slots // GROUP,)),
        ],
        compiler_params=pltpu.CompilerParams(vmem_limit_bytes=VMEM_BYTES),
    )(live_slots, patterns, *tables, probe, *vmem_args)


def exchange(value, axes):
    return lax.all_to_all(value, axes, 0, 0, tiled=True)


def core_swap(value):
    return lax.ppermute(value, "core", [(0, 1), (1, 0)])


def plane_shares(half):
    return exchange(half.reshape(lax.axis_size(PLANE), -1, LANES), PLANE)


def depth_shares(shares):
    share = shares.sum(0)
    return exchange(jnp.broadcast_to(share, (lax.axis_size("z"),) + share.shape), "z")


def gathered(shares, shape):
    plane = lax.axis_size(PLANE)
    share = shares.sum(0)
    return exchange(jnp.broadcast_to(share, (plane,) + share.shape), PLANE).reshape(shape)


def side_sum(own, side0, side2, at_end):
    return own + side0 + jnp.where(at_end, 0.0, side2)


def to_sides(blocks):
    odd = lax.rem(lax.axis_index(COL), 2) == 1
    return jnp.where(odd, blocks[0], blocks[2]), jnp.where(odd, blocks[2], blocks[0])


def strip_around(own):
    odd = lax.rem(lax.axis_index(COL), 2) == 1
    side0 = paired(own, COL, 0)
    side2 = jnp.where(place_of(COL)[2], 0.0, paired(own, COL, 2))
    return jnp.stack([jnp.where(odd, side0, side2), own, jnp.where(odd, side2, side0)])


def after(value, *others):
    return lax.optimization_barrier((value, others))[0]


def last_probe_kernel(probe_ref, mine_ref, other_ref, out_ref):
    first = lax.axis_index("core") == 0
    mine, other = mine_ref[...], other_ref[...]
    total = jnp.stack([jnp.where(first, mine, other), jnp.where(first, other, mine)])
    new = updated_probe(probe_ref[...], total)
    for part in range(2):
        for v in range(2):
            out_ref[part, :, v * LANES : (v + 1) * LANES] = new[part, v]


def last_probe(probe, mine, other):
    vmem = pl.BlockSpec(memory_space=pltpu.VMEM)
    size = probe.shape[2]
    return pl.pallas_call(
        last_probe_kernel,
        out_shape=jax.ShapeDtypeStruct((2, size, 2 * LANES), F32),
        in_specs=[vmem] * 3,
        out_specs=vmem,
        compiler_params=pltpu.CompilerParams(vmem_limit_bytes=8 * 1024 * 1024),
    )(probe, mine, other)


def body(object_field, probe_field, intensity, scan_offsets, pattern_counts):
    size = probe_field.shape[1]
    slots = intensity.shape[2]
    patterns = intensity.reshape(slots, size, size)
    live_slots = jnp.concatenate(
        [scan_offsets.reshape(slots, 2).T, jnp.broadcast_to(pattern_counts, (1, slots))], axis=0
    )
    tables = dft_tables(size)
    row_end, col_end = place_of(ROW)[2], place_of(COL)[2]

    own = object_field.reshape(2, TILES, 8, LANES)
    strip = strip_around(own)
    strips = (strip, paired(strip, ROW, 0), paired(strip, ROW, 2))
    row0, row1, row2, keep, send, peak = gradients(True, live_slots, patterns, tables, probe_field, *strips)
    half = keep + core_swap(send)
    row0 = after(row0, half)
    sums = side_sum(row1, paired(row0, ROW, 0), paired(row2, ROW, 2), row_end)
    payloads = to_sides(sums)
    shares = after(plane_shares(half), *payloads)
    grad = side_sum(sums[1], paired(payloads[0], COL, 0), paired(payloads[1], COL, 2), col_end)
    own = own - grad / peak
    shares = after(depth_shares(shares), own)
    strip = strip_around(own)
    strips = (strip, paired(strip, ROW, 0), paired(strip, ROW, 2))
    mine = gathered(shares, keep.shape)
    totals = (mine, core_swap(mine))

    row0, row1, row2, keep, send, peak, probe = gradients(
        False, live_slots, patterns, tables, probe_field, *strips, *totals
    )
    shares = plane_shares(keep + core_swap(send))
    shares, (row0, row2) = lax.optimization_barrier((shares, (row0, row2)))
    sums = side_sum(row1, paired(row0, ROW, 0), paired(row2, ROW, 2), row_end)
    payloads = to_sides(sums)
    shares = after(depth_shares(shares), *payloads)
    grad = side_sum(sums[1], paired(payloads[0], COL, 0), paired(payloads[1], COL, 2), col_end)
    new_object = (own - grad / peak).reshape(object_field.shape)
    mine = gathered(shares, keep.shape)
    return (new_object, last_probe(probe, mine, core_swap(mine)))


def solution(mesh):
    split = Mesh(mesh.devices.reshape(4, 2, 8, 4), ("y", "core", "z", "x"))
    in_specs = (
        P(None, ROW, COL),
        P(),
        P(ROW, COL, None, None, None),
        P(ROW, COL, None, None),
        P(ROW, COL),
    )
    out_specs = (P(None, ROW, COL), P())
    return jax.shard_map(body, mesh=split, in_specs=in_specs, out_specs=out_specs, check_vma=False)
```
